32 devices in a mesh: chan: 4 (over x, core), sym: 4 (over z), sub: 2 (over y).
Axes of the slice: x: 2, y: 2, z: 4, core: 2. Of those that a mesh axis runs over, the one named last changes fastest.
Arguments:
- samples: float32 [2, 64, 24, 9216], P(None, ('chan', 'sub'), 'sym'), parts along dimension 1, may hold values from -16 to 16
- constellation_index: int32 [96, 4096], P(('chan', 'sym'), 'sub'), parts along dimension 0, may hold values from 0 to 63, as said below
- pilot_offsets: int32 [24], P('sym'), may hold values from 0 to 11
- cp_offset: int32 [96], P(('chan', 'sym')), parts along dimension 0, may hold values from 0 to 1024, as said below
Outputs:
- caf: float32 [2, 64, 24, 1024], P(None, 'chan', 'sym', 'sub'), parts along dimension 1
The draws below stay inside these ranges and needn't reach their ends.
There are 4 independent parts, one for each index of `chan`. The reference program is written for one: setup_inputs(seed, part) draws one part's arguments, and reference() takes and returns one part's arrays. A program takes and returns all parts, laid end to end along the dimension named above; an argument that names none is the same for every part. Nothing has to cross between parts.
Inputs may be any that keep to these rules, and one draw needn't show every extreme that they name: Symbol m's scattered pilots sit on the active subcarriers k with k mod 12 == pilot_offsets[m]. The transform window of symbol m is samples cp_offset[m] to cp_offset[m] + 64 * 128 - 1 of its record. `constellation_index`: the index's low three bits give the in-phase level, the high three the quadrature level.
All inputs are finite; a program needn't handle non-finite values.
Results may differ from the reference program's by a relative error of at most 0.0003.
Values may be sent and summed in bfloat16 or wider, within the bound.
No kernel may reach another device: no remote copies, remote signals or barrier semaphores. Data moves between devices by JAX's collectives and lax.ppermute only.
A program may use at most 64 MiB of HBM per device.

```python
import math
import jax
import jax.numpy as jnp
from jax import lax

OUTER_FACTOR = 64
INNER_FACTOR = 128
ACTIVE_TONES = 4096
GUARD_SAMPLES = 1024
SMOOTH_HALFSPAN = 48
PSP = 12
CH = 16
SYMBOL_COUNT = 24


TWO_PI = 2.0 * math.pi


HIGHEST = lax.Precision.HIGHEST


def decoded_levels(key):
    return jax.random.randint(jax.random.fold_in(key, 101), (SYMBOL_COUNT, ACTIVE_TONES), 0, 64, dtype=jnp.int32)


def window_starts(key):
    return jax.random.randint(jax.random.fold_in(key, 202), (SYMBOL_COUNT,), 0, GUARD_SAMPLES + 1, dtype=jnp.int32)


def draw_constellation_index(key, part):
    return decoded_levels(key)


def draw_cp_offset(key, part):
    return window_starts(key)


def phase_table(product, period):
    angle = TWO_PI / period * (product % period).astype(jnp.float32)
    return (jnp.cos(angle), jnp.sin(angle))


def inverse_transform(spec_re, spec_im):
    full_length = OUTER_FACTOR * INNER_FACTOR
    leading = spec_re.shape[:-1]
    block_re = spec_re.reshape(leading + (OUTER_FACTOR, INNER_FACTOR))
    block_im = spec_im.reshape(leading + (OUTER_FACTOR, INNER_FACTOR))
    index_outer = jnp.arange(OUTER_FACTOR, dtype=jnp.int32)
    index_inner = jnp.arange(INNER_FACTOR, dtype=jnp.int32)
    cos_outer, sin_outer = phase_table(index_outer[:, None] * index_outer[None, :], OUTER_FACTOR)
    first_re = jnp.einsum('nb,...bq->...nq', cos_outer, block_re, precision=HIGHEST) - jnp.einsum('nb,...bq->...nq', sin_outer, block_im, precision=HIGHEST)
    first_im = jnp.einsum('nb,...bq->...nq', cos_outer, block_im, precision=HIGHEST) + jnp.einsum('nb,...bq->...nq', sin_outer, block_re, precision=HIGHEST)
    cos_twist, sin_twist = phase_table(index_outer[:, None] * index_inner[None, :], full_length)
    twist_re = first_re * cos_twist - first_im * sin_twist
    twist_im = first_re * sin_twist + first_im * cos_twist
    cos_inner, sin_inner = phase_table(index_inner[:, None] * index_inner[None, :], INNER_FACTOR)
    final_re = jnp.einsum('...nq,qm->...mn', twist_re, cos_inner, precision=HIGHEST) - jnp.einsum('...nq,qm->...mn', twist_im, sin_inner, precision=HIGHEST)
    final_im = jnp.einsum('...nq,qm->...mn', twist_re, sin_inner, precision=HIGHEST) + jnp.einsum('...nq,qm->...mn', twist_im, cos_inner, precision=HIGHEST)
    normalizer = 1.0 / math.sqrt(full_length)
    return (final_re.reshape(leading + (full_length,)) * normalizer, final_im.reshape(leading + (full_length,)) * normalizer)


def echo_response(key, salt, weakest, strongest, bin_index):
    full_length = OUTER_FACTOR * INNER_FACTOR
    delays = jax.random.randint(jax.random.fold_in(key, salt), (CH,), 3 * full_length // 16, 7 * full_length // 16, dtype=jnp.int32)
    log_strength = jax.random.uniform(jax.random.fold_in(key, salt + 1), (CH,), jnp.float32, math.log(weakest), math.log(strongest))
    strength = jnp.exp(log_strength)
    phase_angle = jax.random.uniform(jax.random.fold_in(key, salt + 2), (CH,), jnp.float32, -math.pi, math.pi)
    cos_delay, sin_delay = phase_table(bin_index[None, :] * delays[:, None], full_length)
    turn_re = jnp.cos(phase_angle)[:, None] * cos_delay + jnp.sin(phase_angle)[:, None] * sin_delay
    turn_im = jnp.sin(phase_angle)[:, None] * cos_delay - jnp.cos(phase_angle)[:, None] * sin_delay
    return (strength[:, None] * turn_re, strength[:, None] * turn_im)


def draw_samples(key, part):
    full_length = OUTER_FACTOR * INNER_FACTOR
    lower_edge = (full_length - ACTIVE_TONES) // 2
    symbol_index = decoded_levels(key)
    starts = window_starts(key)
    level_re = (2 * (symbol_index % 8) - 7).astype(jnp.float32) / math.sqrt(42.0)
    level_im = (2 * (symbol_index // 8) - 7).astype(jnp.float32) / math.sqrt(42.0)
    padding = ((0, 0), (lower_edge, full_length - ACTIVE_TONES - lower_edge))
    data_re = jnp.pad(level_re, padding)
    data_im = jnp.pad(level_im, padding)
    bin_index = jnp.arange(full_length, dtype=jnp.int32)
    chan_re, chan_im = echo_response(key, 303, 1.5, 3.0, bin_index)
    spec_re = data_re[None] * chan_re[:, None] - data_im[None] * chan_im[:, None]
    spec_im = data_re[None] * chan_im[:, None] + data_im[None] * chan_re[:, None]
    wave_re, wave_im = inverse_transform(spec_re, spec_im)
    noise_key = jax.random.fold_in(key, 505)
    noise_part = 0.15 * jax.random.normal(noise_key, (2, CH, SYMBOL_COUNT, full_length), jnp.float32)
    waveform = jnp.stack([wave_re, wave_im]) + noise_part
    places = jnp.arange(full_length + GUARD_SAMPLES, dtype=jnp.int32)
    source = (places[None, :] - starts[:, None]) % full_length
    gather_index = jnp.broadcast_to(source[None, None], (2, CH, SYMBOL_COUNT, full_length + GUARD_SAMPLES))
    picked = jnp.take_along_axis(waveform, gather_index, axis=3)
    return jnp.clip(picked, -16.0, 16.0).astype(jnp.float32)


def plant(array, own_key, low, largest):
    index_at = [jax.random.randint(jax.random.fold_in(own_key, axis), (), 0, length) for axis, length in enumerate(array.shape)]
    main_axis = array.shape.index(max(array.shape))
    next_to = index_at[:main_axis] + [(index_at[main_axis] + 1) % array.shape[main_axis]] + index_at[main_axis + 1:]
    return array.at[tuple(index_at)].set(low).at[tuple(next_to)].set(largest)


def setup_inputs(seed: int = 0, part: int = 0) -> dict:
    keys = jax.random.split(jax.random.key(seed), 5)
    part_keys = jax.random.split(jax.random.fold_in(keys[4], part), 5)
    return {
        "samples": draw_samples(jax.random.fold_in(jax.random.fold_in(keys[4], part), 71), part),
        "constellation_index": draw_constellation_index(jax.random.fold_in(jax.random.fold_in(keys[4], part), 71), part),
        "pilot_offsets": plant(jax.random.randint(keys[2], (SYMBOL_COUNT,), 0, PSP), jax.random.fold_in(keys[2], 1), 0, PSP - 1).astype(jnp.int32),
        "cp_offset": draw_cp_offset(jax.random.fold_in(jax.random.fold_in(keys[4], part), 71), part),
    }


def reference(samples, constellation_index, pilot_offsets, cp_offset):
    grand_total = OUTER_FACTOR * INNER_FACTOR

    def one_symbol(record, offset):
        return lax.dynamic_slice_in_dim(record, offset.astype(jnp.int32), grand_total, axis=2)
    symbol_windows = jax.vmap(one_symbol, in_axes=(2, 0), out_axes=2)(samples, cp_offset)
    symbol_spectrum = jnp.fft.fft(symbol_windows[0] + 1j * symbol_windows[1], axis=-1) / math.sqrt(grand_total)
    lower_edge = (grand_total - ACTIVE_TONES) // 2
    band_slice = symbol_spectrum[..., lower_edge:lower_edge + ACTIVE_TONES]
    level_real = (2 * (constellation_index % 8) - 7).astype(jnp.float32)
    level_imaginary = (2 * (constellation_index // 8) - 7).astype(jnp.float32)
    factor = math.sqrt(42.0) / (level_real * level_real + level_imaginary * level_imaginary)
    ratio_re = (jnp.real(band_slice) * level_real + jnp.imag(band_slice) * level_imaginary) * factor
    ratio_im = (jnp.imag(band_slice) * level_real - jnp.real(band_slice) * level_imaginary) * factor
    ratio = jnp.stack([ratio_re, ratio_im])
    positions = jnp.arange(ACTIVE_TONES, dtype=jnp.int32)
    pilot = (positions[None, :] % PSP == pilot_offsets[:, None]).astype(jnp.float32)
    values = ratio * pilot
    zero_padded = jnp.pad(values, ((0, 0), (0, 0), (0, 0), (SMOOTH_HALFSPAN, SMOOTH_HALFSPAN)))
    pilot_padded = jnp.pad(pilot, ((0, 0), (SMOOTH_HALFSPAN, SMOOTH_HALFSPAN)))
    numerator = jnp.zeros(values.shape, jnp.float32)
    denominator = jnp.zeros(pilot.shape, jnp.float32)
    for shift_amount in range(-SMOOTH_HALFSPAN, SMOOTH_HALFSPAN + 1):
        taper_weight = float(SMOOTH_HALFSPAN + 1 - abs(shift_amount))
        numerator = numerator + taper_weight * zero_padded[..., SMOOTH_HALFSPAN + shift_amount:SMOOTH_HALFSPAN + shift_amount + ACTIVE_TONES]
        denominator = denominator + taper_weight * pilot_padded[:, SMOOTH_HALFSPAN + shift_amount:SMOOTH_HALFSPAN + shift_amount + ACTIVE_TONES]
    purified = ratio - numerator / denominator
    delay_profile = jnp.fft.ifft(purified[0] + 1j * purified[1], axis=-1)[..., :GUARD_SAMPLES] * math.sqrt(ACTIVE_TONES)
    spread = jnp.fft.fft(delay_profile, axis=1) / math.sqrt(delay_profile.shape[1])
    return jnp.stack([jnp.real(spread), jnp.imag(spread)]).astype(jnp.float32)
```

```python
import functools
import math

import jax
import jax.numpy as jnp
import ml_dtypes
import numpy as np
from jax import lax
from jax.experimental import pallas as pl
from jax.experimental.pallas import tpu as pltpu
from jax.sharding import PartitionSpec as P

OUTER_FACTOR = 64
INNER_FACTOR = 128
ACTIVE_TONES = 4096
GUARD_SAMPLES = 1024
SMOOTH_HALFSPAN = 48
PSP = 12

TWO_PI = 2.0 * math.pi
ROOT_FORTYTWO = math.sqrt(42.0)
HIGHEST = lax.Precision.HIGHEST

WHOLE = OUTER_FACTOR * INNER_FACTOR
FOLD = 32
WIDE = WHOLE // FOLD
LANES = 128
ROWS = 8
LOWEST = (WHOLE - ACTIVE_TONES) // 2
RANGE_ROWS = GUARD_SAMPLES // LANES
VMEM_LIMIT = 48 * 1024 * 1024


def split_table(table):
    high = table.astype(np.float32).astype(ml_dtypes.bfloat16)
    low = (table - high.astype(np.float64)).astype(np.float32).astype(ml_dtypes.bfloat16)
    return high, low


def turning(sign, product, period):
    angle = sign * TWO_PI / period * (product % period)
    cosine, sine = np.cos(angle), np.sin(angle)
    return np.block([[cosine, sine], [-sine, cosine]])


def residue_order():
    row = np.arange(FOLD)
    return row // 8 + 4 * (row % 8)


def spectrum_tables():
    b = np.arange(WIDE)
    j = LOWEST // FOLD + np.arange(ACTIVE_TONES // FOLD)
    high, low = split_table(turning(-1, b[:, None] * j[None, :], WIDE))
    angle = -TWO_PI / WHOLE * (residue_order()[:, None] * b[None, :])
    return high, low, np.stack([np.cos(angle), np.sin(angle)]).astype(np.float32)


def range_tables():
    j = np.arange(ACTIVE_TONES // FOLD)
    l = np.arange(LANES)
    high, low = split_table(turning(1, j[:, None] * l[None, :], ACTIVE_TONES // FOLD))
    angle = TWO_PI / ACTIVE_TONES * (residue_order()[:, None] * l[None, :])
    return high, low, np.stack([np.cos(angle), np.sin(angle)]).astype(np.float32)


def times(x, turn):
    re, im = x
    turn = turn % 1.0
    eighth = round(turn * 8)
    if abs(turn * 8 - eighth) < 1e-9:
        eighth %= 8
        if eighth % 2 == 0:
            return [(re, im), (-im, re), (-re, -im), (im, -re)][eighth // 2]
        half = math.sqrt(0.5)
        add, sub = (re + im) * half, (re - im) * half
        return [(sub, add), (-add, sub), (-sub, -add), (add, -sub)][eighth // 2]
    c, s = math.cos(TWO_PI * turn), math.sin(TWO_PI * turn)
    return re * c - im * s, re * s + im * c


def plus(x, y):
    return x[0] + y[0], x[1] + y[1]


def minus(x, y):
    return x[0] - y[0], x[1] - y[1]


def turn_quarter(x, sign):
    return (-x[1], x[0]) if sign > 0 else (x[1], -x[0])


def dft4(x, sign):
    a, b = plus(x[0], x[2]), minus(x[0], x[2])
    c, d = plus(x[1], x[3]), turn_quarter(minus(x[1], x[3]), sign)
    return [plus(a, c), plus(b, d), minus(a, c), minus(b, d)]


def dft8(x, sign):
    even, odd = dft4(x[0::2], sign), dft4(x[1::2], sign)
    odd = [times(o, sign * k / 8) for k, o in enumerate(odd)]
    return [plus(e, o) for e, o in zip(even, odd)] + [minus(e, o) for e, o in zip(even, odd)]


def dft3(x, sign):
    total, diff = plus(x[1], x[2]), minus(x[1], x[2])
    mid = (x[0][0] - 0.5 * total[0], x[0][1] - 0.5 * total[1])
    root = sign * math.sqrt(0.75)
    side = (-root * diff[1], root * diff[0])
    return [plus(x[0], total), plus(mid, side), minus(mid, side)]


def dft6(x, sign):
    even, odd = dft3(x[0::2], sign), dft3(x[1::2], sign)
    odd = [times(o, sign * k / 6) for k, o in enumerate(odd)]
    return [plus(e, o) for e, o in zip(even, odd)] + [minus(e, o) for e, o in zip(even, odd)]


def split_rows(x):
    high = x.astype(jnp.bfloat16)
    return high, (x - high.astype(jnp.float32)).astype(jnp.bfloat16)


def dot(x, w):
    return lax.dot_general(x, w, (((1,), (0,)), ((), ())), preferred_element_type=jnp.float32)


def spectrum_kernel(off_ref, x_ref, high_ref, low_ref, twist_ref, out_ref, mid_ref, rows_ref):
    off = off_ref[pl.program_id(0)]
    lane = lax.broadcasted_iota(jnp.int32, (ROWS, LANES), 1)

    def sample(part, chunk):
        value = x_ref[part, 0, :, chunk * LANES : (chunk + 1) * LANES]
        if chunk * LANES < GUARD_SAMPLES:
            wrapped = x_ref[part, 0, :, WHOLE + chunk * LANES : WHOLE + (chunk + 1) * LANES]
            value = jnp.where(lane < off - chunk * LANES, wrapped, value)
        return value

    halves = WIDE // LANES
    for h in range(halves):
        for v in range(8):
            chunks = [halves * (8 * u + v) + h for u in range(4)]
            y = dft4([(sample(0, c), sample(1, c)) for c in chunks], -1)
            for p in range(4):
                mid_ref[h, p, v, 0], mid_ref[h, p, v, 1] = times(y[p], -v * p / FOLD)
    for h in range(halves):
        for p in range(4):
            x = [(mid_ref[h, p, v, 0], mid_ref[h, p, v, 1]) for v in range(8)]
            y = dft8(x, -1)
            for q in range(0, 8, 2):
                pair = []
                for row in (p * 8 + q, p * 8 + q + 1):
                    re, im = y[row - p * 8]
                    c = twist_ref[0, row : row + 1, h * LANES : (h + 1) * LANES]
                    s = twist_ref[1, row : row + 1, h * LANES : (h + 1) * LANES]
                    pair.append((re * c - im * s, re * s + im * c))
                at = slice((p * 8 + q) * ROWS, (p * 8 + q + 2) * ROWS)
                for part in range(2):
                    high, low = split_rows(jnp.concatenate([pair[0][part], pair[1][part]], axis=0))
                    column = part * WIDE + h * LANES
                    rows_ref[at, column : column + LANES] = high
                    rows_ref[at, 2 * WIDE + column : 2 * WIDE + column + LANES] = low
    high = rows_ref[:, : 2 * WIDE]
    low = rows_ref[:, 2 * WIDE :]
    out_ref[0, 0] = dot(high, high_ref[...]) + dot(low, high_ref[...]) + dot(high, low_ref[...])


def profile_kernel(
    blocks, scale, off_ref, pilot_ref, place_ref, s_ref, index_ref, high_ref, low_ref, twist_ref, *refs
):
    outs = refs[:blocks]
    gain_ref, ratio_ref, num_ref, rows_ref, range_ref, prof_ref = refs[blocks:]
    m = pl.program_id(0)
    off, offset = off_ref[m], pilot_ref[m]
    tones = ACTIVE_TONES // FOLD

    row = lax.broadcasted_iota(jnp.int32, (FOLD, tones), 0)
    lane = lax.broadcasted_iota(jnp.int32, (FOLD, tones), 1)
    k = (row >> 3) + 4 * (row & 7) + FOLD * lane
    angle = ((off * (k + LOWEST)) & (WHOLE - 1)).astype(jnp.float32) * (TWO_PI / WHOLE)
    index = index_ref[0].astype(jnp.float32)
    high_bits = jnp.floor(index * 0.125)
    level_re = 2.0 * (index - 8.0 * high_bits) - 7.0
    level_im = 2.0 * high_bits - 7.0
    factor = scale / (level_re * level_re + level_im * level_im)
    c, s = jnp.cos(angle), jnp.sin(angle)
    gain_ref[0] = (c * level_re + s * level_im) * factor
    gain_ref[1] = (s * level_re - c * level_im) * factor
    span = SMOOTH_HALFSPAN + 1
    is_pilot = lax.rem(k + (PSP - offset), PSP) == 0
    total = jnp.where(is_pilot, 201.0, 200.0)
    first_after = ACTIVE_TONES + lax.rem(offset + PSP * ACTIVE_TONES - ACTIVE_TONES, PSP)
    for i in range(4):
        before = span - (k - offset + PSP * (i + 1))
        after = span - (first_after + PSP * i - k)
        total = total - jnp.maximum(before, 0).astype(jnp.float32) - jnp.maximum(after, 0).astype(jnp.float32)
    gain_ref[2] = 1.0 / total
    gain_ref[3] = jnp.where(is_pilot, 1.0, 0.0)

    for i in range(FOLD):
        re = s_ref[0, 0, i * ROWS : (i + 1) * ROWS, :tones]
        im = s_ref[0, 0, i * ROWS : (i + 1) * ROWS, tones:]
        c = gain_ref[0, i : i + 1, :]
        s = gain_ref[1, i : i + 1, :]
        ratio_ref[0, i] = re * c - im * s
        ratio_ref[1, i] = re * s + im * c

    r = offset & 3
    lane = lax.broadcasted_iota(jnp.int32, (ROWS, tones), 1)
    for part in range(2):
        picked = [ratio_ref[part, r * 8 + a] * gain_ref[3, pl.ds(r * 8 + a, 1), :] for a in range(8)]

        def pilot(i):
            b, a = i // 8, i % 8
            if b == 0:
                return picked[a]
            rolled = pltpu.roll(picked[a], (-b) % tones, 1)
            return jnp.where((lane + b >= 0) & (lane + b < tones), rolled, 0.0)

        q = {i: pilot(i) for i in range(-13, 21)}
        slope = sum(q[i] for i in range(0, 12)) - sum(q[i] for i in range(-12, 0))
        value = sum((49 - 4 * abs(i + 1)) * q[i] for i in range(-13, 12))
        for a in range(-1, 8):
            for s in range(4):
                place = r + s
                here = value if s == 0 else value + s * slope - q[a - 12]
                num_ref[part, (place & 3) * 10 + a + 1 + (place >> 2)] = here
            value = value + 4.0 * slope - q[a - 12] + q[a + 13]
            if a < 7:
                slope = slope + q[a + 13] - 2.0 * q[a + 1] + q[a - 11]

    for i in range(0, FOLD, 2):
        for part in range(2):
            pair = []
            for row in (i, i + 1):
                smooth = num_ref[part, (row // 8) * 10 + row % 8 + 1] * gain_ref[2, row : row + 1, :]
                pair.append(ratio_ref[part, row] - smooth)
            high, low = split_rows(jnp.concatenate(pair, axis=0))
            at = slice(i * ROWS, (i + 2) * ROWS)
            rows_ref[at, part * tones : (part + 1) * tones] = high
            rows_ref[at, (2 + part) * tones : (3 + part) * tones] = low
    high = rows_ref[:, : 2 * tones]
    low = rows_ref[:, 2 * tones :]
    range_ref[...] = dot(high, high_ref[...]) + dot(low, high_ref[...]) + dot(high, low_ref[...])

    sums = None
    for p in range(4):
        x = []
        for q in range(8):
            i = p * 8 + q
            re = range_ref[i * ROWS : (i + 1) * ROWS, :LANES]
            im = range_ref[i * ROWS : (i + 1) * ROWS, LANES:]
            c = twist_ref[0, i : i + 1, :]
            s = twist_ref[1, i : i + 1, :]
            x.append((re * c - im * s, re * s + im * c))
        y = [times(v, p * h / FOLD) for h, v in enumerate(dft8(x, 1))]
        sums = y if sums is None else [plus(a, b) for a, b in zip(sums, y)]
    if blocks == 1:
        for h in range(RANGE_ROWS):
            outs[0][0, 0, 0, h], outs[0][0, 0, 1, h] = sums[h]
        return
    for h in range(RANGE_ROWS):
        prof_ref[0, h], prof_ref[1, h] = sums[h]
    each = RANGE_ROWS // blocks
    for d in range(blocks):
        block = place_ref[0] ^ d
        for part in range(2):
            for h in range(each):
                outs[d][0, 0, part, h] = prof_ref[part, block * each + h]


def doppler_kernel(place_ref, *refs):
    pieces, outs, (turned_ref, spread_ref) = refs[:4], refs[4:8], refs[8:]
    own, rank = place_ref[0], place_ref[1]
    local_symbols, _, _, each = pieces[0].shape[:4]
    for d in range(4):
        for m in range(local_symbols):
            turned_ref[own ^ d, m] = pieces[d][m, 0]
    for h in range(each):
        grid = {}
        for m in range(local_symbols):
            x = [(turned_ref[s, m, 0, h], turned_ref[s, m, 1, h]) for s in range(4)]
            for p, y in enumerate(dft4(x, -1)):
                grid[p, m] = times(y, -m * p / (4 * local_symbols))
        for p in range(4):
            for q, y in enumerate(dft6([grid[p, m] for m in range(local_symbols)], -1)):
                f = p + 4 * q
                at = slice(h * LANES, (h + 1) * LANES)
                spread_ref[f // local_symbols, 0, f % local_symbols, :, at] = y[0]
                spread_ref[f // local_symbols, 1, f % local_symbols, :, at] = y[1]
    for d in range(4):
        outs[d][...] = spread_ref[rank ^ d]


def join_kernel(place_ref, *refs):
    pieces, out_ref = refs[:4], refs[4]
    own = place_ref[0]
    wide = pieces[0].shape[-1]
    for d in range(4):
        h = own ^ d
        rows = pl.ds(pl.multiple_of((h & 1) * ROWS, ROWS), ROWS)
        columns = pl.ds(pl.multiple_of((h >> 1) * wide, LANES), wide)
        out_ref[:, :, rows, columns] = pieces[d][...]


def spectra(windows, cp_offset):
    _, symbols, channels, record = windows.shape
    high, low, twist = spectrum_tables()
    tones = ACTIVE_TONES // FOLD
    whole = lambda a: pl.BlockSpec(a.shape, lambda m, g, *_: (0,) * a.ndim)
    return pl.pallas_call(
        spectrum_kernel,
        grid_spec=pltpu.PrefetchScalarGridSpec(
            num_scalar_prefetch=1,
            grid=(symbols, channels // ROWS),
            in_specs=[
                pl.BlockSpec((2, 1, ROWS, record), lambda m, g, *_: (0, m, g, 0)),
                whole(high),
                whole(low),
                whole(twist),
            ],
            out_specs=pl.BlockSpec((1, 1, FOLD * ROWS, 2 * tones), lambda m, g, *_: (m, g, 0, 0)),
            scratch_shapes=[
                pltpu.VMEM((WIDE // LANES, 4, 8, 2, ROWS, LANES), jnp.float32),
                pltpu.VMEM((FOLD * ROWS, 4 * WIDE), jnp.bfloat16),
            ],
        ),
        out_shape=jax.ShapeDtypeStruct((symbols, channels // ROWS, FOLD * ROWS, 2 * tones), jnp.float32),
        compiler_params=pltpu.CompilerParams(vmem_limit_bytes=VMEM_LIMIT),
        name="spectra",
    )(cp_offset, windows, high, low, twist)


def profiles(spectrum, index, pilot_offsets, cp_offset, place, blocks, scale):
    symbols, groups = spectrum.shape[:2]
    high, low, twist = range_tables()
    tones = ACTIVE_TONES // FOLD
    each = RANGE_ROWS // blocks
    whole = lambda a: pl.BlockSpec(a.shape, lambda m, g, *_: (0,) * a.ndim)
    block = (1, 1, 2, each, ROWS, LANES)
    return pl.pallas_call(
        functools.partial(profile_kernel, blocks, scale),
        grid_spec=pltpu.PrefetchScalarGridSpec(
            num_scalar_prefetch=3,
            grid=(symbols, groups),
            in_specs=[
                pl.BlockSpec((1, 1, FOLD * ROWS, 2 * tones), lambda m, g, *_: (m, g, 0, 0)),
                pl.BlockSpec((1, FOLD, tones), lambda m, g, *_: (m, 0, 0)),
                whole(high),
                whole(low),
                whole(twist),
            ],
            out_specs=[pl.BlockSpec(block, lambda m, g, *_: (m, g, 0, 0, 0, 0))] * blocks,
            scratch_shapes=[
                pltpu.VMEM((4, FOLD, tones), jnp.float32),
                pltpu.VMEM((2, FOLD, ROWS, tones), jnp.float32),
                pltpu.VMEM((2, 40, ROWS, tones), jnp.float32),
                pltpu.VMEM((FOLD * ROWS, 4 * tones), jnp.bfloat16),
                pltpu.VMEM((FOLD * ROWS, 2 * LANES), jnp.float32),
                pltpu.VMEM((2, RANGE_ROWS, ROWS, LANES), jnp.float32),
            ],
        ),
        out_shape=[jax.ShapeDtypeStruct((symbols, groups) + block[2:], jnp.float32)] * blocks,
        compiler_params=pltpu.CompilerParams(vmem_limit_bytes=VMEM_LIMIT),
        name="profiles",
    )(cp_offset, pilot_offsets, place, spectrum, index, high, low, twist)


def doppler_plain(own_profiles, symbols):
    turned = lax.all_to_all(own_profiles, "sub", split_axis=3, concat_axis=1, tiled=True)
    turned = lax.all_to_all(turned, "sym", split_axis=3, concat_axis=2, tiled=True)
    ids = np.arange(symbols)
    angle = TWO_PI / symbols * (ids[:, None] * ids[None, :] % symbols)
    c, s = np.cos(angle).astype(np.float32), np.sin(angle).astype(np.float32)
    product = lambda t, x: jnp.einsum("fm,cmq->cfq", t, x, precision=HIGHEST)
    re = product(c, turned[0]) + product(s, turned[1])
    im = product(c, turned[1]) - product(s, turned[0])
    return lax.all_to_all(jnp.stack([re, im]), "sym", split_axis=2, concat_axis=3, tiled=True)


def doppler_paired(pieces, place, rank, syms, subs):
    share = syms // subs
    got = [pieces[0]] + [
        lax.ppermute(pieces[d], "sym", [(i, i ^ d) for i in range(syms)]) for d in range(1, syms)
    ]
    symbols, _, _, each = got[0].shape[:4]
    piece = jax.ShapeDtypeStruct((2, symbols, ROWS, each * LANES), jnp.float32)
    in_vmem = pl.BlockSpec(memory_space=pltpu.VMEM)
    in_smem = pl.BlockSpec(memory_space=pltpu.SMEM)
    spread = pl.pallas_call(
        doppler_kernel,
        in_specs=[in_smem] + [in_vmem] * syms,
        out_specs=[in_vmem] * syms,
        out_shape=[piece] * syms,
        scratch_shapes=[
            pltpu.VMEM((syms, symbols, 2, each, ROWS, LANES), jnp.float32),
            pltpu.VMEM((syms,) + piece.shape, jnp.float32),
        ],
        compiler_params=pltpu.CompilerParams(vmem_limit_bytes=VMEM_LIMIT),
        name="doppler",
    )(jnp.stack([place, rank]), *got)
    joined = []
    for d in range(syms):
        route = [
            (s * subs + u, (((s % share) * subs + u) ^ d) * subs + s // share)
            for s in range(syms)
            for u in range(subs)
        ]
        joined.append(lax.ppermute(spread[d], ("sym", "sub"), route))
    out = pl.pallas_call(
        join_kernel,
        in_specs=[in_smem] + [in_vmem] * syms,
        out_specs=in_vmem,
        out_shape=jax.ShapeDtypeStruct((2, symbols, subs * ROWS, share * each * LANES), jnp.float32),
        compiler_params=pltpu.CompilerParams(vmem_limit_bytes=VMEM_LIMIT),
        name="join",
    )(place[None], *joined)
    return jnp.transpose(out, (0, 2, 1, 3))


def local(samples, constellation_index, pilot_offsets, cp_offset):
    syms, subs = lax.axis_size("sym"), lax.axis_size("sub")
    place, sub = lax.axis_index("sym"), lax.axis_index("sub")
    channels, symbols = samples.shape[1:3]
    index = constellation_index.reshape(symbols, -1, 8, 4).transpose(0, 3, 2, 1)
    index = index.reshape(symbols, FOLD, -1).astype(jnp.bfloat16)
    index = lax.all_gather(index, "sub", axis=2, tiled=True)
    windows = jnp.transpose(samples, (0, 2, 1, 3))
    short = -channels % ROWS
    if short:
        windows = jnp.pad(windows, ((0, 0), (0, 0), (0, short), (0, 0)))
    spectrum = spectra(windows, cp_offset)
    scale = ROOT_FORTYTWO / math.sqrt(WHOLE * ACTIVE_TONES * symbols * syms)
    paired = syms == 4 and subs == 2 and channels == ROWS and symbols == 6
    got = profiles(
        spectrum, index, pilot_offsets, cp_offset, place[None], syms if paired else 1, scale
    )
    if paired:
        rank = (place % (syms // subs)) * subs + sub
        return doppler_paired(got, place, rank, syms, subs)
    own = jnp.transpose(got[0], (2, 1, 4, 0, 3, 5))
    own = own.reshape(2, channels + short, symbols, GUARD_SAMPLES)[:, :channels]
    return doppler_plain(own, symbols * syms)


def solution(mesh):
    return jax.shard_map(
        local,
        mesh=mesh,
        in_specs=(
            P(None, ("chan", "sub"), "sym", None),
            P(("chan", "sym"), "sub"),
            P("sym"),
            P(("chan", "sym")),
        ),
        out_specs=P(None, "chan", "sym", "sub"),
        check_vma=False,
    )
```

```python
import functools
import math

import jax
import jax.numpy as jnp
import ml_dtypes
import numpy as np
from jax import lax
from jax.experimental import pallas as pl
from jax.experimental.pallas import tpu as pltpu
from jax.sharding import PartitionSpec as P

OUTER_FACTOR = 64
INNER_FACTOR = 128
ACTIVE_TONES = 4096
GUARD_SAMPLES = 1024
SMOOTH_HALFSPAN = 48
PSP = 12

TWO_PI = 2.0 * math.pi
ROOT_FORTYTWO = math.sqrt(42.0)
HIGHEST = lax.Precision.HIGHEST

WHOLE = OUTER_FACTOR * INNER_FACTOR
FOLD = 32
WIDE = WHOLE // FOLD
LANES = 128
ROWS = 8
LOWEST = (WHOLE - ACTIVE_TONES) // 2
RANGE_ROWS = GUARD_SAMPLES // LANES
VMEM_LIMIT = 48 * 1024 * 1024
SPECTRA_VMEM_LIMIT = 62 * 1024 * 1024


def split_table(table):
    high = table.astype(np.float32).astype(ml_dtypes.bfloat16)
    low = (table - high.astype(np.float64)).astype(np.float32).astype(ml_dtypes.bfloat16)
    return high, low


def turning(sign, product, period):
    angle = sign * TWO_PI / period * (product % period)
    cosine, sine = np.cos(angle), np.sin(angle)
    return np.block([[cosine, sine], [-sine, cosine]])


def residue_order():
    row = np.arange(FOLD)
    return row // 8 + 4 * (row % 8)


def spectrum_tables():
    b = np.arange(WIDE)
    j = LOWEST // FOLD + np.arange(ACTIVE_TONES // FOLD)
    high, low = split_table(turning(-1, b[:, None] * j[None, :], WIDE))
    angle = -TWO_PI / WHOLE * (residue_order()[:, None] * b[None, :])
    return high, low, np.stack([np.cos(angle), np.sin(angle)]).astype(np.float32)


def range_tables():
    j = np.arange(ACTIVE_TONES // FOLD)
    l = np.arange(LANES)
    high, low = split_table(turning(1, j[:, None] * l[None, :], ACTIVE_TONES // FOLD))
    angle = TWO_PI / ACTIVE_TONES * (residue_order()[:, None] * l[None, :])
    return high, low, np.stack([np.cos(angle), np.sin(angle)]).astype(np.float32)


def times(x, turn):
    re, im = x
    turn = turn % 1.0
    eighth = round(turn * 8)
    if abs(turn * 8 - eighth) < 1e-9:
        eighth %= 8
        if eighth % 2 == 0:
            return [(re, im), (-im, re), (-re, -im), (im, -re)][eighth // 2]
        half = math.sqrt(0.5)
        add, sub = (re + im) * half, (re - im) * half
        return [(sub, add), (-add, sub), (-sub, -add), (add, -sub)][eighth // 2]
    c, s = math.cos(TWO_PI * turn), math.sin(TWO_PI * turn)
    return re * c - im * s, re * s + im * c


def plus(x, y):
    return x[0] + y[0], x[1] + y[1]


def minus(x, y):
    return x[0] - y[0], x[1] - y[1]


def turn_quarter(x, sign):
    return (-x[1], x[0]) if sign > 0 else (x[1], -x[0])


def dft4(x, sign):
    a, b = plus(x[0], x[2]), minus(x[0], x[2])
    c, d = plus(x[1], x[3]), turn_quarter(minus(x[1], x[3]), sign)
    return [plus(a, c), plus(b, d), minus(a, c), minus(b, d)]


def dft8(x, sign):
    even, odd = dft4(x[0::2], sign), dft4(x[1::2], sign)
    odd = [times(o, sign * k / 8) for k, o in enumerate(odd)]
    return [plus(e, o) for e, o in zip(even, odd)] + [minus(e, o) for e, o in zip(even, odd)]


def dft3(x, sign):
    total, diff = plus(x[1], x[2]), minus(x[1], x[2])
    mid = (x[0][0] - 0.5 * total[0], x[0][1] - 0.5 * total[1])
    root = sign * math.sqrt(0.75)
    side = (-root * diff[1], root * diff[0])
    return [plus(x[0], total), plus(mid, side), minus(mid, side)]


def dft6(x, sign):
    even, odd = dft3(x[0::2], sign), dft3(x[1::2], sign)
    odd = [times(o, sign * k / 6) for k, o in enumerate(odd)]
    return [plus(e, o) for e, o in zip(even, odd)] + [minus(e, o) for e, o in zip(even, odd)]


def split_rows(x):
    high = x.astype(jnp.bfloat16)
    return high, (x - high.astype(jnp.float32)).astype(jnp.bfloat16)


def dot(x, w):
    return lax.dot_general(x, w, (((1,), (0,)), ((), ())), preferred_element_type=jnp.float32)


def spectrum_kernel(off_ref, x_hbm, high_hbm, low_hbm, twist_hbm, out_ref, x_ref, high_ref, low_ref, twist_ref, mid_ref, rows_ref, sems):
    symbols, groups = out_ref.shape[:2]
    tasks = [(m, g) for m in range(symbols) for g in range(groups)]
    fetches = []
    for n, (m, g) in enumerate(tasks):
        source = x_hbm.at[:, m, g * ROWS : (g + 1) * ROWS, :]
        fetches.append(pltpu.make_async_copy(source, x_ref.at[n], sems.at[3 + n]))
    tables = [
        pltpu.make_async_copy(source, target, sems.at[n])
        for n, (source, target) in enumerate([(twist_hbm, twist_ref), (high_hbm, high_ref), (low_hbm, low_ref)])
    ]
    fetches[0].start()
    for table in tables:
        table.start()
    for fetch in fetches[1:]:
        fetch.start()
    lane = lax.broadcasted_iota(jnp.int32, (ROWS, LANES), 1)
    halves = WIDE // LANES
    for n, (m, g) in enumerate(tasks):
        fetches[n].wait()
        off, slot = off_ref[m], n % 2

        def sample(part, chunk):
            value = x_ref[n, part, :, chunk * LANES : (chunk + 1) * LANES]
            if chunk * LANES < GUARD_SAMPLES:
                wrapped = x_ref[n, part, :, WHOLE + chunk * LANES : WHOLE + (chunk + 1) * LANES]
                value = jnp.where(lane < off - chunk * LANES, wrapped, value)
            return value

        for h in range(halves):
            for v in range(8):
                chunks = [halves * (8 * u + v) + h for u in range(4)]
                y = dft4([(sample(0, c), sample(1, c)) for c in chunks], -1)
                for p in range(4):
                    at = (slot, h, p, v)
                    mid_ref[at + (0,)], mid_ref[at + (1,)] = times(y[p], -v * p / FOLD)
        if n == 0:
            tables[0].wait()
        for p in range(4):
            for h in range(halves):
                at = (slot, h, p)
                y = dft8([(mid_ref[at + (v, 0)], mid_ref[at + (v, 1)]) for v in range(8)], -1)
                for q in range(0, 8, 2):
                    pair = []
                    for row in (p * 8 + q, p * 8 + q + 1):
                        re, im = y[row - p * 8]
                        c = twist_ref[0, row : row + 1, h * LANES : (h + 1) * LANES]
                        s = twist_ref[1, row : row + 1, h * LANES : (h + 1) * LANES]
                        pair.append((re * c - im * s, re * s + im * c))
                    at_rows = slice((p * 8 + q) * ROWS, (p * 8 + q + 2) * ROWS)
                    for part in range(2):
                        high, low = split_rows(jnp.concatenate([pair[0][part], pair[1][part]], axis=0))
                        column = part * WIDE + h * LANES
                        rows_ref[slot, at_rows, column : column + LANES] = high
                        rows_ref[slot, at_rows, 2 * WIDE + column : 2 * WIDE + column + LANES] = low
        if n == 0:
            tables[1].wait()
            tables[2].wait()
        high = rows_ref[slot, :, : 2 * WIDE]
        low = rows_ref[slot, :, 2 * WIDE :]
        out_ref[m, g] = dot(high, high_ref[...]) + dot(low, high_ref[...]) + dot(high, low_ref[...])


def symbol_phases(off_ref, symbols):
    tones = ACTIVE_TONES // FOLD
    row = lax.broadcasted_iota(jnp.int32, (ROWS, tones), 0)
    lane = lax.broadcasted_iota(jnp.int32, (ROWS, tones), 1)
    by_row = by_lane = jnp.zeros((ROWS, tones), jnp.int32)
    for m in range(symbols):
        by_row = jnp.where(row == m, off_ref[m], by_row)
        by_lane = jnp.where(lane == m, off_ref[m], by_lane)

    def phase(product):
        angle = (product & (WHOLE - 1)).astype(jnp.float32) * (TWO_PI / WHOLE)
        return jnp.cos(angle), jnp.sin(angle)

    return phase(by_row * (LOWEST + FOLD * lane)), [phase(by_lane * (p + 4 * row)) for p in range(4)]


def profile_kernel(
    blocks, scale, off_ref, pilot_ref, place_ref, s_ref, own_ref, other_ref, spot_ref, high_ref, low_ref, twist_ref, *refs
):
    outs = refs[:blocks]
    flat_ref, turned_ref, gain_ref, ratio_ref, num_ref, rows_ref, range_ref, prof_ref = refs[blocks:]
    symbols, groups = s_ref.shape[:2]
    tones = ACTIVE_TONES // FOLD
    own_place, swapped = place_ref[0], place_ref[1] > 0
    for j in range(FOLD // 2):
        at = slice(j * LANES, (j + 1) * LANES)
        own, other = own_ref[:, at], other_ref[:, at]
        flat_ref[j, :symbols] = jnp.where(swapped, other, own).astype(jnp.float32)
        flat_ref[FOLD // 2 + j, :symbols] = jnp.where(swapped, own, other).astype(jnp.float32)
    (lane_re, lane_im), row_phases = symbol_phases(off_ref, symbols)

    for m in range(symbols):
        slot = m % 2
        offset = pilot_ref[m]
        stood = flat_ref[:, m, :].T.astype(jnp.bfloat16)
        spread = dot(stood, spot_ref[...])
        turned_ref[slot] = sum(
            spread[FOLD * l : FOLD * (l + 1), tones * l : tones * (l + 1)] for l in range(LANES // FOLD)
        )
        row = lax.broadcasted_iota(jnp.int32, (ROWS, tones), 0)
        lane = lax.broadcasted_iota(jnp.int32, (ROWS, tones), 1)
        first_after = ACTIVE_TONES + lax.rem(offset + PSP * ACTIVE_TONES - ACTIVE_TONES, PSP)
        span = SMOOTH_HALFSPAN + 1
        for p in range(4):
            at = slice(p * 8, p * 8 + 8)
            index = turned_ref[slot, pl.ds(p, 8, stride=4), :]
            high_bits = jnp.floor(index * 0.125)
            level_re = 2.0 * (index - 8.0 * high_bits) - 7.0
            level_im = 2.0 * high_bits - 7.0
            factor = scale / (level_re * level_re + level_im * level_im)
            a, b = lane_re[m : m + 1, :], lane_im[m : m + 1, :]
            c, s = row_phases[p][0][:, m : m + 1], row_phases[p][1][:, m : m + 1]
            c, s = a * c - b * s, a * s + b * c
            gain_ref[slot, 0, at] = (c * level_re + s * level_im) * factor
            gain_ref[slot, 1, at] = (s * level_re - c * level_im) * factor
            k = p + 4 * row + FOLD * lane
            is_pilot = lax.rem(k + (PSP - offset), PSP) == 0
            total = jnp.where(is_pilot, 201.0, 200.0)
            for i in range(4):
                before = span - (k - offset + PSP * (i + 1))
                after = span - (first_after + PSP * i - k)
                total -= (jnp.maximum(before, 0) + jnp.maximum(after, 0)).astype(jnp.float32)
            gain_ref[slot, 2, at] = 1.0 / total
            gain_ref[slot, 3, at] = jnp.where(is_pilot, 1.0, 0.0)

        for g in range(groups):
            for i in range(FOLD):
                re = s_ref[m, g, i * ROWS : (i + 1) * ROWS, :tones]
                im = s_ref[m, g, i * ROWS : (i + 1) * ROWS, tones:]
                c = gain_ref[slot, 0, i : i + 1, :]
                s = gain_ref[slot, 1, i : i + 1, :]
                ratio_ref[slot, 0, i] = re * c - im * s
                ratio_ref[slot, 1, i] = re * s + im * c

            r = offset & 3
            for part in range(2):
                picked = [
                    ratio_ref[slot, part, r * 8 + a] * gain_ref[slot, 3, pl.ds(r * 8 + a, 1), :] for a in range(8)
                ]

                def pilot(i):
                    b, a = i // 8, i % 8
                    if b == 0:
                        return picked[a]
                    rolled = pltpu.roll(picked[a], (-b) % tones, 1)
                    return jnp.where((lane < tones - b) if b > 0 else (lane >= -b), rolled, 0.0)

                q = {i: pilot(i) for i in range(-13, 21)}
                slope = sum(q[i] for i in range(0, 12)) - sum(q[i] for i in range(-12, 0))
                value = sum((49 - 4 * abs(i + 1)) * q[i] for i in range(-13, 12))
                for a in range(-1, 8):
                    for s in range(4):
                        to = r + s
                        here = value if s == 0 else value + s * slope - q[a - 12]
                        num_ref[slot, part, (to & 3) * 10 + a + 1 + (to >> 2)] = here
                    value = value + 4.0 * slope - q[a - 12] + q[a + 13]
                    if a < 7:
                        slope = slope + q[a + 13] - 2.0 * q[a + 1] + q[a - 11]

            for i in range(0, FOLD, 2):
                for part in range(2):
                    pair = []
                    for n in (i, i + 1):
                        smooth = num_ref[slot, part, (n // 8) * 10 + n % 8 + 1] * gain_ref[slot, 2, n : n + 1, :]
                        pair.append(ratio_ref[slot, part, n] - smooth)
                    high, low = split_rows(jnp.concatenate(pair, axis=0))
                    at = slice(i * ROWS, (i + 2) * ROWS)
                    rows_ref[slot, at, part * tones : (part + 1) * tones] = high
                    rows_ref[slot, at, (2 + part) * tones : (3 + part) * tones] = low
            high = rows_ref[slot, :, : 2 * tones]
            low = rows_ref[slot, :, 2 * tones :]
            range_ref[slot] = dot(high, high_ref[...]) + dot(low, high_ref[...]) + dot(high, low_ref[...])

            sums = None
            for p in range(4):
                x = []
                for i in range(p * 8, p * 8 + 8):
                    re = range_ref[slot, i * ROWS : (i + 1) * ROWS, :LANES]
                    im = range_ref[slot, i * ROWS : (i + 1) * ROWS, LANES:]
                    c = twist_ref[0, i : i + 1, :]
                    s = twist_ref[1, i : i + 1, :]
                    x.append((re * c - im * s, re * s + im * c))
                y = [times(v, p * h / FOLD) for h, v in enumerate(dft8(x, 1))]
                sums = y if sums is None else [plus(a, b) for a, b in zip(sums, y)]
            if blocks == 1:
                for h in range(RANGE_ROWS):
                    outs[0][m, g, 0, h], outs[0][m, g, 1, h] = sums[h]
                continue
            for h in range(RANGE_ROWS):
                prof_ref[slot, 0, h], prof_ref[slot, 1, h] = sums[h]
            each = RANGE_ROWS // blocks
            for d in range(blocks):
                block = own_place ^ d
                for part in range(2):
                    for h in range(each):
                        outs[d][m, g, part, h] = prof_ref[slot, part, block * each + h]


def doppler_kernel(place_ref, *refs):
    pieces, outs, (turned_ref, spread_ref) = refs[:4], refs[4:8], refs[8:]
    own, rank = place_ref[0], place_ref[1]
    local_symbols, _, _, each = pieces[0].shape[:4]
    for d in range(4):
        for m in range(local_symbols):
            turned_ref[own ^ d, m] = pieces[d][m, 0]
    for h in range(each):
        grid = {}
        for m in range(local_symbols):
            x = [(turned_ref[s, m, 0, h], turned_ref[s, m, 1, h]) for s in range(4)]
            for p, y in enumerate(dft4(x, -1)):
                grid[p, m] = times(y, -m * p / (4 * local_symbols))
        for p in range(4):
            for q, y in enumerate(dft6([grid[p, m] for m in range(local_symbols)], -1)):
                f = p + 4 * q
                at = slice(h * LANES, (h + 1) * LANES)
                spread_ref[f // local_symbols, 0, f % local_symbols, :, at] = y[0]
                spread_ref[f // local_symbols, 1, f % local_symbols, :, at] = y[1]
    for d in range(4):
        outs[d][...] = spread_ref[rank ^ d]


def join_kernel(place_ref, *refs):
    pieces, out_ref = refs[:4], refs[4]
    own = place_ref[0]
    wide = pieces[0].shape[-1]
    for d in range(4):
        h = own ^ d
        rows = pl.ds(pl.multiple_of((h & 1) * ROWS, ROWS), ROWS)
        columns = pl.ds(pl.multiple_of((h >> 1) * wide, LANES), wide)
        out_ref[:, :, rows, columns] = pieces[d][...]


IN_VMEM = pl.BlockSpec(memory_space=pltpu.VMEM)
IN_SMEM = pl.BlockSpec(memory_space=pltpu.SMEM)
IN_HBM = pl.BlockSpec(memory_space=pltpu.HBM)


def spectra(windows, cp_offset):
    _, symbols, channels, record = windows.shape
    groups = channels // ROWS
    high, low, twist = spectrum_tables()
    tones = ACTIVE_TONES // FOLD
    return pl.pallas_call(
        spectrum_kernel,
        in_specs=[IN_SMEM] + [IN_HBM] * 4,
        out_specs=IN_VMEM,
        scratch_shapes=[
            pltpu.VMEM((symbols * groups, 2, ROWS, record), jnp.float32),
            pltpu.VMEM(high.shape, jnp.bfloat16),
            pltpu.VMEM(low.shape, jnp.bfloat16),
            pltpu.VMEM(twist.shape, jnp.float32),
            pltpu.VMEM((2, WIDE // LANES, 4, 8, 2, ROWS, LANES), jnp.float32),
            pltpu.VMEM((2, FOLD * ROWS, 4 * WIDE), jnp.bfloat16),
            pltpu.SemaphoreType.DMA((3 + symbols * groups,)),
        ],
        out_shape=jax.ShapeDtypeStruct((symbols, groups, FOLD * ROWS, 2 * tones), jnp.float32),
        compiler_params=pltpu.CompilerParams(vmem_limit_bytes=SPECTRA_VMEM_LIMIT),
        cost_estimate=pl.CostEstimate(flops=2 * 10**9, bytes_accessed=8 * 10**6, transcendentals=0),
        name="spectra",
    )(cp_offset, windows, high, low, twist)


def profiles(spectrum, own, other, pilot_offsets, cp_offset, places, blocks, scale):
    symbols, groups = spectrum.shape[:2]
    high, low, twist = range_tables()
    tones = ACTIVE_TONES // FOLD
    each = RANGE_ROWS // blocks
    n, column = np.arange(FOLD)[:, None], np.arange(LANES // FOLD * tones)[None, :]
    spot = (column % tones == LANES // FOLD * n + column // tones).astype(ml_dtypes.bfloat16)
    out = jax.ShapeDtypeStruct((symbols, groups, 2, each, ROWS, LANES), jnp.float32)
    return pl.pallas_call(
        functools.partial(profile_kernel, blocks, scale),
        in_specs=[IN_SMEM] * 3 + [IN_VMEM] * 7,
        out_specs=[IN_VMEM] * blocks,
        scratch_shapes=[
            pltpu.VMEM((FOLD, ROWS, LANES), jnp.float32),
            pltpu.VMEM((2, FOLD, tones), jnp.float32),
            pltpu.VMEM((2, 4, FOLD, tones), jnp.float32),
            pltpu.VMEM((2, 2, FOLD, ROWS, tones), jnp.float32),
            pltpu.VMEM((2, 2, 40, ROWS, tones), jnp.float32),
            pltpu.VMEM((2, FOLD * ROWS, 4 * tones), jnp.bfloat16),
            pltpu.VMEM((2, FOLD * ROWS, 2 * LANES), jnp.float32),
            pltpu.VMEM((2, 2, RANGE_ROWS, ROWS, LANES), jnp.float32),
        ],
        out_shape=[out] * blocks,
        compiler_params=pltpu.CompilerParams(vmem_limit_bytes=VMEM_LIMIT),
        cost_estimate=pl.CostEstimate(flops=10**9, bytes_accessed=4 * 10**6, transcendentals=0),
        name="profiles",
    )(cp_offset, pilot_offsets, places, spectrum, own, other, spot, high, low, twist)


def doppler_plain(own_profiles, symbols):
    turned = lax.all_to_all(own_profiles, "sub", split_axis=3, concat_axis=1, tiled=True)
    turned = lax.all_to_all(turned, "sym", split_axis=3, concat_axis=2, tiled=True)
    ids = np.arange(symbols)
    angle = TWO_PI / symbols * (ids[:, None] * ids[None, :] % symbols)
    c, s = np.cos(angle).astype(np.float32), np.sin(angle).astype(np.float32)
    product = lambda t, x: jnp.einsum("fm,cmq->cfq", t, x, precision=HIGHEST)
    re = product(c, turned[0]) + product(s, turned[1])
    im = product(c, turned[1]) - product(s, turned[0])
    return lax.all_to_all(jnp.stack([re, im]), "sym", split_axis=2, concat_axis=3, tiled=True)


def doppler_paired(pieces, place, rank, syms, subs):
    share = syms // subs
    got = [pieces[0]] + [
        lax.ppermute(pieces[d], "sym", [(i, i ^ d) for i in range(syms)]) for d in range(1, syms)
    ]
    symbols, _, _, each = got[0].shape[:4]
    piece = jax.ShapeDtypeStruct((2, symbols, ROWS, each * LANES), jnp.float32)
    spread = pl.pallas_call(
        doppler_kernel,
        in_specs=[IN_SMEM] + [IN_VMEM] * syms,
        out_specs=[IN_VMEM] * syms,
        out_shape=[piece] * syms,
        scratch_shapes=[
            pltpu.VMEM((syms, symbols, 2, each, ROWS, LANES), jnp.float32),
            pltpu.VMEM((syms,) + piece.shape, jnp.float32),
        ],
        compiler_params=pltpu.CompilerParams(vmem_limit_bytes=VMEM_LIMIT),
        name="doppler",
    )(jnp.stack([place, rank]), *got)
    joined = []
    for d in range(syms):
        route = [
            (s * subs + u, (((s % share) * subs + u) ^ d) * subs + s // share)
            for s in range(syms)
            for u in range(subs)
        ]
        joined.append(lax.ppermute(spread[d], ("sym", "sub"), route))
    out = pl.pallas_call(
        join_kernel,
        in_specs=[IN_SMEM] + [IN_VMEM] * syms,
        out_specs=IN_VMEM,
        out_shape=jax.ShapeDtypeStruct((2, symbols, subs * ROWS, share * each * LANES), jnp.float32),
        compiler_params=pltpu.CompilerParams(vmem_limit_bytes=VMEM_LIMIT),
        name="join",
    )(place[None], *joined)
    return jnp.transpose(out, (0, 2, 1, 3))


def local(samples, constellation_index, pilot_offsets, cp_offset):
    syms, subs = lax.axis_size("sym"), lax.axis_size("sub")
    place, sub = lax.axis_index("sym"), lax.axis_index("sub")
    channels, symbols = samples.shape[1:3]
    paired = syms == 4 and subs == 2 and channels == ROWS and symbols == 6
    half = ACTIVE_TONES // 2
    if paired:
        own = constellation_index
        other = lax.ppermute(own, "sub", [(0, 1), (1, 0)])
        swapped = sub
    else:
        index = lax.all_gather(constellation_index, "sub", axis=1, tiled=True)
        own, other, swapped = index[:, :half], index[:, half:], jnp.zeros_like(sub)
    windows = jnp.transpose(samples, (0, 2, 1, 3))
    short = -channels % ROWS
    if short:
        windows = jnp.pad(windows, ((0, 0), (0, 0), (0, short), (0, 0)))
    spectrum = spectra(windows, cp_offset)
    scale = ROOT_FORTYTWO / math.sqrt(WHOLE * ACTIVE_TONES * symbols * syms)
    places = jnp.stack([place, swapped])
    blocks = syms if paired else 1
    got = profiles(spectrum, own, other, pilot_offsets, cp_offset, places, blocks, scale)
    if paired:
        rank = (place % (syms // subs)) * subs + sub
        return doppler_paired(got, place, rank, syms, subs)
    own = jnp.transpose(got[0], (2, 1, 4, 0, 3, 5))
    own = own.reshape(2, channels + short, symbols, GUARD_SAMPLES)[:, :channels]
    return doppler_plain(own, symbols * syms)


def solution(mesh):
    return jax.shard_map(
        local,
        mesh=mesh,
        in_specs=(
            P(None, ("chan", "sub"), "sym", None),
            P(("chan", "sym"), "sub"),
            P("sym"),
            P(("chan", "sym")),
        ),
        out_specs=P(None, "chan", "sym", "sub"),
        check_vma=False,
    )
```

```python
import functools
import math

import jax
import jax.numpy as jnp
import ml_dtypes
import numpy as np
from jax import lax
from jax.experimental import pallas as pl
from jax.experimental.pallas import tpu as pltpu
from jax.sharding import PartitionSpec as P

OUTER_FACTOR = 64
INNER_FACTOR = 128
ACTIVE_TONES = 4096
GUARD_SAMPLES = 1024
SMOOTH_HALFSPAN = 48
PSP = 12

TWO_PI = 2.0 * math.pi
ROOT_FORTYTWO = math.sqrt(42.0)
HIGHEST = lax.Precision.HIGHEST

WHOLE = OUTER_FACTOR * INNER_FACTOR
FOLD = 32
WIDE = WHOLE // FOLD
LANES = 128
ROWS = 8
LOWEST = (WHOLE - ACTIVE_TONES) // 2
RANGE_ROWS = GUARD_SAMPLES // LANES
VMEM_LIMIT = 48 * 1024 * 1024
SPECTRA_VMEM_LIMIT = 52 * 1024 * 1024


def split_table(table):
    high = table.astype(np.float32).astype(ml_dtypes.bfloat16)
    low = (table - high.astype(np.float64)).astype(np.float32).astype(ml_dtypes.bfloat16)
    return high, low


def turning(sign, product, period):
    angle = sign * TWO_PI / period * (product % period)
    cosine, sine = np.cos(angle), np.sin(angle)
    return np.block([[cosine, sine], [-sine, cosine]])


def residue_order():
    row = np.arange(FOLD)
    return row // 8 + 4 * (row % 8)


def range_tables():
    j = np.arange(ACTIVE_TONES // FOLD)
    l = np.arange(LANES)
    high, low = split_table(turning(1, j[:, None] * l[None, :], ACTIVE_TONES // FOLD))
    angle = TWO_PI / ACTIVE_TONES * (residue_order()[:, None] * l[None, :])
    return high, low, np.stack([np.cos(angle), np.sin(angle)]).astype(np.float32)


def times(x, turn):
    re, im = x
    turn = turn % 1.0
    eighth = round(turn * 8)
    if abs(turn * 8 - eighth) < 1e-9:
        eighth %= 8
        if eighth % 2 == 0:
            return [(re, im), (-im, re), (-re, -im), (im, -re)][eighth // 2]
        half = math.sqrt(0.5)
        add, sub = (re + im) * half, (re - im) * half
        return [(sub, add), (-add, sub), (-sub, -add), (add, -sub)][eighth // 2]
    c, s = math.cos(TWO_PI * turn), math.sin(TWO_PI * turn)
    return re * c - im * s, re * s + im * c


def plus(x, y):
    return x[0] + y[0], x[1] + y[1]


def minus(x, y):
    return x[0] - y[0], x[1] - y[1]


def turn_quarter(x, sign):
    return (-x[1], x[0]) if sign > 0 else (x[1], -x[0])


def dft4(x, sign):
    a, b = plus(x[0], x[2]), minus(x[0], x[2])
    c, d = plus(x[1], x[3]), turn_quarter(minus(x[1], x[3]), sign)
    return [plus(a, c), plus(b, d), minus(a, c), minus(b, d)]


def dft8(x, sign):
    even, odd = dft4(x[0::2], sign), dft4(x[1::2], sign)
    odd = [times(o, sign * k / 8) for k, o in enumerate(odd)]
    return [plus(e, o) for e, o in zip(even, odd)] + [minus(e, o) for e, o in zip(even, odd)]


def dft3(x, sign):
    total, diff = plus(x[1], x[2]), minus(x[1], x[2])
    mid = (x[0][0] - 0.5 * total[0], x[0][1] - 0.5 * total[1])
    root = sign * math.sqrt(0.75)
    side = (-root * diff[1], root * diff[0])
    return [plus(x[0], total), plus(mid, side), minus(mid, side)]


def dft6(x, sign):
    even, odd = dft3(x[0::2], sign), dft3(x[1::2], sign)
    odd = [times(o, sign * k / 6) for k, o in enumerate(odd)]
    return [plus(e, o) for e, o in zip(even, odd)] + [minus(e, o) for e, o in zip(even, odd)]


def split_rows(x):
    high = x.astype(jnp.bfloat16)
    return high, (x - high.astype(jnp.float32)).astype(jnp.bfloat16)


def dot(x, w):
    return lax.dot_general(x, w, (((1,), (0,)), ((), ())), preferred_element_type=jnp.float32)


def split_product(rows_ref, high_ref, low_ref):
    width = high_ref.shape[0]
    high, low = rows_ref[:, :width], rows_ref[:, width:]
    return dot(high, high_ref[...]) + dot(low, high_ref[...]) + dot(high, low_ref[...])


def code_scale(peak):
    return jnp.ceil(jnp.log2(jnp.maximum(peak, 1e-30)) * 64.0)


def encode(x, code):
    size = jnp.sqrt(jnp.abs(x)) * (32767.0 * jnp.exp2(code * (-1.0 / 128.0))) + 0.5
    return jnp.where(x < 0.0, -size, size).astype(jnp.int32)


def decode(n, code):
    n = n.astype(jnp.int32).astype(jnp.float32)
    return n * jnp.abs(n) * (jnp.exp2(code * (1.0 / 64.0)) * (1.0 / 32767.0**2))


def peak_of(values):
    top = functools.reduce(jnp.maximum, [jnp.abs(v) for v in values])
    return jnp.max(top, axis=1, keepdims=True)


def phase(product, period):
    n = product & (period - 1)
    quarter = (n + period // 8) // (period // 4)
    x = (n - quarter * (period // 4)).astype(jnp.float32) * (TWO_PI / period)
    y = x * x
    sine = x * (1 + y * (-1 / 6 + y * (1 / 120 + y * (-1 / 5040 + y * (1 / 362880)))))
    cosine = 1 + y * (-1 / 2 + y * (1 / 24 + y * (-1 / 720 + y * (1 / 40320 - y * (1 / 3628800)))))
    odd, low, turned = (quarter & 1) == 1, (quarter & 2) == 2, ((quarter + 1) & 2) == 2
    c, s = jnp.where(odd, sine, cosine), jnp.where(odd, cosine, sine)
    return jnp.where(turned, -c, c), jnp.where(low, -s, s)


def spectrum_kernel(off_ref, x_hbm, out_ref, x_ref, high_ref, low_ref, twist_ref, mid_ref, rows_ref, sems):
    symbols, groups = out_ref.shape[:2]
    tones = ACTIVE_TONES // FOLD
    tasks = [(m, g) for m in range(symbols) for g in range(groups)]
    fetches = []
    for n, (m, g) in enumerate(tasks):
        source = x_hbm.at[:, m, g * ROWS : (g + 1) * ROWS, :]
        fetches.append(pltpu.make_async_copy(source, x_ref.at[n], sems.at[n]))
        fetches[-1].start()
    row = lax.broadcasted_iota(jnp.int32, (ROWS, WIDE), 0)
    lane = lax.broadcasted_iota(jnp.int32, (ROWS, WIDE), 1)
    for p in range(4):
        c, s = phase((p + 4 * row) * lane, WHOLE)
        twist_ref[0, p * 8 : p * 8 + 8], twist_ref[1, p * 8 : p * 8 + 8] = c, -s
    row = lax.broadcasted_iota(jnp.int32, (2 * ROWS, tones), 0)
    lane = lax.broadcasted_iota(jnp.int32, (2 * ROWS, tones), 1)
    for b in range(0, WIDE, 2 * ROWS):
        c, s = phase((b + row) * (LOWEST // FOLD + lane), WIDE)
        upper, lower = slice(b, b + 2 * ROWS), slice(WIDE + b, WIDE + b + 2 * ROWS)
        (c, c_low), (s, s_low) = split_rows(c), split_rows(s)
        high_ref[upper, :tones], high_ref[upper, tones:] = c, -s
        high_ref[lower, :tones], high_ref[lower, tones:] = s, c
        low_ref[upper, :tones], low_ref[upper, tones:] = c_low, -s_low
        low_ref[lower, :tones], low_ref[lower, tones:] = s_low, c_low
    lane = lax.broadcasted_iota(jnp.int32, (ROWS, LANES), 1)
    halves = WIDE // LANES
    for n, (m, g) in enumerate(tasks):
        fetches[n].wait()
        off, slot = off_ref[m], n % 2
        base = n * FOLD * ROWS

        def sample(part, chunk):
            value = x_ref[n, part, :, chunk * LANES : (chunk + 1) * LANES]
            if chunk * LANES < GUARD_SAMPLES:
                wrapped = x_ref[n, part, :, WHOLE + chunk * LANES : WHOLE + (chunk + 1) * LANES]
                value = jnp.where(lane < off - chunk * LANES, wrapped, value)
            return value

        for h in range(halves):
            for v in range(8):
                chunks = [halves * (8 * u + v) + h for u in range(4)]
                y = dft4([(sample(0, c), sample(1, c)) for c in chunks], -1)
                for p in range(4):
                    at = (slot, h, p, v)
                    mid_ref[at + (0,)], mid_ref[at + (1,)] = times(y[p], -v * p / FOLD)
        for p in range(4):
            for h in range(halves):
                at = (slot, h, p)
                y = dft8([(mid_ref[at + (v, 0)], mid_ref[at + (v, 1)]) for v in range(8)], -1)
                for q in range(0, 8, 2):
                    pair = []
                    for row in (p * 8 + q, p * 8 + q + 1):
                        re, im = y[row - p * 8]
                        c = twist_ref[0, row : row + 1, h * LANES : (h + 1) * LANES]
                        s = twist_ref[1, row : row + 1, h * LANES : (h + 1) * LANES]
                        pair.append((re * c - im * s, re * s + im * c))
                    at_rows = slice(base + (p * 8 + q) * ROWS, base + (p * 8 + q + 2) * ROWS)
                    for part in range(2):
                        high, low = split_rows(jnp.concatenate([pair[0][part], pair[1][part]], axis=0))
                        column = part * WIDE + h * LANES
                        rows_ref[at_rows, column : column + LANES] = high
                        rows_ref[at_rows, 2 * WIDE + column : 2 * WIDE + column + LANES] = low
    out_ref[...] = split_product(rows_ref, high_ref, low_ref).reshape(out_ref.shape)


def symbol_phases(off_ref, symbols):
    tones = ACTIVE_TONES // FOLD
    row = lax.broadcasted_iota(jnp.int32, (ROWS, tones), 0)
    lane = lax.broadcasted_iota(jnp.int32, (ROWS, tones), 1)
    by_row = by_lane = jnp.zeros((ROWS, tones), jnp.int32)
    for m in range(symbols):
        by_row = jnp.where(row == m, off_ref[m], by_row)
        by_lane = jnp.where(lane == m, off_ref[m], by_lane)

    by_lanes = phase(by_row * (LOWEST + FOLD * lane), WHOLE)
    return by_lanes, [phase(by_lane * (p + 4 * row), WHOLE) for p in range(4)]


def profile_kernel(
    syms, scale, off_ref, pilot_ref, place_ref, s_ref, own_ref, other_ref, spot_ref, high_ref, low_ref, twist_ref, *refs
):
    outs = refs[: max(syms, 1)]
    flat_ref, turned_ref, gain_ref, ratio_ref, num_ref, rows_ref, range_ref, prof_ref = refs[max(syms, 1) :]
    symbols, groups = s_ref.shape[:2]
    tones = ACTIVE_TONES // FOLD
    own_place, swapped = place_ref[0], place_ref[1] > 0
    for j in range(FOLD // 2):
        at = slice(j * LANES, (j + 1) * LANES)
        own, other = own_ref[:, at], other_ref[:, at]
        flat_ref[j, :symbols] = jnp.where(swapped, other, own).astype(jnp.float32)
        flat_ref[FOLD // 2 + j, :symbols] = jnp.where(swapped, own, other).astype(jnp.float32)
    (lane_re, lane_im), row_phases = symbol_phases(off_ref, symbols)

    for m in range(symbols):
        slot = m % 2
        offset = pilot_ref[m]
        stood = flat_ref[:, m, :].T.astype(jnp.bfloat16)
        spread = dot(stood, spot_ref[...])
        turned_ref[slot] = sum(
            spread[FOLD * l : FOLD * (l + 1), tones * l : tones * (l + 1)] for l in range(LANES // FOLD)
        )
        row = lax.broadcasted_iota(jnp.int32, (ROWS, tones), 0)
        lane = lax.broadcasted_iota(jnp.int32, (ROWS, tones), 1)
        first_after = ACTIVE_TONES + lax.rem(offset + PSP * ACTIVE_TONES - ACTIVE_TONES, PSP)
        span = SMOOTH_HALFSPAN + 1
        for p in range(4):
            at = slice(p * 8, p * 8 + 8)
            index = turned_ref[slot, pl.ds(p, 8, stride=4), :]
            high_bits = jnp.floor(index * 0.125)
            level_re = 2.0 * (index - 8.0 * high_bits) - 7.0
            level_im = 2.0 * high_bits - 7.0
            factor = scale / (level_re * level_re + level_im * level_im)
            a, b = lane_re[m : m + 1, :], lane_im[m : m + 1, :]
            c, s = row_phases[p][0][:, m : m + 1], row_phases[p][1][:, m : m + 1]
            c, s = a * c - b * s, a * s + b * c
            gain_ref[slot, 0, at] = (c * level_re + s * level_im) * factor
            gain_ref[slot, 1, at] = (s * level_re - c * level_im) * factor
            k = p + 4 * row + FOLD * lane
            is_pilot = lax.rem(k + (PSP - offset), PSP) == 0
            total = jnp.where(is_pilot, 201.0, 200.0)
            for i in range(4):
                before = span - (k - offset + PSP * (i + 1))
                after = span - (first_after + PSP * i - k)
                total -= (jnp.maximum(before, 0) + jnp.maximum(after, 0)).astype(jnp.float32)
            gain_ref[slot, 2, at] = 1.0 / total
            gain_ref[slot, 3, at] = jnp.where(is_pilot, 1.0, 0.0)

        for g in range(groups):
            base = (m * groups + g) * FOLD * ROWS
            for i in range(FOLD):
                re = s_ref[m, g, i * ROWS : (i + 1) * ROWS, :tones]
                im = s_ref[m, g, i * ROWS : (i + 1) * ROWS, tones:]
                c = gain_ref[slot, 0, i : i + 1, :]
                s = gain_ref[slot, 1, i : i + 1, :]
                ratio_ref[slot, 0, i] = re * c - im * s
                ratio_ref[slot, 1, i] = re * s + im * c

            r = offset & 3
            for part in range(2):
                picked = [
                    ratio_ref[slot, part, r * 8 + a] * gain_ref[slot, 3, pl.ds(r * 8 + a, 1), :] for a in range(8)
                ]

                def pilot(i):
                    b, a = i // 8, i % 8
                    if b == 0:
                        return picked[a]
                    rolled = pltpu.roll(picked[a], (-b) % tones, 1)
                    return jnp.where((lane < tones - b) if b > 0 else (lane >= -b), rolled, 0.0)

                q = {i: pilot(i) for i in range(-13, 21)}
                slope = sum(q[i] for i in range(0, 12)) - sum(q[i] for i in range(-12, 0))
                value = sum((49 - 4 * abs(i + 1)) * q[i] for i in range(-13, 12))
                for a in range(-1, 8):
                    for s in range(4):
                        to = r + s
                        here = value if s == 0 else value + s * slope - q[a - 12]
                        num_ref[slot, part, (to & 3) * 10 + a + 1 + (to >> 2)] = here
                    value = value + 4.0 * slope - q[a - 12] + q[a + 13]
                    if a < 7:
                        slope = slope + q[a + 13] - 2.0 * q[a + 1] + q[a - 11]

            for i in range(0, FOLD, 2):
                for part in range(2):
                    pair = []
                    for n in (i, i + 1):
                        smooth = num_ref[slot, part, (n // 8) * 10 + n % 8 + 1] * gain_ref[slot, 2, n : n + 1, :]
                        pair.append(ratio_ref[slot, part, n] - smooth)
                    high, low = split_rows(jnp.concatenate(pair, axis=0))
                    at = slice(base + i * ROWS, base + (i + 2) * ROWS)
                    rows_ref[at, part * tones : (part + 1) * tones] = high
                    rows_ref[at, (2 + part) * tones : (3 + part) * tones] = low

    range_ref[...] = split_product(rows_ref, high_ref, low_ref)
    lane = lax.broadcasted_iota(jnp.int32, (ROWS, LANES), 1)
    codes = jnp.zeros((ROWS, LANES), jnp.float32)
    for m in range(symbols):
        for g in range(groups):
            base, slot = (m * groups + g) * FOLD * ROWS, m % 2
            sums = None
            for p in range(4):
                x = []
                for i in range(p * 8, p * 8 + 8):
                    at = slice(base + i * ROWS, base + (i + 1) * ROWS)
                    re, im = range_ref[at, :LANES], range_ref[at, LANES:]
                    c, s = twist_ref[0, i : i + 1, :], twist_ref[1, i : i + 1, :]
                    x.append((re * c - im * s, re * s + im * c))
                y = [times(v, p * h / FOLD) for h, v in enumerate(dft8(x, 1))]
                sums = y if sums is None else [plus(a, b) for a, b in zip(sums, y)]
            if not syms:
                for h in range(RANGE_ROWS):
                    outs[0][m, g, 0, h], outs[0][m, g, 1, h] = sums[h]
                continue
            code = code_scale(peak_of([v for pair in sums for v in pair]))
            codes = jnp.where(lane == m, code, codes)
            for h in range(RANGE_ROWS):
                prof_ref[slot, h, 0], prof_ref[slot, h, 1] = sums[h]
            for h in range(RANGE_ROWS // syms):
                for d in range(syms):
                    row = syms * h + (own_place ^ d)
                    if d == 0:
                        outs[0][m, h] = prof_ref[slot, row]
                        continue
                    packed = [encode(prof_ref[slot, row, part], code) for part in range(2)]
                    outs[d][m * (RANGE_ROWS // syms) + h] = jnp.concatenate(packed, axis=0).astype(jnp.int16)
    if syms:
        packed = jnp.concatenate([codes, codes], axis=0).astype(jnp.int32).astype(jnp.int16)
        for d in range(1, syms):
            outs[d][symbols * (RANGE_ROWS // syms)] = packed


def doppler_kernel(place_ref, own_ref, *refs):
    (first, second, third), out_ref, turned_ref, spread_ref = refs[:3], refs[3], refs[4], refs[5]
    symbols, rows = own_ref.shape[:2]
    syms = 4
    own = place_ref[0]
    turned_ref[own] = own_ref[...]
    for d, piece in enumerate((first, second, third), 1):
        codes = piece[symbols * rows].astype(jnp.int32).astype(jnp.float32)
        for m in range(symbols):
            code = codes[:, m : m + 1]
            for h in range(rows):
                value = decode(piece[m * rows + h], code)
                turned_ref[own ^ d, m, h, 0], turned_ref[own ^ d, m, h, 1] = value[:ROWS], value[ROWS:]
    for h in range(rows):
        grid, bins = {}, {}
        for m in range(symbols):
            x = [(turned_ref[s, m, h, 0], turned_ref[s, m, h, 1]) for s in range(syms)]
            for p, y in enumerate(dft4(x, -1)):
                grid[p, m] = times(y, -m * p / (syms * symbols))
        for p in range(syms):
            for q, y in enumerate(dft6([grid[p, m] for m in range(symbols)], -1)):
                f = p + syms * q
                spread_ref[h, f, 0], spread_ref[h, f, 1] = y
    for s in range(syms):
        for h in range(rows):
            values = [spread_ref[h, s * symbols + f] for f in range(symbols)]
            code = code_scale(peak_of([v[part] for v in values for part in range(2)]))
            to = s * rows + h
            for f in range(symbols):
                packed = [encode(values[f][part], code) for part in range(2)]
                out_ref[to, f] = jnp.concatenate(packed, axis=0).astype(jnp.int16)
            codes = jnp.broadcast_to(code, (ROWS, LANES)).astype(jnp.int32)
            out_ref[to, symbols] = jnp.concatenate([codes, codes], axis=0).astype(jnp.int16)


def join_kernel(piece_ref, out_ref):
    _, symbols, channels, width = out_ref.shape
    subs = channels // ROWS
    for n in range(piece_ref.shape[0]):
        s, u = n // subs, n % subs
        code = piece_ref[n, symbols].astype(jnp.int32).astype(jnp.float32)
        gain = jnp.exp2(code * (1.0 / 64.0)) * (1.0 / 32767.0**2)
        for f in range(symbols):
            value = piece_ref[n, f].astype(jnp.int32).astype(jnp.float32)
            value = value * jnp.abs(value) * gain
            for part in range(2):
                at = slice(part * ROWS, (part + 1) * ROWS)
                out_ref[part, f, u * ROWS : (u + 1) * ROWS, s * LANES : (s + 1) * LANES] = value[at]


IN_VMEM = pl.BlockSpec(memory_space=pltpu.VMEM)
IN_SMEM = pl.BlockSpec(memory_space=pltpu.SMEM)
IN_HBM = pl.BlockSpec(memory_space=pltpu.HBM)


def spectra(windows, cp_offset):
    _, symbols, channels, record = windows.shape
    groups = channels // ROWS
    tones = ACTIVE_TONES // FOLD
    return pl.pallas_call(
        spectrum_kernel,
        in_specs=[IN_SMEM, IN_HBM],
        out_specs=IN_VMEM,
        scratch_shapes=[
            pltpu.VMEM((symbols * groups, 2, ROWS, record), jnp.float32),
            pltpu.VMEM((2 * WIDE, 2 * tones), jnp.bfloat16),
            pltpu.VMEM((2 * WIDE, 2 * tones), jnp.bfloat16),
            pltpu.VMEM((2, FOLD, WIDE), jnp.float32),
            pltpu.VMEM((2, WIDE // LANES, 4, 8, 2, ROWS, LANES), jnp.float32),
            pltpu.VMEM((symbols * groups * FOLD * ROWS, 4 * WIDE), jnp.bfloat16),
            pltpu.SemaphoreType.DMA((symbols * groups,)),
        ],
        out_shape=jax.ShapeDtypeStruct((symbols, groups, FOLD * ROWS, 2 * tones), jnp.float32),
        compiler_params=pltpu.CompilerParams(vmem_limit_bytes=SPECTRA_VMEM_LIMIT),
        cost_estimate=pl.CostEstimate(flops=2 * 10**9, bytes_accessed=8 * 10**6, transcendentals=0),
        name="spectra",
    )(cp_offset, windows)


def profiles(spectrum, own, other, pilot_offsets, cp_offset, places, syms, scale):
    symbols, groups = spectrum.shape[:2]
    high, low, twist = range_tables()
    tones = ACTIVE_TONES // FOLD
    n, column = np.arange(FOLD)[:, None], np.arange(LANES // FOLD * tones)[None, :]
    spot = (column % tones == LANES // FOLD * n + column // tones).astype(ml_dtypes.bfloat16)
    if syms:
        rows = RANGE_ROWS // syms
        piece = jax.ShapeDtypeStruct((symbols * rows + 1, 2 * ROWS, LANES), jnp.int16)
        outs = [jax.ShapeDtypeStruct((symbols, rows, 2, ROWS, LANES), jnp.float32)] + [piece] * (syms - 1)
    else:
        outs = [jax.ShapeDtypeStruct((symbols, groups, 2, RANGE_ROWS, ROWS, LANES), jnp.float32)]
    return pl.pallas_call(
        functools.partial(profile_kernel, syms, scale),
        in_specs=[IN_SMEM] * 3 + [IN_VMEM] * 7,
        out_specs=[IN_VMEM] * len(outs),
        scratch_shapes=[
            pltpu.VMEM((FOLD, ROWS, LANES), jnp.float32),
            pltpu.VMEM((2, FOLD, tones), jnp.float32),
            pltpu.VMEM((2, 4, FOLD, tones), jnp.float32),
            pltpu.VMEM((2, 2, FOLD, ROWS, tones), jnp.float32),
            pltpu.VMEM((2, 2, 40, ROWS, tones), jnp.float32),
            pltpu.VMEM((symbols * groups * FOLD * ROWS, 4 * tones), jnp.bfloat16),
            pltpu.VMEM((symbols * groups * FOLD * ROWS, 2 * LANES), jnp.float32),
            pltpu.VMEM((2, RANGE_ROWS, 2, ROWS, LANES), jnp.float32),
        ],
        out_shape=outs,
        compiler_params=pltpu.CompilerParams(vmem_limit_bytes=VMEM_LIMIT),
        cost_estimate=pl.CostEstimate(flops=10**9, bytes_accessed=4 * 10**6, transcendentals=0),
        name="profiles",
    )(cp_offset, pilot_offsets, places, spectrum, own, other, spot, high, low, twist)


def doppler_plain(own_profiles, symbols):
    turned = lax.all_to_all(own_profiles, "sub", split_axis=3, concat_axis=1, tiled=True)
    turned = lax.all_to_all(turned, "sym", split_axis=3, concat_axis=2, tiled=True)
    ids = np.arange(symbols)
    angle = TWO_PI / symbols * (ids[:, None] * ids[None, :] % symbols)
    c, s = np.cos(angle).astype(np.float32), np.sin(angle).astype(np.float32)
    product = lambda t, x: jnp.einsum("fm,cmq->cfq", t, x, precision=HIGHEST)
    re = product(c, turned[0]) + product(s, turned[1])
    im = product(c, turned[1]) - product(s, turned[0])
    return lax.all_to_all(jnp.stack([re, im]), "sym", split_axis=2, concat_axis=3, tiled=True)


def doppler_paired(pieces, places, syms, subs):
    got = [pieces[0]] + [
        lax.ppermute(pieces[d], "sym", [(i, i ^ d) for i in range(syms)]) for d in range(1, syms)
    ]
    symbols, rows = got[0].shape[:2]
    coded = pl.pallas_call(
        doppler_kernel,
        in_specs=[IN_SMEM] + [IN_VMEM] * syms,
        out_specs=IN_VMEM,
        out_shape=jax.ShapeDtypeStruct((syms * subs, symbols + 1, 2 * ROWS, LANES), jnp.int16),
        scratch_shapes=[
            pltpu.VMEM((syms, symbols, rows, 2, ROWS, LANES), jnp.float32),
            pltpu.VMEM((rows, syms * symbols, 2, ROWS, LANES), jnp.float32),
        ],
        compiler_params=pltpu.CompilerParams(vmem_limit_bytes=VMEM_LIMIT),
        name="doppler",
    )(places, *got)
    coded = lax.all_to_all(coded, ("sym", "sub"), split_axis=0, concat_axis=0)
    out = pl.pallas_call(
        join_kernel,
        in_specs=[IN_VMEM],
        out_specs=IN_VMEM,
        out_shape=jax.ShapeDtypeStruct((2, symbols, subs * ROWS, syms * LANES), jnp.float32),
        compiler_params=pltpu.CompilerParams(vmem_limit_bytes=VMEM_LIMIT),
        name="join",
    )(coded)
    return jnp.transpose(out, (0, 2, 1, 3))


def local(samples, constellation_index, pilot_offsets, cp_offset):
    syms, subs = lax.axis_size("sym"), lax.axis_size("sub")
    place, sub = lax.axis_index("sym"), lax.axis_index("sub")
    channels, symbols = samples.shape[1:3]
    paired = syms == 4 and syms * subs == RANGE_ROWS and channels == ROWS and symbols == 6
    half = ACTIVE_TONES // 2
    if paired:
        own = constellation_index
        other = lax.ppermute(own, "sub", [(0, 1), (1, 0)])
        swapped = sub
    else:
        index = lax.all_gather(constellation_index, "sub", axis=1, tiled=True)
        own, other, swapped = index[:, :half], index[:, half:], jnp.zeros_like(sub)
    windows = jnp.transpose(samples, (0, 2, 1, 3))
    short = -channels % ROWS
    if short:
        windows = jnp.pad(windows, ((0, 0), (0, 0), (0, short), (0, 0)))
    spectrum = spectra(windows, cp_offset)
    scale = ROOT_FORTYTWO / math.sqrt(WHOLE * ACTIVE_TONES * symbols * syms)
    places = jnp.stack([place, swapped])
    got = profiles(
        spectrum, own, other, pilot_offsets, cp_offset, places, syms if paired else 0, scale
    )
    if paired:
        return doppler_paired(got, places, syms, subs)
    own = jnp.transpose(got[0], (2, 1, 4, 0, 3, 5))
    own = own.reshape(2, channels + short, symbols, GUARD_SAMPLES)[:, :channels]
    return doppler_plain(own, symbols * syms)


def solution(mesh):
    return jax.shard_map(
        local,
        mesh=mesh,
        in_specs=(
            P(None, ("chan", "sub"), "sym", None),
            P(("chan", "sym"), "sub"),
            P("sym"),
            P(("chan", "sym")),
        ),
        out_specs=P(None, "chan", "sym", "sub"),
        check_vma=False,
    )
```

```python
import functools
import math

import jax
import jax.numpy as jnp
import ml_dtypes
import numpy as np
from jax import lax
from jax.experimental import pallas as pl
from jax.experimental.pallas import tpu as pltpu
from jax.sharding import PartitionSpec as P

OUTER_FACTOR = 64
INNER_FACTOR = 128
ACTIVE_TONES = 4096
GUARD_SAMPLES = 1024
SMOOTH_HALFSPAN = 48
PSP = 12

TWO_PI = 2.0 * math.pi
ROOT_FORTYTWO = math.sqrt(42.0)
HIGHEST = lax.Precision.HIGHEST

WHOLE = OUTER_FACTOR * INNER_FACTOR
FOLD = 32
WIDE = WHOLE // FOLD
LANES = 128
ROWS = 8
LOWEST = (WHOLE - ACTIVE_TONES) // 2
RANGE_ROWS = GUARD_SAMPLES // LANES
VMEM_LIMIT = 48 * 1024 * 1024
SPECTRA_VMEM_LIMIT = 52 * 1024 * 1024


def split_table(table):
    high = table.astype(np.float32).astype(ml_dtypes.bfloat16)
    low = (table - high.astype(np.float64)).astype(np.float32).astype(ml_dtypes.bfloat16)
    return high, low


def turning(sign, product, period):
    angle = sign * TWO_PI / period * (product % period)
    cosine, sine = np.cos(angle), np.sin(angle)
    return np.block([[cosine, sine], [-sine, cosine]])


def residue_order():
    row = np.arange(FOLD)
    return row // 8 + 4 * (row % 8)


def range_tables():
    j = np.arange(ACTIVE_TONES // FOLD)
    l = np.arange(LANES)
    high, low = split_table(turning(1, j[:, None] * l[None, :], ACTIVE_TONES // FOLD))
    angle = TWO_PI / ACTIVE_TONES * (residue_order()[:, None] * l[None, :])
    return high, low, np.stack([np.cos(angle), np.sin(angle)]).astype(np.float32)


def times(x, turn):
    re, im = x
    turn = turn % 1.0
    eighth = round(turn * 8)
    if abs(turn * 8 - eighth) < 1e-9:
        eighth %= 8
        if eighth % 2 == 0:
            return [(re, im), (-im, re), (-re, -im), (im, -re)][eighth // 2]
        half = math.sqrt(0.5)
        add, sub = (re + im) * half, (re - im) * half
        return [(sub, add), (-add, sub), (-sub, -add), (add, -sub)][eighth // 2]
    c, s = math.cos(TWO_PI * turn), math.sin(TWO_PI * turn)
    return re * c - im * s, re * s + im * c


def plus(x, y):
    return x[0] + y[0], x[1] + y[1]


def minus(x, y):
    return x[0] - y[0], x[1] - y[1]


def turn_quarter(x, sign):
    return (-x[1], x[0]) if sign > 0 else (x[1], -x[0])


def dft4(x, sign):
    a, b = plus(x[0], x[2]), minus(x[0], x[2])
    c, d = plus(x[1], x[3]), turn_quarter(minus(x[1], x[3]), sign)
    return [plus(a, c), plus(b, d), minus(a, c), minus(b, d)]


def dft8(x, sign):
    even, odd = dft4(x[0::2], sign), dft4(x[1::2], sign)
    odd = [times(o, sign * k / 8) for k, o in enumerate(odd)]
    return [plus(e, o) for e, o in zip(even, odd)] + [minus(e, o) for e, o in zip(even, odd)]


def dft3(x, sign):
    total, diff = plus(x[1], x[2]), minus(x[1], x[2])
    mid = (x[0][0] - 0.5 * total[0], x[0][1] - 0.5 * total[1])
    root = sign * math.sqrt(0.75)
    side = (-root * diff[1], root * diff[0])
    return [plus(x[0], total), plus(mid, side), minus(mid, side)]


def dft6(x, sign):
    even, odd = dft3(x[0::2], sign), dft3(x[1::2], sign)
    odd = [times(o, sign * k / 6) for k, o in enumerate(odd)]
    return [plus(e, o) for e, o in zip(even, odd)] + [minus(e, o) for e, o in zip(even, odd)]


def split_rows(x):
    high = x.astype(jnp.bfloat16)
    return high, (x - high.astype(jnp.float32)).astype(jnp.bfloat16)


def dot(x, w):
    return lax.dot_general(x, w, (((1,), (0,)), ((), ())), preferred_element_type=jnp.float32)


def split_product(rows_ref, high_ref, low_ref):
    width = high_ref.shape[0]
    high, low = rows_ref[:, :width], rows_ref[:, width:]
    return dot(high, high_ref[...]) + dot(low, high_ref[...]) + dot(high, low_ref[...])


def code_scale(peak):
    return jnp.ceil(jnp.log2(jnp.maximum(peak, 1e-30)) * 64.0)


def encode(x, code):
    size = jnp.sqrt(jnp.abs(x)) * (32767.0 * jnp.exp2(code * (-1.0 / 128.0))) + 0.5
    return jnp.where(x < 0.0, -size, size).astype(jnp.int32)


def decode(n, code):
    n = n.astype(jnp.int32).astype(jnp.float32)
    return n * jnp.abs(n) * (jnp.exp2(code * (1.0 / 64.0)) * (1.0 / 32767.0**2))


def peak_of(values):
    top = functools.reduce(jnp.maximum, [jnp.abs(v) for v in values])
    return jnp.max(top, axis=1, keepdims=True)


def phase(product, period):
    n = product & (period - 1)
    quarter = (n + period // 8) // (period // 4)
    x = (n - quarter * (period // 4)).astype(jnp.float32) * (TWO_PI / period)
    y = x * x
    sine = x * (1 + y * (-1 / 6 + y * (1 / 120 + y * (-1 / 5040 + y * (1 / 362880)))))
    cosine = 1 + y * (-1 / 2 + y * (1 / 24 + y * (-1 / 720 + y * (1 / 40320 - y * (1 / 3628800)))))
    odd, low, turned = (quarter & 1) == 1, (quarter & 2) == 2, ((quarter + 1) & 2) == 2
    c, s = jnp.where(odd, sine, cosine), jnp.where(odd, cosine, sine)
    return jnp.where(turned, -c, c), jnp.where(low, -s, s)


def spectrum_kernel(off_hbm, x_hbm, out_ref, off_ref, x_ref, high_ref, low_ref, twist_ref, mid_ref, rows_ref, sems):
    symbols, groups = out_ref.shape[:2]
    tones = ACTIVE_TONES // FOLD
    tasks = [(m, g) for m in range(symbols) for g in range(groups)]
    fetches = []
    for n, (m, g) in enumerate(tasks):
        source = x_hbm.at[:, m, g * ROWS : (g + 1) * ROWS, :]
        fetches.append(pltpu.make_async_copy(source, x_ref.at[n], sems.at[n]))
        fetches[-1].start()
        if n == 0:
            starts = pltpu.make_async_copy(off_hbm, off_ref, sems.at[len(tasks)])
            starts.start()
    row = lax.broadcasted_iota(jnp.int32, (ROWS, WIDE), 0)
    lane = lax.broadcasted_iota(jnp.int32, (ROWS, WIDE), 1)
    for p in range(4):
        c, s = phase((p + 4 * row) * lane, WHOLE)
        twist_ref[0, p * 8 : p * 8 + 8], twist_ref[1, p * 8 : p * 8 + 8] = c, -s
    row = lax.broadcasted_iota(jnp.int32, (2 * ROWS, tones), 0)
    lane = lax.broadcasted_iota(jnp.int32, (2 * ROWS, tones), 1)
    for b in range(0, WIDE, 2 * ROWS):
        c, s = phase((b + row) * (LOWEST // FOLD + lane), WIDE)
        upper, lower = slice(b, b + 2 * ROWS), slice(WIDE + b, WIDE + b + 2 * ROWS)
        (c, c_low), (s, s_low) = split_rows(c), split_rows(s)
        high_ref[upper, :tones], high_ref[upper, tones:] = c, -s
        high_ref[lower, :tones], high_ref[lower, tones:] = s, c
        low_ref[upper, :tones], low_ref[upper, tones:] = c_low, -s_low
        low_ref[lower, :tones], low_ref[lower, tones:] = s_low, c_low
    lane = lax.broadcasted_iota(jnp.int32, (ROWS, LANES), 1)
    halves = WIDE // LANES
    starts.wait()
    for n, (m, g) in enumerate(tasks):
        fetches[n].wait()
        off, slot = off_ref[m], n % 2
        base = n * FOLD * ROWS

        def sample(part, chunk):
            value = x_ref[n, part, :, chunk * LANES : (chunk + 1) * LANES]
            if chunk * LANES < GUARD_SAMPLES:
                wrapped = x_ref[n, part, :, WHOLE + chunk * LANES : WHOLE + (chunk + 1) * LANES]
                value = jnp.where(lane < off - chunk * LANES, wrapped, value)
            return value

        for h in range(halves):
            for v in range(8):
                chunks = [halves * (8 * u + v) + h for u in range(4)]
                y = dft4([(sample(0, c), sample(1, c)) for c in chunks], -1)
                for p in range(4):
                    at = (slot, h, p, v)
                    mid_ref[at + (0,)], mid_ref[at + (1,)] = times(y[p], -v * p / FOLD)
        for p in range(4):
            for h in range(halves):
                at = (slot, h, p)
                y = dft8([(mid_ref[at + (v, 0)], mid_ref[at + (v, 1)]) for v in range(8)], -1)
                for q in range(0, 8, 2):
                    pair = []
                    for row in (p * 8 + q, p * 8 + q + 1):
                        re, im = y[row - p * 8]
                        c = twist_ref[0, row : row + 1, h * LANES : (h + 1) * LANES]
                        s = twist_ref[1, row : row + 1, h * LANES : (h + 1) * LANES]
                        pair.append((re * c - im * s, re * s + im * c))
                    at_rows = slice(base + (p * 8 + q) * ROWS, base + (p * 8 + q + 2) * ROWS)
                    for part in range(2):
                        high, low = split_rows(jnp.concatenate([pair[0][part], pair[1][part]], axis=0))
                        column = part * WIDE + h * LANES
                        rows_ref[at_rows, column : column + LANES] = high
                        rows_ref[at_rows, 2 * WIDE + column : 2 * WIDE + column + LANES] = low
    out_ref[...] = split_product(rows_ref, high_ref, low_ref).reshape(out_ref.shape)


def symbol_phases(off_ref, symbols):
    tones = ACTIVE_TONES // FOLD
    row = lax.broadcasted_iota(jnp.int32, (ROWS, tones), 0)
    lane = lax.broadcasted_iota(jnp.int32, (ROWS, tones), 1)
    by_row = by_lane = jnp.zeros((ROWS, tones), jnp.int32)
    for m in range(symbols):
        by_row = jnp.where(row == m, off_ref[m], by_row)
        by_lane = jnp.where(lane == m, off_ref[m], by_lane)

    by_lanes = phase(by_row * (LOWEST + FOLD * lane), WHOLE)
    return by_lanes, [phase(by_lane * (p + 4 * row), WHOLE) for p in range(4)]


def profile_kernel(
    syms, scale, off_ref, pilot_ref, place_ref, s_ref, own_ref, other_ref, spot_ref, high_ref, low_ref, twist_ref, *refs
):
    outs = refs[: max(syms, 1)]
    flat_ref, turned_ref, gain_ref, ratio_ref, num_ref, rows_ref, range_ref, prof_ref = refs[max(syms, 1) :]
    symbols, groups = s_ref.shape[:2]
    tones = ACTIVE_TONES // FOLD
    own_place, swapped = place_ref[0], place_ref[1] > 0
    for j in range(FOLD // 2):
        at = slice(j * LANES, (j + 1) * LANES)
        own, other = own_ref[:, at], other_ref[:, at]
        flat_ref[j, :symbols] = jnp.where(swapped, other, own).astype(jnp.float32)
        flat_ref[FOLD // 2 + j, :symbols] = jnp.where(swapped, own, other).astype(jnp.float32)
    (lane_re, lane_im), row_phases = symbol_phases(off_ref, symbols)

    for m in range(symbols):
        slot = m % 2
        offset = pilot_ref[m]
        stood = flat_ref[:, m, :].T.astype(jnp.bfloat16)
        spread = dot(stood, spot_ref[...])
        turned_ref[slot] = sum(
            spread[FOLD * l : FOLD * (l + 1), tones * l : tones * (l + 1)] for l in range(LANES // FOLD)
        )
        row = lax.broadcasted_iota(jnp.int32, (ROWS, tones), 0)
        lane = lax.broadcasted_iota(jnp.int32, (ROWS, tones), 1)
        first_after = ACTIVE_TONES + lax.rem(offset + PSP * ACTIVE_TONES - ACTIVE_TONES, PSP)
        span = SMOOTH_HALFSPAN + 1
        for p in range(4):
            at = slice(p * 8, p * 8 + 8)
            index = turned_ref[slot, pl.ds(p, 8, stride=4), :]
            high_bits = jnp.floor(index * 0.125)
            level_re = 2.0 * (index - 8.0 * high_bits) - 7.0
            level_im = 2.0 * high_bits - 7.0
            factor = scale / (level_re * level_re + level_im * level_im)
            a, b = lane_re[m : m + 1, :], lane_im[m : m + 1, :]
            c, s = row_phases[p][0][:, m : m + 1], row_phases[p][1][:, m : m + 1]
            c, s = a * c - b * s, a * s + b * c
            gain_ref[slot, 0, at] = (c * level_re + s * level_im) * factor
            gain_ref[slot, 1, at] = (s * level_re - c * level_im) * factor
            k = p + 4 * row + FOLD * lane
            is_pilot = lax.rem(k + (PSP - offset), PSP) == 0
            total = jnp.where(is_pilot, 201.0, 200.0)
            for i in range(4):
                before = span - (k - offset + PSP * (i + 1))
                after = span - (first_after + PSP * i - k)
                total -= (jnp.maximum(before, 0) + jnp.maximum(after, 0)).astype(jnp.float32)
            gain_ref[slot, 2, at] = 1.0 / total
            gain_ref[slot, 3, at] = jnp.where(is_pilot, 1.0, 0.0)

        for g in range(groups):
            base = (m * groups + g) * FOLD * ROWS
            for i in range(FOLD):
                re = s_ref[m, g, i * ROWS : (i + 1) * ROWS, :tones]
                im = s_ref[m, g, i * ROWS : (i + 1) * ROWS, tones:]
                c = gain_ref[slot, 0, i : i + 1, :]
                s = gain_ref[slot, 1, i : i + 1, :]
                ratio_ref[slot, 0, i] = re * c - im * s
                ratio_ref[slot, 1, i] = re * s + im * c

            r = offset & 3
            for part in range(2):
                picked = [
                    ratio_ref[slot, part, r * 8 + a] * gain_ref[slot, 3, pl.ds(r * 8 + a, 1), :] for a in range(8)
                ]

                def pilot(i):
                    b, a = i // 8, i % 8
                    if b == 0:
                        return picked[a]
                    rolled = pltpu.roll(picked[a], (-b) % tones, 1)
                    return jnp.where((lane < tones - b) if b > 0 else (lane >= -b), rolled, 0.0)

                q = {i: pilot(i) for i in range(-13, 21)}
                slope = sum(q[i] for i in range(0, 12)) - sum(q[i] for i in range(-12, 0))
                value = sum((49 - 4 * abs(i + 1)) * q[i] for i in range(-13, 12))
                for a in range(-1, 8):
                    for s in range(4):
                        to = r + s
                        here = value if s == 0 else value + s * slope - q[a - 12]
                        num_ref[slot, part, (to & 3) * 10 + a + 1 + (to >> 2)] = here
                    value = value + 4.0 * slope - q[a - 12] + q[a + 13]
                    if a < 7:
                        slope = slope + q[a + 13] - 2.0 * q[a + 1] + q[a - 11]

            for i in range(0, FOLD, 2):
                for part in range(2):
                    pair = []
                    for n in (i, i + 1):
                        smooth = num_ref[slot, part, (n // 8) * 10 + n % 8 + 1] * gain_ref[slot, 2, n : n + 1, :]
                        pair.append(ratio_ref[slot, part, n] - smooth)
                    high, low = split_rows(jnp.concatenate(pair, axis=0))
                    at = slice(base + i * ROWS, base + (i + 2) * ROWS)
                    rows_ref[at, part * tones : (part + 1) * tones] = high
                    rows_ref[at, (2 + part) * tones : (3 + part) * tones] = low

    range_ref[...] = split_product(rows_ref, high_ref, low_ref)
    lane = lax.broadcasted_iota(jnp.int32, (ROWS, LANES), 1)
    codes = jnp.zeros((ROWS, LANES), jnp.float32)
    for m in range(symbols):
        for g in range(groups):
            base, slot = (m * groups + g) * FOLD * ROWS, m % 2
            sums = None
            for p in range(4):
                x = []
                for i in range(p * 8, p * 8 + 8):
                    at = slice(base + i * ROWS, base + (i + 1) * ROWS)
                    re, im = range_ref[at, :LANES], range_ref[at, LANES:]
                    c, s = twist_ref[0, i : i + 1, :], twist_ref[1, i : i + 1, :]
                    x.append((re * c - im * s, re * s + im * c))
                y = [times(v, p * h / FOLD) for h, v in enumerate(dft8(x, 1))]
                sums = y if sums is None else [plus(a, b) for a, b in zip(sums, y)]
            if not syms:
                for h in range(RANGE_ROWS):
                    outs[0][m, g, 0, h], outs[0][m, g, 1, h] = sums[h]
                continue
            code = code_scale(peak_of([v for pair in sums for v in pair]))
            codes = jnp.where(lane == m, code, codes)
            for h in range(RANGE_ROWS):
                prof_ref[slot, h, 0], prof_ref[slot, h, 1] = sums[h]
            for h in range(RANGE_ROWS // syms):
                for d in range(syms):
                    row = syms * h + (own_place ^ d)
                    if d == 0:
                        outs[0][m, h] = prof_ref[slot, row]
                        continue
                    packed = [encode(prof_ref[slot, row, part], code) for part in range(2)]
                    outs[d][m * (RANGE_ROWS // syms) + h] = jnp.concatenate(packed, axis=0).astype(jnp.int16)
    if syms:
        packed = jnp.concatenate([codes, codes], axis=0).astype(jnp.int32).astype(jnp.int16)
        for d in range(1, syms):
            outs[d][symbols * (RANGE_ROWS // syms)] = packed


SEND_ORDER = (3, 1, 2)


def doppler_kernel(place_ref, own_ref, *refs):
    pieces, (out_ref, turned_ref, spread_ref) = refs[:3], refs[3:]
    symbols, rows = own_ref.shape[:2]
    syms = 4
    own = place_ref[0]
    turned_ref[own] = own_ref[...]
    for d, piece in zip(SEND_ORDER, pieces):
        codes = piece[symbols * rows].astype(jnp.int32).astype(jnp.float32)
        for m in range(symbols):
            code = codes[:, m : m + 1]
            for h in range(rows):
                value = decode(piece[m * rows + h], code)
                turned_ref[own ^ d, m, h, 0], turned_ref[own ^ d, m, h, 1] = value[:ROWS], value[ROWS:]
    for h in range(rows):
        grid, bins = {}, {}
        for m in range(symbols):
            x = [(turned_ref[s, m, h, 0], turned_ref[s, m, h, 1]) for s in range(syms)]
            for p, y in enumerate(dft4(x, -1)):
                grid[p, m] = times(y, -m * p / (syms * symbols))
        for p in range(syms):
            for q, y in enumerate(dft6([grid[p, m] for m in range(symbols)], -1)):
                f = p + syms * q
                spread_ref[h, f, 0], spread_ref[h, f, 1] = y
    for s in range(syms):
        for h in range(rows):
            values = [spread_ref[h, s * symbols + f] for f in range(symbols)]
            code = code_scale(peak_of([v[part] for v in values for part in range(2)]))
            to = s * rows + h
            for f in range(symbols):
                packed = [encode(values[f][part], code) for part in range(2)]
                out_ref[to, f] = jnp.concatenate(packed, axis=0).astype(jnp.int16)
            codes = jnp.broadcast_to(code, (ROWS, LANES)).astype(jnp.int32)
            out_ref[to, symbols] = jnp.concatenate([codes, codes], axis=0).astype(jnp.int16)


def join_kernel(piece_ref, out_ref):
    _, symbols, channels, width = out_ref.shape
    subs = channels // ROWS
    for n in range(piece_ref.shape[0]):
        s, u = n // subs, n % subs
        code = piece_ref[n, symbols].astype(jnp.int32).astype(jnp.float32)
        gain = jnp.exp2(code * (1.0 / 64.0)) * (1.0 / 32767.0**2)
        for f in range(symbols):
            value = piece_ref[n, f].astype(jnp.int32).astype(jnp.float32)
            value = value * jnp.abs(value) * gain
            for part in range(2):
                at = slice(part * ROWS, (part + 1) * ROWS)
                out_ref[part, f, u * ROWS : (u + 1) * ROWS, s * LANES : (s + 1) * LANES] = value[at]


IN_VMEM = pl.BlockSpec(memory_space=pltpu.VMEM)
IN_SMEM = pl.BlockSpec(memory_space=pltpu.SMEM)
IN_HBM = pl.BlockSpec(memory_space=pltpu.HBM)


def spectra(windows, cp_offset):
    _, symbols, channels, record = windows.shape
    groups = channels // ROWS
    tones = ACTIVE_TONES // FOLD
    return pl.pallas_call(
        spectrum_kernel,
        in_specs=[IN_HBM, IN_HBM],
        out_specs=IN_VMEM,
        scratch_shapes=[
            pltpu.SMEM((symbols,), jnp.int32),
            pltpu.VMEM((symbols * groups, 2, ROWS, record), jnp.float32),
            pltpu.VMEM((2 * WIDE, 2 * tones), jnp.bfloat16),
            pltpu.VMEM((2 * WIDE, 2 * tones), jnp.bfloat16),
            pltpu.VMEM((2, FOLD, WIDE), jnp.float32),
            pltpu.VMEM((2, WIDE // LANES, 4, 8, 2, ROWS, LANES), jnp.float32),
            pltpu.VMEM((symbols * groups * FOLD * ROWS, 4 * WIDE), jnp.bfloat16),
            pltpu.SemaphoreType.DMA((symbols * groups + 1,)),
        ],
        out_shape=jax.ShapeDtypeStruct((symbols, groups, FOLD * ROWS, 2 * tones), jnp.float32),
        compiler_params=pltpu.CompilerParams(vmem_limit_bytes=SPECTRA_VMEM_LIMIT),
        cost_estimate=pl.CostEstimate(flops=2 * 10**9, bytes_accessed=8 * 10**6, transcendentals=0),
        name="spectra",
    )(cp_offset, windows)


def profiles(spectrum, own, other, pilot_offsets, cp_offset, places, syms, scale):
    symbols, groups = spectrum.shape[:2]
    high, low, twist = range_tables()
    tones = ACTIVE_TONES // FOLD
    n, column = np.arange(FOLD)[:, None], np.arange(LANES // FOLD * tones)[None, :]
    spot = (column % tones == LANES // FOLD * n + column // tones).astype(ml_dtypes.bfloat16)
    if syms:
        rows = RANGE_ROWS // syms
        piece = jax.ShapeDtypeStruct((symbols * rows + 1, 2 * ROWS, LANES), jnp.int16)
        outs = [jax.ShapeDtypeStruct((symbols, rows, 2, ROWS, LANES), jnp.float32)] + [piece] * (syms - 1)
    else:
        outs = [jax.ShapeDtypeStruct((symbols, groups, 2, RANGE_ROWS, ROWS, LANES), jnp.float32)]
    return pl.pallas_call(
        functools.partial(profile_kernel, syms, scale),
        in_specs=[IN_SMEM] * 3 + [IN_VMEM] * 7,
        out_specs=[IN_VMEM] * len(outs),
        scratch_shapes=[
            pltpu.VMEM((FOLD, ROWS, LANES), jnp.float32),
            pltpu.VMEM((2, FOLD, tones), jnp.float32),
            pltpu.VMEM((2, 4, FOLD, tones), jnp.float32),
            pltpu.VMEM((2, 2, FOLD, ROWS, tones), jnp.float32),
            pltpu.VMEM((2, 2, 40, ROWS, tones), jnp.float32),
            pltpu.VMEM((symbols * groups * FOLD * ROWS, 4 * tones), jnp.bfloat16),
            pltpu.VMEM((symbols * groups * FOLD * ROWS, 2 * LANES), jnp.float32),
            pltpu.VMEM((2, RANGE_ROWS, 2, ROWS, LANES), jnp.float32),
        ],
        out_shape=outs,
        compiler_params=pltpu.CompilerParams(vmem_limit_bytes=VMEM_LIMIT),
        cost_estimate=pl.CostEstimate(flops=10**9, bytes_accessed=4 * 10**6, transcendentals=0),
        name="profiles",
    )(cp_offset, pilot_offsets, places, spectrum, own, other, spot, high, low, twist)


def doppler_plain(own_profiles, symbols):
    turned = lax.all_to_all(own_profiles, "sub", split_axis=3, concat_axis=1, tiled=True)
    turned = lax.all_to_all(turned, "sym", split_axis=3, concat_axis=2, tiled=True)
    ids = np.arange(symbols)
    angle = TWO_PI / symbols * (ids[:, None] * ids[None, :] % symbols)
    c, s = np.cos(angle).astype(np.float32), np.sin(angle).astype(np.float32)
    product = lambda t, x: jnp.einsum("fm,cmq->cfq", t, x, precision=HIGHEST)
    re = product(c, turned[0]) + product(s, turned[1])
    im = product(c, turned[1]) - product(s, turned[0])
    return lax.all_to_all(jnp.stack([re, im]), "sym", split_axis=2, concat_axis=3, tiled=True)


def doppler_paired(pieces, places, syms, subs):
    got = [pieces[0]] + [
        lax.ppermute(pieces[d], "sym", [(i, i ^ d) for i in range(syms)]) for d in SEND_ORDER
    ]
    symbols, rows = got[0].shape[:2]
    coded = pl.pallas_call(
        doppler_kernel,
        in_specs=[IN_SMEM] + [IN_VMEM] * syms,
        out_specs=IN_VMEM,
        out_shape=jax.ShapeDtypeStruct((syms * subs, symbols + 1, 2 * ROWS, LANES), jnp.int16),
        scratch_shapes=[
            pltpu.VMEM((syms, symbols, rows, 2, ROWS, LANES), jnp.float32),
            pltpu.VMEM((rows, syms * symbols, 2, ROWS, LANES), jnp.float32),
        ],
        compiler_params=pltpu.CompilerParams(vmem_limit_bytes=VMEM_LIMIT),
        name="doppler",
    )(places, *got)
    coded = lax.all_to_all(coded, ("sym", "sub"), split_axis=0, concat_axis=0)
    out = pl.pallas_call(
        join_kernel,
        in_specs=[IN_VMEM],
        out_specs=IN_VMEM,
        out_shape=jax.ShapeDtypeStruct((2, symbols, subs * ROWS, syms * LANES), jnp.float32),
        compiler_params=pltpu.CompilerParams(vmem_limit_bytes=VMEM_LIMIT),
        name="join",
    )(coded)
    return jnp.transpose(out, (0, 2, 1, 3))


def local(samples, constellation_index, pilot_offsets, cp_offset):
    syms, subs = lax.axis_size("sym"), lax.axis_size("sub")
    place, sub = lax.axis_index("sym"), lax.axis_index("sub")
    channels, symbols = samples.shape[1:3]
    paired = syms == 4 and syms * subs == RANGE_ROWS and channels == ROWS and symbols == 6
    half = ACTIVE_TONES // 2
    if paired:
        own = constellation_index
        other = lax.ppermute(own, "sub", [(0, 1), (1, 0)])
        swapped = sub
    else:
        index = lax.all_gather(constellation_index, "sub", axis=1, tiled=True)
        own, other, swapped = index[:, :half], index[:, half:], jnp.zeros_like(sub)
    windows = jnp.transpose(samples, (0, 2, 1, 3))
    short = -channels % ROWS
    if short:
        windows = jnp.pad(windows, ((0, 0), (0, 0), (0, short), (0, 0)))
    spectrum = spectra(windows, cp_offset)
    scale = ROOT_FORTYTWO / math.sqrt(WHOLE * ACTIVE_TONES * symbols * syms)
    places = jnp.stack([place, swapped])
    got = profiles(
        spectrum, own, other, pilot_offsets, cp_offset, places, syms if paired else 0, scale
    )
    if paired:
        return doppler_paired(got, places, syms, subs)
    own = jnp.transpose(got[0], (2, 1, 4, 0, 3, 5))
    own = own.reshape(2, channels + short, symbols, GUARD_SAMPLES)[:, :channels]
    return doppler_plain(own, symbols * syms)


def solution(mesh):
    return jax.shard_map(
        local,
        mesh=mesh,
        in_specs=(
            P(None, ("chan", "sub"), "sym", None),
            P(("chan", "sym"), "sub"),
            P("sym"),
            P(("chan", "sym")),
        ),
        out_specs=P(None, "chan", "sym", "sub"),
        check_vma=False,
    )
```

```python
import functools
import math

import jax
import jax.numpy as jnp
import ml_dtypes
import numpy as np
from jax import lax
from jax.experimental import pallas as pl
from jax.experimental.pallas import tpu as pltpu
from jax.sharding import PartitionSpec as P

OUTER_FACTOR = 64
INNER_FACTOR = 128
ACTIVE_TONES = 4096
GUARD_SAMPLES = 1024
SMOOTH_HALFSPAN = 48
PSP = 12

TWO_PI = 2.0 * math.pi
ROOT_FORTYTWO = math.sqrt(42.0)
HIGHEST = lax.Precision.HIGHEST

WHOLE = OUTER_FACTOR * INNER_FACTOR
FOLD = 32
WIDE = WHOLE // FOLD
LANES = 128
ROWS = 8
LOWEST = (WHOLE - ACTIVE_TONES) // 2
RANGE_ROWS = GUARD_SAMPLES // LANES
VMEM_LIMIT = 48 * 1024 * 1024
SPECTRA_VMEM_LIMIT = 52 * 1024 * 1024


def split_table(table):
    high = table.astype(np.float32).astype(ml_dtypes.bfloat16)
    low = (table - high.astype(np.float64)).astype(np.float32).astype(ml_dtypes.bfloat16)
    return high, low


def turning(sign, product, period):
    angle = sign * TWO_PI / period * (product % period)
    cosine, sine = np.cos(angle), np.sin(angle)
    return np.block([[cosine, sine], [-sine, cosine]])


def residue_order():
    row = np.arange(FOLD)
    return row // 8 + 4 * (row % 8)


def range_tables():
    j = np.arange(ACTIVE_TONES // FOLD)
    l = np.arange(LANES)
    high, low = split_table(turning(1, j[:, None] * l[None, :], ACTIVE_TONES // FOLD))
    angle = TWO_PI / ACTIVE_TONES * (residue_order()[:, None] * l[None, :])
    return high, low, np.stack([np.cos(angle), np.sin(angle)]).astype(np.float32)


def times(x, turn):
    re, im = x
    turn = turn % 1.0
    eighth = round(turn * 8)
    if abs(turn * 8 - eighth) < 1e-9:
        eighth %= 8
        if eighth % 2 == 0:
            return [(re, im), (-im, re), (-re, -im), (im, -re)][eighth // 2]
        half = math.sqrt(0.5)
        add, sub = (re + im) * half, (re - im) * half
        return [(sub, add), (-add, sub), (-sub, -add), (add, -sub)][eighth // 2]
    c, s = math.cos(TWO_PI * turn), math.sin(TWO_PI * turn)
    return re * c - im * s, re * s + im * c


def plus(x, y):
    return x[0] + y[0], x[1] + y[1]


def minus(x, y):
    return x[0] - y[0], x[1] - y[1]


def turn_quarter(x, sign):
    return (-x[1], x[0]) if sign > 0 else (x[1], -x[0])


def dft4(x, sign):
    a, b = plus(x[0], x[2]), minus(x[0], x[2])
    c, d = plus(x[1], x[3]), turn_quarter(minus(x[1], x[3]), sign)
    return [plus(a, c), plus(b, d), minus(a, c), minus(b, d)]


def dft8(x, sign):
    even, odd = dft4(x[0::2], sign), dft4(x[1::2], sign)
    odd = [times(o, sign * k / 8) for k, o in enumerate(odd)]
    return [plus(e, o) for e, o in zip(even, odd)] + [minus(e, o) for e, o in zip(even, odd)]


def dft3(x, sign):
    total, diff = plus(x[1], x[2]), minus(x[1], x[2])
    mid = (x[0][0] - 0.5 * total[0], x[0][1] - 0.5 * total[1])
    root = sign * math.sqrt(0.75)
    side = (-root * diff[1], root * diff[0])
    return [plus(x[0], total), plus(mid, side), minus(mid, side)]


def dft6(x, sign):
    even, odd = dft3(x[0::2], sign), dft3(x[1::2], sign)
    odd = [times(o, sign * k / 6) for k, o in enumerate(odd)]
    return [plus(e, o) for e, o in zip(even, odd)] + [minus(e, o) for e, o in zip(even, odd)]


def split_rows(x):
    high = x.astype(jnp.bfloat16)
    return high, (x - high.astype(jnp.float32)).astype(jnp.bfloat16)


def dot(x, w):
    return lax.dot_general(x, w, (((1,), (0,)), ((), ())), preferred_element_type=jnp.float32)


def split_product(rows_ref, high_ref, low_ref):
    width = high_ref.shape[0]
    high, low = rows_ref[:, :width], rows_ref[:, width:]
    return dot(high, high_ref[...]) + dot(low, high_ref[...]) + dot(high, low_ref[...])


def code_scale(peak):
    return jnp.ceil(jnp.log2(jnp.maximum(peak, 1e-30)) * 64.0)


def encode(x, code):
    size = jnp.sqrt(jnp.abs(x)) * (32767.0 * jnp.exp2(code * (-1.0 / 128.0))) + 0.5
    return jnp.where(x < 0.0, -size, size).astype(jnp.int32)


def decode(n, code):
    n = n.astype(jnp.int32).astype(jnp.float32)
    return n * jnp.abs(n) * (jnp.exp2(code * (1.0 / 64.0)) * (1.0 / 32767.0**2))


def peak_of(values):
    top = functools.reduce(jnp.maximum, [jnp.abs(v) for v in values])
    return jnp.max(top, axis=1, keepdims=True)


def phase(product, period):
    n = product & (period - 1)
    quarter = (n + period // 8) // (period // 4)
    x = (n - quarter * (period // 4)).astype(jnp.float32) * (TWO_PI / period)
    y = x * x
    sine = x * (1 + y * (-1 / 6 + y * (1 / 120 + y * (-1 / 5040 + y * (1 / 362880)))))
    cosine = 1 + y * (-1 / 2 + y * (1 / 24 + y * (-1 / 720 + y * (1 / 40320 - y * (1 / 3628800)))))
    odd, low, turned = (quarter & 1) == 1, (quarter & 2) == 2, ((quarter + 1) & 2) == 2
    c, s = jnp.where(odd, sine, cosine), jnp.where(odd, cosine, sine)
    return jnp.where(turned, -c, c), jnp.where(low, -s, s)


def spectrum_kernel(off_hbm, pilot_hbm, x_hbm, out_ref, table_ref, off_ref, pilot_ref, x_ref, high_ref, low_ref, twist_ref, mid_ref, rows_ref, sems):
    symbols, groups = out_ref.shape[:2]
    tones = ACTIVE_TONES // FOLD
    tasks = [(m, g) for m in range(symbols) for g in range(groups)]
    fetches = []
    for n, (m, g) in enumerate(tasks):
        source = x_hbm.at[:, m, g * ROWS : (g + 1) * ROWS, :]
        fetches.append(pltpu.make_async_copy(source, x_ref.at[n], sems.at[n]))
        fetches[-1].start()
        if n == 0:
            scalars = [
                pltpu.make_async_copy(off_hbm, off_ref, sems.at[len(tasks)]),
                pltpu.make_async_copy(pilot_hbm, pilot_ref, sems.at[len(tasks) + 1]),
            ]
            for scalar in scalars:
                scalar.start()
    row = lax.broadcasted_iota(jnp.int32, (ROWS, WIDE), 0)
    lane = lax.broadcasted_iota(jnp.int32, (ROWS, WIDE), 1)
    for p in range(4):
        c, s = phase((p + 4 * row) * lane, WHOLE)
        twist_ref[0, p * 8 : p * 8 + 8], twist_ref[1, p * 8 : p * 8 + 8] = c, -s
    row = lax.broadcasted_iota(jnp.int32, (2 * ROWS, tones), 0)
    lane = lax.broadcasted_iota(jnp.int32, (2 * ROWS, tones), 1)
    for b in range(0, WIDE, 2 * ROWS):
        c, s = phase((b + row) * (LOWEST // FOLD + lane), WIDE)
        upper, lower = slice(b, b + 2 * ROWS), slice(WIDE + b, WIDE + b + 2 * ROWS)
        (c, c_low), (s, s_low) = split_rows(c), split_rows(s)
        high_ref[upper, :tones], high_ref[upper, tones:] = c, -s
        high_ref[lower, :tones], high_ref[lower, tones:] = s, c
        low_ref[upper, :tones], low_ref[upper, tones:] = c_low, -s_low
        low_ref[lower, :tones], low_ref[lower, tones:] = s_low, c_low
    lane = lax.broadcasted_iota(jnp.int32, (ROWS, LANES), 1)
    halves = WIDE // LANES
    for scalar in scalars:
        scalar.wait()
    symbol_tables(off_ref, pilot_ref, table_ref)
    for n, (m, g) in enumerate(tasks):
        fetches[n].wait()
        off, slot = off_ref[m], n % 2
        base = n * FOLD * ROWS

        def sample(part, chunk):
            value = x_ref[n, part, :, chunk * LANES : (chunk + 1) * LANES]
            if chunk * LANES < GUARD_SAMPLES:
                wrapped = x_ref[n, part, :, WHOLE + chunk * LANES : WHOLE + (chunk + 1) * LANES]
                value = jnp.where(lane < off - chunk * LANES, wrapped, value)
            return value

        for h in range(halves):
            for v in range(8):
                chunks = [halves * (8 * u + v) + h for u in range(4)]
                y = dft4([(sample(0, c), sample(1, c)) for c in chunks], -1)
                for p in range(4):
                    at = (slot, h, p, v)
                    mid_ref[at + (0,)], mid_ref[at + (1,)] = times(y[p], -v * p / FOLD)
        for p in range(4):
            for h in range(halves):
                at = (slot, h, p)
                y = dft8([(mid_ref[at + (v, 0)], mid_ref[at + (v, 1)]) for v in range(8)], -1)
                for q in range(0, 8, 2):
                    pair = []
                    for row in (p * 8 + q, p * 8 + q + 1):
                        re, im = y[row - p * 8]
                        c = twist_ref[0, row : row + 1, h * LANES : (h + 1) * LANES]
                        s = twist_ref[1, row : row + 1, h * LANES : (h + 1) * LANES]
                        pair.append((re * c - im * s, re * s + im * c))
                    at_rows = slice(base + (p * 8 + q) * ROWS, base + (p * 8 + q + 2) * ROWS)
                    for part in range(2):
                        high, low = split_rows(jnp.concatenate([pair[0][part], pair[1][part]], axis=0))
                        column = part * WIDE + h * LANES
                        rows_ref[at_rows, column : column + LANES] = high
                        rows_ref[at_rows, 2 * WIDE + column : 2 * WIDE + column + LANES] = low
    out_ref[...] = split_product(rows_ref, high_ref, low_ref).reshape(out_ref.shape)


def symbol_tables(off_ref, pilot_ref, table_ref):
    symbols = table_ref.shape[0]
    tones = ACTIVE_TONES // FOLD
    row = lax.broadcasted_iota(jnp.int32, (ROWS, tones), 0)
    lane = lax.broadcasted_iota(jnp.int32, (ROWS, tones), 1)
    by_row = by_lane = jnp.zeros((ROWS, tones), jnp.int32)
    for m in range(symbols):
        by_row = jnp.where(row == m, off_ref[m], by_row)
        by_lane = jnp.where(lane == m, off_ref[m], by_lane)
    lane_re, lane_im = phase(by_row * (LOWEST + FOLD * lane), WHOLE)
    row_phases = [phase(by_lane * (p + 4 * row), WHOLE) for p in range(4)]
    span = SMOOTH_HALFSPAN + 1
    for m in range(symbols):
        offset = pilot_ref[m]
        first_after = ACTIVE_TONES + lax.rem(offset + PSP * ACTIVE_TONES - ACTIVE_TONES, PSP)
        a, b = lane_re[m : m + 1, :], lane_im[m : m + 1, :]
        for p in range(4):
            at = slice(p * 8, p * 8 + 8)
            c, s = row_phases[p][0][:, m : m + 1], row_phases[p][1][:, m : m + 1]
            table_ref[m, 0, at], table_ref[m, 1, at] = a * c - b * s, a * s + b * c
            k = p + 4 * row + FOLD * lane
            is_pilot = lax.rem(k + (PSP - offset), PSP) == 0
            total = jnp.where(is_pilot, 201.0, 200.0)
            for i in range(4):
                before = span - (k - offset + PSP * (i + 1))
                after = span - (first_after + PSP * i - k)
                total -= (jnp.maximum(before, 0) + jnp.maximum(after, 0)).astype(jnp.float32)
            table_ref[m, 2, at] = 1.0 / total
            table_ref[m, 3, at] = jnp.where(is_pilot, 1.0, 0.0)


def profile_kernel(
    syms, scale, pilot_ref, place_ref, s_ref, table_ref, own_ref, other_ref, spot_ref, high_ref, low_ref, twist_ref, *refs
):
    outs = refs[: max(syms, 1)]
    flat_ref, turned_ref, gain_ref, ratio_ref, num_ref, rows_ref, range_ref, prof_ref = refs[max(syms, 1) :]
    symbols, groups = s_ref.shape[:2]
    tones = ACTIVE_TONES // FOLD
    own_place, swapped = place_ref[0], place_ref[1] > 0
    for j in range(FOLD // 2):
        at = slice(j * LANES, (j + 1) * LANES)
        own, other = own_ref[:, at], other_ref[:, at]
        flat_ref[j, :symbols] = jnp.where(swapped, other, own).astype(jnp.float32)
        flat_ref[FOLD // 2 + j, :symbols] = jnp.where(swapped, own, other).astype(jnp.float32)

    for m in range(symbols):
        slot = m % 2
        offset = pilot_ref[m]
        stood = flat_ref[:, m, :].T.astype(jnp.bfloat16)
        spread = dot(stood, spot_ref[...])
        turned_ref[slot] = sum(
            spread[FOLD * l : FOLD * (l + 1), tones * l : tones * (l + 1)] for l in range(LANES // FOLD)
        )
        lane = lax.broadcasted_iota(jnp.int32, (ROWS, tones), 1)
        for p in range(4):
            at = slice(p * 8, p * 8 + 8)
            index = turned_ref[slot, pl.ds(p, 8, stride=4), :]
            high_bits = jnp.floor(index * 0.125)
            level_re = 2.0 * (index - 8.0 * high_bits) - 7.0
            level_im = 2.0 * high_bits - 7.0
            factor = scale / (level_re * level_re + level_im * level_im)
            c, s = table_ref[m, 0, at], table_ref[m, 1, at]
            gain_ref[slot, 0, at] = (c * level_re + s * level_im) * factor
            gain_ref[slot, 1, at] = (s * level_re - c * level_im) * factor

        for g in range(groups):
            base = (m * groups + g) * FOLD * ROWS
            for i in range(FOLD):
                re = s_ref[m, g, i * ROWS : (i + 1) * ROWS, :tones]
                im = s_ref[m, g, i * ROWS : (i + 1) * ROWS, tones:]
                c = gain_ref[slot, 0, i : i + 1, :]
                s = gain_ref[slot, 1, i : i + 1, :]
                ratio_ref[slot, 0, i] = re * c - im * s
                ratio_ref[slot, 1, i] = re * s + im * c

            r = offset & 3
            for part in range(2):
                picked = [
                    ratio_ref[slot, part, r * 8 + a] * table_ref[m, 3, pl.ds(r * 8 + a, 1), :] for a in range(8)
                ]

                def pilot(i):
                    b, a = i // 8, i % 8
                    if b == 0:
                        return picked[a]
                    rolled = pltpu.roll(picked[a], (-b) % tones, 1)
                    return jnp.where((lane < tones - b) if b > 0 else (lane >= -b), rolled, 0.0)

                q = {i: pilot(i) for i in range(-13, 21)}
                slope = sum(q[i] for i in range(0, 12)) - sum(q[i] for i in range(-12, 0))
                value = sum((49 - 4 * abs(i + 1)) * q[i] for i in range(-13, 12))
                for a in range(-1, 8):
                    for s in range(4):
                        to = r + s
                        here = value if s == 0 else value + s * slope - q[a - 12]
                        num_ref[slot, part, (to & 3) * 10 + a + 1 + (to >> 2)] = here
                    value = value + 4.0 * slope - q[a - 12] + q[a + 13]
                    if a < 7:
                        slope = slope + q[a + 13] - 2.0 * q[a + 1] + q[a - 11]

            for i in range(0, FOLD, 2):
                for part in range(2):
                    pair = []
                    for n in (i, i + 1):
                        smooth = num_ref[slot, part, (n // 8) * 10 + n % 8 + 1] * table_ref[m, 2, n : n + 1, :]
                        pair.append(ratio_ref[slot, part, n] - smooth)
                    high, low = split_rows(jnp.concatenate(pair, axis=0))
                    at = slice(base + i * ROWS, base + (i + 2) * ROWS)
                    rows_ref[at, part * tones : (part + 1) * tones] = high
                    rows_ref[at, (2 + part) * tones : (3 + part) * tones] = low

    range_ref[...] = split_product(rows_ref, high_ref, low_ref)
    lane = lax.broadcasted_iota(jnp.int32, (ROWS, LANES), 1)
    codes = jnp.zeros((ROWS, LANES), jnp.float32)
    for m in range(symbols):
        for g in range(groups):
            base, slot = (m * groups + g) * FOLD * ROWS, m % 2
            sums = None
            for p in range(4):
                x = []
                for i in range(p * 8, p * 8 + 8):
                    at = slice(base + i * ROWS, base + (i + 1) * ROWS)
                    re, im = range_ref[at, :LANES], range_ref[at, LANES:]
                    c, s = twist_ref[0, i : i + 1, :], twist_ref[1, i : i + 1, :]
                    x.append((re * c - im * s, re * s + im * c))
                y = [times(v, p * h / FOLD) for h, v in enumerate(dft8(x, 1))]
                sums = y if sums is None else [plus(a, b) for a, b in zip(sums, y)]
            if not syms:
                for h in range(RANGE_ROWS):
                    outs[0][m, g, 0, h], outs[0][m, g, 1, h] = sums[h]
                continue
            code = code_scale(peak_of([v for pair in sums for v in pair]))
            codes = jnp.where(lane == m, code, codes)
            for h in range(RANGE_ROWS):
                prof_ref[slot, h, 0], prof_ref[slot, h, 1] = sums[h]
            for h in range(RANGE_ROWS // syms):
                for d in range(syms):
                    row = syms * h + (own_place ^ d)
                    if d == 0:
                        outs[0][m, h] = prof_ref[slot, row]
                        continue
                    packed = [encode(prof_ref[slot, row, part], code) for part in range(2)]
                    outs[d][m * (RANGE_ROWS // syms) + h] = jnp.concatenate(packed, axis=0).astype(jnp.int16)
    if syms:
        packed = jnp.concatenate([codes, codes], axis=0).astype(jnp.int32).astype(jnp.int16)
        for d in range(1, syms):
            outs[d][symbols * (RANGE_ROWS // syms)] = packed


SEND_ORDER = (3, 1, 2)


def doppler_kernel(place_ref, own_ref, *refs):
    pieces, (out_ref, turned_ref, spread_ref) = refs[:3], refs[3:]
    symbols, rows = own_ref.shape[:2]
    syms = 4
    own = place_ref[0]
    turned_ref[own] = own_ref[...]
    for d, piece in zip(SEND_ORDER, pieces):
        codes = piece[symbols * rows].astype(jnp.int32).astype(jnp.float32)
        for m in range(symbols):
            code = codes[:, m : m + 1]
            for h in range(rows):
                value = decode(piece[m * rows + h], code)
                turned_ref[own ^ d, m, h, 0], turned_ref[own ^ d, m, h, 1] = value[:ROWS], value[ROWS:]
    for h in range(rows):
        grid, bins = {}, {}
        for m in range(symbols):
            x = [(turned_ref[s, m, h, 0], turned_ref[s, m, h, 1]) for s in range(syms)]
            for p, y in enumerate(dft4(x, -1)):
                grid[p, m] = times(y, -m * p / (syms * symbols))
        for p in range(syms):
            for q, y in enumerate(dft6([grid[p, m] for m in range(symbols)], -1)):
                f = p + syms * q
                spread_ref[h, f, 0], spread_ref[h, f, 1] = y
    for s in range(syms):
        for h in range(rows):
            values = [spread_ref[h, s * symbols + f] for f in range(symbols)]
            code = code_scale(peak_of([v[part] for v in values for part in range(2)]))
            to = s * rows + h
            for f in range(symbols):
                packed = [encode(values[f][part], code) for part in range(2)]
                out_ref[to, f] = jnp.concatenate(packed, axis=0).astype(jnp.int16)
            codes = jnp.broadcast_to(code, (ROWS, LANES)).astype(jnp.int32)
            out_ref[to, symbols] = jnp.concatenate([codes, codes], axis=0).astype(jnp.int16)


def join_kernel(piece_ref, out_ref):
    _, symbols, channels, width = out_ref.shape
    subs = channels // ROWS
    for n in range(piece_ref.shape[0]):
        s, u = n // subs, n % subs
        code = piece_ref[n, symbols].astype(jnp.int32).astype(jnp.float32)
        gain = jnp.exp2(code * (1.0 / 64.0)) * (1.0 / 32767.0**2)
        for f in range(symbols):
            value = piece_ref[n, f].astype(jnp.int32).astype(jnp.float32)
            value = value * jnp.abs(value) * gain
            for part in range(2):
                at = slice(part * ROWS, (part + 1) * ROWS)
                out_ref[part, f, u * ROWS : (u + 1) * ROWS, s * LANES : (s + 1) * LANES] = value[at]


IN_VMEM = pl.BlockSpec(memory_space=pltpu.VMEM)
IN_SMEM = pl.BlockSpec(memory_space=pltpu.SMEM)
IN_HBM = pl.BlockSpec(memory_space=pltpu.HBM)


def spectra(windows, cp_offset, pilot_offsets):
    _, symbols, channels, record = windows.shape
    groups = channels // ROWS
    tones = ACTIVE_TONES // FOLD
    return pl.pallas_call(
        spectrum_kernel,
        in_specs=[IN_HBM] * 3,
        out_specs=[IN_VMEM] * 2,
        scratch_shapes=[
            pltpu.SMEM((symbols,), jnp.int32),
            pltpu.SMEM((symbols,), jnp.int32),
            pltpu.VMEM((symbols * groups, 2, ROWS, record), jnp.float32),
            pltpu.VMEM((2 * WIDE, 2 * tones), jnp.bfloat16),
            pltpu.VMEM((2 * WIDE, 2 * tones), jnp.bfloat16),
            pltpu.VMEM((2, FOLD, WIDE), jnp.float32),
            pltpu.VMEM((2, WIDE // LANES, 4, 8, 2, ROWS, LANES), jnp.float32),
            pltpu.VMEM((symbols * groups * FOLD * ROWS, 4 * WIDE), jnp.bfloat16),
            pltpu.SemaphoreType.DMA((symbols * groups + 2,)),
        ],
        out_shape=[
            jax.ShapeDtypeStruct((symbols, groups, FOLD * ROWS, 2 * tones), jnp.float32),
            jax.ShapeDtypeStruct((symbols, 4, FOLD, tones), jnp.float32),
        ],
        compiler_params=pltpu.CompilerParams(vmem_limit_bytes=SPECTRA_VMEM_LIMIT),
        cost_estimate=pl.CostEstimate(flops=2 * 10**9, bytes_accessed=8 * 10**6, transcendentals=0),
        name="spectra",
    )(*(pltpu.with_memory_space_constraint(a, pltpu.HBM) for a in (cp_offset, pilot_offsets, windows)))


def profiles(spectrum, tables, own, other, pilot_offsets, places, syms, scale):
    symbols, groups = spectrum.shape[:2]
    high, low, twist = range_tables()
    tones = ACTIVE_TONES // FOLD
    n, column = np.arange(FOLD)[:, None], np.arange(LANES // FOLD * tones)[None, :]
    spot = (column % tones == LANES // FOLD * n + column // tones).astype(ml_dtypes.bfloat16)
    if syms:
        rows = RANGE_ROWS // syms
        piece = jax.ShapeDtypeStruct((symbols * rows + 1, 2 * ROWS, LANES), jnp.int16)
        outs = [jax.ShapeDtypeStruct((symbols, rows, 2, ROWS, LANES), jnp.float32)] + [piece] * (syms - 1)
    else:
        outs = [jax.ShapeDtypeStruct((symbols, groups, 2, RANGE_ROWS, ROWS, LANES), jnp.float32)]
    return pl.pallas_call(
        functools.partial(profile_kernel, syms, scale),
        in_specs=[IN_SMEM] * 2 + [IN_VMEM] * 8,
        out_specs=[IN_VMEM] * len(outs),
        scratch_shapes=[
            pltpu.VMEM((FOLD, ROWS, LANES), jnp.float32),
            pltpu.VMEM((2, FOLD, tones), jnp.float32),
            pltpu.VMEM((2, 2, FOLD, tones), jnp.float32),
            pltpu.VMEM((2, 2, FOLD, ROWS, tones), jnp.float32),
            pltpu.VMEM((2, 2, 40, ROWS, tones), jnp.float32),
            pltpu.VMEM((symbols * groups * FOLD * ROWS, 4 * tones), jnp.bfloat16),
            pltpu.VMEM((symbols * groups * FOLD * ROWS, 2 * LANES), jnp.float32),
            pltpu.VMEM((2, RANGE_ROWS, 2, ROWS, LANES), jnp.float32),
        ],
        out_shape=outs,
        compiler_params=pltpu.CompilerParams(vmem_limit_bytes=VMEM_LIMIT),
        cost_estimate=pl.CostEstimate(flops=10**9, bytes_accessed=4 * 10**6, transcendentals=0),
        name="profiles",
    )(pilot_offsets, places, spectrum, tables, own, other, spot, high, low, twist)


def doppler_plain(own_profiles, symbols):
    turned = lax.all_to_all(own_profiles, "sub", split_axis=3, concat_axis=1, tiled=True)
    turned = lax.all_to_all(turned, "sym", split_axis=3, concat_axis=2, tiled=True)
    ids = np.arange(symbols)
    angle = TWO_PI / symbols * (ids[:, None] * ids[None, :] % symbols)
    c, s = np.cos(angle).astype(np.float32), np.sin(angle).astype(np.float32)
    product = lambda t, x: jnp.einsum("fm,cmq->cfq", t, x, precision=HIGHEST)
    re = product(c, turned[0]) + product(s, turned[1])
    im = product(c, turned[1]) - product(s, turned[0])
    return lax.all_to_all(jnp.stack([re, im]), "sym", split_axis=2, concat_axis=3, tiled=True)


def doppler_paired(pieces, places, syms, subs):
    got = [pieces[0]] + [
        lax.ppermute(pieces[d], "sym", [(i, i ^ d) for i in range(syms)]) for d in SEND_ORDER
    ]
    symbols, rows = got[0].shape[:2]
    coded = pl.pallas_call(
        doppler_kernel,
        in_specs=[IN_SMEM] + [IN_VMEM] * syms,
        out_specs=IN_VMEM,
        out_shape=jax.ShapeDtypeStruct((syms * subs, symbols + 1, 2 * ROWS, LANES), jnp.int16),
        scratch_shapes=[
            pltpu.VMEM((syms, symbols, rows, 2, ROWS, LANES), jnp.float32),
            pltpu.VMEM((rows, syms * symbols, 2, ROWS, LANES), jnp.float32),
        ],
        compiler_params=pltpu.CompilerParams(vmem_limit_bytes=VMEM_LIMIT),
        name="doppler",
    )(places, *got)
    coded = lax.all_to_all(coded, ("sym", "sub"), split_axis=0, concat_axis=0)
    out = pl.pallas_call(
        join_kernel,
        in_specs=[IN_VMEM],
        out_specs=IN_VMEM,
        out_shape=jax.ShapeDtypeStruct((2, symbols, subs * ROWS, syms * LANES), jnp.float32),
        compiler_params=pltpu.CompilerParams(vmem_limit_bytes=VMEM_LIMIT),
        name="join",
    )(coded)
    return jnp.transpose(out, (0, 2, 1, 3))


def local(samples, constellation_index, pilot_offsets, cp_offset):
    syms, subs = lax.axis_size("sym"), lax.axis_size("sub")
    place, sub = lax.axis_index("sym"), lax.axis_index("sub")
    channels, symbols = samples.shape[1:3]
    paired = syms == 4 and syms * subs == RANGE_ROWS and channels == ROWS and symbols == 6
    half = ACTIVE_TONES // 2
    if paired:
        own = constellation_index
        other = lax.ppermute(own, "sub", [(0, 1), (1, 0)])
        swapped = sub
    else:
        index = lax.all_gather(constellation_index, "sub", axis=1, tiled=True)
        own, other, swapped = index[:, :half], index[:, half:], jnp.zeros_like(sub)
    windows = jnp.transpose(samples, (0, 2, 1, 3))
    short = -channels % ROWS
    if short:
        windows = jnp.pad(windows, ((0, 0), (0, 0), (0, short), (0, 0)))
    spectrum, tables = spectra(windows, cp_offset, pilot_offsets)
    scale = ROOT_FORTYTWO / math.sqrt(WHOLE * ACTIVE_TONES * symbols * syms)
    places = jnp.stack([place, swapped])
    got = profiles(
        spectrum, tables, own, other, pilot_offsets, places, syms if paired else 0, scale
    )
    if paired:
        return doppler_paired(got, places, syms, subs)
    own = jnp.transpose(got[0], (2, 1, 4, 0, 3, 5))
    own = own.reshape(2, channels + short, symbols, GUARD_SAMPLES)[:, :channels]
    return doppler_plain(own, symbols * syms)


def solution(mesh):
    return jax.shard_map(
        local,
        mesh=mesh,
        in_specs=(
            P(None, ("chan", "sub"), "sym", None),
            P(("chan", "sym"), "sub"),
            P("sym"),
            P(("chan", "sym")),
        ),
        out_specs=P(None, "chan", "sym", "sub"),
        check_vma=False,
    )
```

```python
import functools
import math

import jax
import jax.numpy as jnp
import ml_dtypes
import numpy as np
from jax import lax
from jax.experimental import pallas as pl
from jax.experimental.pallas import tpu as pltpu
from jax.sharding import PartitionSpec as P

OUTER_FACTOR = 64
INNER_FACTOR = 128
ACTIVE_TONES = 4096
GUARD_SAMPLES = 1024
SMOOTH_HALFSPAN = 48
PSP = 12

TWO_PI = 2.0 * math.pi
ROOT_FORTYTWO = math.sqrt(42.0)
HIGHEST = lax.Precision.HIGHEST

WHOLE = OUTER_FACTOR * INNER_FACTOR
FOLD = 32
WIDE = WHOLE // FOLD
LANES = 128
ROWS = 8
LOWEST = (WHOLE - ACTIVE_TONES) // 2
RANGE_ROWS = GUARD_SAMPLES // LANES
VMEM_LIMIT = 48 * 1024 * 1024
SPECTRA_VMEM_LIMIT = 52 * 1024 * 1024


def split_table(table):
    high = table.astype(np.float32).astype(ml_dtypes.bfloat16)
    low = (table - high.astype(np.float64)).astype(np.float32).astype(ml_dtypes.bfloat16)
    return high, low


def turning(sign, product, period):
    angle = sign * TWO_PI / period * (product % period)
    cosine, sine = np.cos(angle), np.sin(angle)
    return np.block([[cosine, sine], [-sine, cosine]])


def residue_order():
    row = np.arange(FOLD)
    return row // 8 + 4 * (row % 8)


def range_tables():
    j = np.arange(ACTIVE_TONES // FOLD)
    l = np.arange(LANES)
    high, low = split_table(turning(1, j[:, None] * l[None, :], ACTIVE_TONES // FOLD))
    angle = TWO_PI / ACTIVE_TONES * (residue_order()[:, None] * l[None, :])
    return high, low, np.stack([np.cos(angle), np.sin(angle)]).astype(np.float32)


def times(x, turn):
    re, im = x
    turn = turn % 1.0
    eighth = round(turn * 8)
    if abs(turn * 8 - eighth) < 1e-9:
        eighth %= 8
        if eighth % 2 == 0:
            return [(re, im), (-im, re), (-re, -im), (im, -re)][eighth // 2]
        half = math.sqrt(0.5)
        add, sub = (re + im) * half, (re - im) * half
        return [(sub, add), (-add, sub), (-sub, -add), (add, -sub)][eighth // 2]
    c, s = math.cos(TWO_PI * turn), math.sin(TWO_PI * turn)
    return re * c - im * s, re * s + im * c


def plus(x, y):
    return x[0] + y[0], x[1] + y[1]


def minus(x, y):
    return x[0] - y[0], x[1] - y[1]


def turn_quarter(x, sign):
    return (-x[1], x[0]) if sign > 0 else (x[1], -x[0])


def dft4(x, sign):
    a, b = plus(x[0], x[2]), minus(x[0], x[2])
    c, d = plus(x[1], x[3]), turn_quarter(minus(x[1], x[3]), sign)
    return [plus(a, c), plus(b, d), minus(a, c), minus(b, d)]


def dft8(x, sign):
    even, odd = dft4(x[0::2], sign), dft4(x[1::2], sign)
    odd = [times(o, sign * k / 8) for k, o in enumerate(odd)]
    return [plus(e, o) for e, o in zip(even, odd)] + [minus(e, o) for e, o in zip(even, odd)]


def dft3(x, sign):
    total, diff = plus(x[1], x[2]), minus(x[1], x[2])
    mid = (x[0][0] - 0.5 * total[0], x[0][1] - 0.5 * total[1])
    root = sign * math.sqrt(0.75)
    side = (-root * diff[1], root * diff[0])
    return [plus(x[0], total), plus(mid, side), minus(mid, side)]


def dft6(x, sign):
    even, odd = dft3(x[0::2], sign), dft3(x[1::2], sign)
    odd = [times(o, sign * k / 6) for k, o in enumerate(odd)]
    return [plus(e, o) for e, o in zip(even, odd)] + [minus(e, o) for e, o in zip(even, odd)]


def split_rows(x):
    high = x.astype(jnp.bfloat16)
    return high, (x - high.astype(jnp.float32)).astype(jnp.bfloat16)


def dot(x, w):
    return lax.dot_general(x, w, (((1,), (0,)), ((), ())), preferred_element_type=jnp.float32)


def split_product(rows_ref, high_ref, low_ref):
    width = high_ref.shape[0]
    high, low = rows_ref[:, :width], rows_ref[:, width:]
    return dot(high, high_ref[...]) + dot(low, high_ref[...]) + dot(high, low_ref[...])


def code_scale(peak):
    return jnp.ceil(jnp.log2(jnp.maximum(peak, 1e-30)) * 64.0)


def encode(x, code):
    size = jnp.sqrt(jnp.abs(x)) * (32767.0 * jnp.exp2(code * (-1.0 / 128.0))) + 0.5
    return jnp.where(x < 0.0, -size, size).astype(jnp.int32)


def decode(n, code):
    n = n.astype(jnp.int32).astype(jnp.float32)
    return n * jnp.abs(n) * (jnp.exp2(code * (1.0 / 64.0)) * (1.0 / 32767.0**2))


def peak_of(values):
    top = functools.reduce(jnp.maximum, [jnp.abs(v) for v in values])
    return jnp.max(top, axis=1, keepdims=True)


def phase(product, period):
    n = product & (period - 1)
    quarter = (n + period // 8) // (period // 4)
    x = (n - quarter * (period // 4)).astype(jnp.float32) * (TWO_PI / period)
    y = x * x
    sine = x * (1 + y * (-1 / 6 + y * (1 / 120 + y * (-1 / 5040 + y * (1 / 362880)))))
    cosine = 1 + y * (-1 / 2 + y * (1 / 24 + y * (-1 / 720 + y * (1 / 40320 - y * (1 / 3628800)))))
    odd, low, turned = (quarter & 1) == 1, (quarter & 2) == 2, ((quarter + 1) & 2) == 2
    c, s = jnp.where(odd, sine, cosine), jnp.where(odd, cosine, sine)
    return jnp.where(turned, -c, c), jnp.where(low, -s, s)


def spectrum_kernel(off_hbm, pilot_hbm, x_hbm, out_ref, table_ref, off_ref, pilot_ref, x_ref, high_ref, low_ref, twist_ref, mid_ref, rows_ref, sems):
    symbols, groups = out_ref.shape[:2]
    tones = ACTIVE_TONES // FOLD
    tasks = [(m, g) for m in range(symbols) for g in range(groups)]
    fetches = []
    for n, (m, g) in enumerate(tasks):
        source = x_hbm.at[:, m, g * ROWS : (g + 1) * ROWS, :]
        fetches.append(pltpu.make_async_copy(source, x_ref.at[n], sems.at[n]))
        fetches[-1].start()
        if n == 0:
            scalars = [
                pltpu.make_async_copy(off_hbm, off_ref, sems.at[len(tasks)]),
                pltpu.make_async_copy(pilot_hbm, pilot_ref, sems.at[len(tasks) + 1]),
            ]
            for scalar in scalars:
                scalar.start()
    row = lax.broadcasted_iota(jnp.int32, (ROWS, WIDE), 0)
    lane = lax.broadcasted_iota(jnp.int32, (ROWS, WIDE), 1)
    for p in range(4):
        c, s = phase((p + 4 * row) * lane, WHOLE)
        twist_ref[0, p * 8 : p * 8 + 8], twist_ref[1, p * 8 : p * 8 + 8] = c, -s
    row = lax.broadcasted_iota(jnp.int32, (2 * ROWS, tones), 0)
    lane = lax.broadcasted_iota(jnp.int32, (2 * ROWS, tones), 1)
    for b in range(0, WIDE, 2 * ROWS):
        c, s = phase((b + row) * (LOWEST // FOLD + lane), WIDE)
        upper, lower = slice(b, b + 2 * ROWS), slice(WIDE + b, WIDE + b + 2 * ROWS)
        (c, c_low), (s, s_low) = split_rows(c), split_rows(s)
        high_ref[upper, :tones], high_ref[upper, tones:] = c, -s
        high_ref[lower, :tones], high_ref[lower, tones:] = s, c
        low_ref[upper, :tones], low_ref[upper, tones:] = c_low, -s_low
        low_ref[lower, :tones], low_ref[lower, tones:] = s_low, c_low
    lane = lax.broadcasted_iota(jnp.int32, (ROWS, LANES), 1)
    halves = WIDE // LANES
    for scalar in scalars:
        scalar.wait()
    symbol_tables(off_ref, pilot_ref, table_ref)
    for n, (m, g) in enumerate(tasks):
        fetches[n].wait()
        off, slot = off_ref[m], n % 2
        base = n * FOLD * ROWS

        def sample(part, chunk):
            value = x_ref[n, part, :, chunk * LANES : (chunk + 1) * LANES]
            if chunk * LANES < GUARD_SAMPLES:
                wrapped = x_ref[n, part, :, WHOLE + chunk * LANES : WHOLE + (chunk + 1) * LANES]
                value = jnp.where(lane < off - chunk * LANES, wrapped, value)
            return value

        for h in range(halves):
            for v in range(8):
                chunks = [halves * (8 * u + v) + h for u in range(4)]
                y = dft4([(sample(0, c), sample(1, c)) for c in chunks], -1)
                for p in range(4):
                    at = (slot, h, p, v)
                    mid_ref[at + (0,)], mid_ref[at + (1,)] = times(y[p], -v * p / FOLD)
        for p in range(4):
            for h in range(halves):
                at = (slot, h, p)
                y = dft8([(mid_ref[at + (v, 0)], mid_ref[at + (v, 1)]) for v in range(8)], -1)
                for q in range(0, 8, 2):
                    pair = []
                    for row in (p * 8 + q, p * 8 + q + 1):
                        re, im = y[row - p * 8]
                        c = twist_ref[0, row : row + 1, h * LANES : (h + 1) * LANES]
                        s = twist_ref[1, row : row + 1, h * LANES : (h + 1) * LANES]
                        pair.append((re * c - im * s, re * s + im * c))
                    at_rows = slice(base + (p * 8 + q) * ROWS, base + (p * 8 + q + 2) * ROWS)
                    for part in range(2):
                        high, low = split_rows(jnp.concatenate([pair[0][part], pair[1][part]], axis=0))
                        column = part * WIDE + h * LANES
                        rows_ref[at_rows, column : column + LANES] = high
                        rows_ref[at_rows, 2 * WIDE + column : 2 * WIDE + column + LANES] = low
    out_ref[...] = split_product(rows_ref, high_ref, low_ref).reshape(out_ref.shape)


def symbol_tables(off_ref, pilot_ref, table_ref):
    symbols = table_ref.shape[0]
    tones = ACTIVE_TONES // FOLD
    row = lax.broadcasted_iota(jnp.int32, (ROWS, tones), 0)
    lane = lax.broadcasted_iota(jnp.int32, (ROWS, tones), 1)
    by_row = by_lane = jnp.zeros((ROWS, tones), jnp.int32)
    for m in range(symbols):
        by_row = jnp.where(row == m, off_ref[m], by_row)
        by_lane = jnp.where(lane == m, off_ref[m], by_lane)
    lane_re, lane_im = phase(by_row * (LOWEST + FOLD * lane), WHOLE)
    row_phases = [phase(by_lane * (p + 4 * row), WHOLE) for p in range(4)]
    span = SMOOTH_HALFSPAN + 1
    for m in range(symbols):
        offset = pilot_ref[m]
        first_after = ACTIVE_TONES + lax.rem(offset + PSP * ACTIVE_TONES - ACTIVE_TONES, PSP)
        a, b = lane_re[m : m + 1, :], lane_im[m : m + 1, :]
        for p in range(4):
            at = slice(p * 8, p * 8 + 8)
            c, s = row_phases[p][0][:, m : m + 1], row_phases[p][1][:, m : m + 1]
            table_ref[m, 0, at], table_ref[m, 1, at] = a * c - b * s, a * s + b * c
            k = p + 4 * row + FOLD * lane
            is_pilot = lax.rem(k + (PSP - offset), PSP) == 0
            total = jnp.where(is_pilot, 201.0, 200.0)
            for i in range(4):
                before = span - (k - offset + PSP * (i + 1))
                after = span - (first_after + PSP * i - k)
                total -= (jnp.maximum(before, 0) + jnp.maximum(after, 0)).astype(jnp.float32)
            table_ref[m, 2, at] = 1.0 / total
            table_ref[m, 3, at] = jnp.where(is_pilot, 1.0, 0.0)


def profile_kernel(
    syms, scale, pilot_ref, place_ref, s_ref, table_ref, own_ref, other_ref, spot_ref, high_ref, low_ref, twist_ref, *refs
):
    outs = refs[: max(syms, 1)]
    flat_ref, turned_ref, gain_ref, ratio_ref, num_ref, rows_ref, range_ref, prof_ref = refs[max(syms, 1) :]
    symbols, groups = s_ref.shape[:2]
    tones = ACTIVE_TONES // FOLD
    own_place, swapped = place_ref[0], place_ref[1] > 0
    for j in range(FOLD // 2):
        at = slice(j * LANES, (j + 1) * LANES)
        own, other = own_ref[:, at], other_ref[:, at]
        flat_ref[j, :symbols] = jnp.where(swapped, other, own).astype(jnp.float32)
        flat_ref[FOLD // 2 + j, :symbols] = jnp.where(swapped, own, other).astype(jnp.float32)

    for m in range(symbols):
        slot = m % 2
        offset = pilot_ref[m]
        stood = flat_ref[:, m, :].T.astype(jnp.bfloat16)
        spread = dot(stood, spot_ref[...])
        turned_ref[slot] = sum(
            spread[FOLD * l : FOLD * (l + 1), tones * l : tones * (l + 1)] for l in range(LANES // FOLD)
        )
        lane = lax.broadcasted_iota(jnp.int32, (ROWS, tones), 1)
        for p in range(4):
            at = slice(p * 8, p * 8 + 8)
            index = turned_ref[slot, pl.ds(p, 8, stride=4), :]
            high_bits = jnp.floor(index * 0.125)
            level_re = 2.0 * (index - 8.0 * high_bits) - 7.0
            level_im = 2.0 * high_bits - 7.0
            factor = scale / (level_re * level_re + level_im * level_im)
            c, s = table_ref[m, 0, at], table_ref[m, 1, at]
            gain_ref[slot, 0, at] = (c * level_re + s * level_im) * factor
            gain_ref[slot, 1, at] = (s * level_re - c * level_im) * factor

        for g in range(groups):
            base = (m * groups + g) * FOLD * ROWS
            for i in range(FOLD):
                re = s_ref[m, g, i * ROWS : (i + 1) * ROWS, :tones]
                im = s_ref[m, g, i * ROWS : (i + 1) * ROWS, tones:]
                c = gain_ref[slot, 0, i : i + 1, :]
                s = gain_ref[slot, 1, i : i + 1, :]
                ratio_ref[slot, 0, i] = re * c - im * s
                ratio_ref[slot, 1, i] = re * s + im * c

            r = offset & 3
            for part in range(2):
                picked = [
                    ratio_ref[slot, part, r * 8 + a] * table_ref[m, 3, pl.ds(r * 8 + a, 1), :] for a in range(8)
                ]

                def pilot(i):
                    b, a = i // 8, i % 8
                    if b == 0:
                        return picked[a]
                    rolled = pltpu.roll(picked[a], (-b) % tones, 1)
                    return jnp.where((lane < tones - b) if b > 0 else (lane >= -b), rolled, 0.0)

                q = {i: pilot(i) for i in range(-13, 21)}
                slope = sum(q[i] for i in range(0, 12)) - sum(q[i] for i in range(-12, 0))
                value = sum((49 - 4 * abs(i + 1)) * q[i] for i in range(-13, 12))
                for a in range(-1, 8):
                    for s in range(4):
                        to = r + s
                        here = value if s == 0 else value + s * slope - q[a - 12]
                        num_ref[slot, part, (to & 3) * 10 + a + 1 + (to >> 2)] = here
                    value = value + 4.0 * slope - q[a - 12] + q[a + 13]
                    if a < 7:
                        slope = slope + q[a + 13] - 2.0 * q[a + 1] + q[a - 11]

            for i in range(0, FOLD, 2):
                for part in range(2):
                    pair = []
                    for n in (i, i + 1):
                        smooth = num_ref[slot, part, (n // 8) * 10 + n % 8 + 1] * table_ref[m, 2, n : n + 1, :]
                        pair.append(ratio_ref[slot, part, n] - smooth)
                    high, low = split_rows(jnp.concatenate(pair, axis=0))
                    at = slice(base + i * ROWS, base + (i + 2) * ROWS)
                    rows_ref[at, part * tones : (part + 1) * tones] = high
                    rows_ref[at, (2 + part) * tones : (3 + part) * tones] = low

    range_ref[...] = split_product(rows_ref, high_ref, low_ref)
    lane = lax.broadcasted_iota(jnp.int32, (ROWS, LANES), 1)
    codes = jnp.zeros((ROWS, LANES), jnp.float32)
    for m in range(symbols):
        for g in range(groups):
            base, slot = (m * groups + g) * FOLD * ROWS, m % 2
            sums = None
            for p in range(4):
                x = []
                for i in range(p * 8, p * 8 + 8):
                    at = slice(base + i * ROWS, base + (i + 1) * ROWS)
                    re, im = range_ref[at, :LANES], range_ref[at, LANES:]
                    c, s = twist_ref[0, i : i + 1, :], twist_ref[1, i : i + 1, :]
                    x.append((re * c - im * s, re * s + im * c))
                y = [times(v, p * h / FOLD) for h, v in enumerate(dft8(x, 1))]
                sums = y if sums is None else [plus(a, b) for a, b in zip(sums, y)]
            if not syms:
                for h in range(RANGE_ROWS):
                    outs[0][m, g, 0, h], outs[0][m, g, 1, h] = sums[h]
                continue
            code = code_scale(peak_of([v for pair in sums for v in pair]))
            codes = jnp.where(lane == m, code, codes)
            for h in range(RANGE_ROWS):
                prof_ref[slot, h, 0], prof_ref[slot, h, 1] = sums[h]
            for h in range(RANGE_ROWS // syms):
                for d in range(syms):
                    row = syms * h + (own_place ^ d)
                    if d == 0:
                        outs[0][m, h] = prof_ref[slot, row]
                        continue
                    to = 2 * (m * (RANGE_ROWS // syms) + h)
                    packed = [encode(prof_ref[slot, row, part], code) for part in range(2)]
                    outs[d][to : to + 2] = jnp.stack(packed).astype(jnp.int16)
    if syms:
        packed = codes.astype(jnp.int32).astype(jnp.int16)
        for d in range(1, syms):
            outs[d][2 * symbols * (RANGE_ROWS // syms)] = packed


SEND_ORDER = (3, 1, 2)


def doppler_kernel(place_ref, own_ref, *refs):
    pieces, (out_ref, turned_ref, spread_ref) = refs[:3], refs[3:]
    symbols, rows = own_ref.shape[:2]
    syms = 4
    own = place_ref[0]
    turned_ref[own] = own_ref[...]
    for d, piece in zip(SEND_ORDER, pieces):
        codes = piece[2 * symbols * rows].astype(jnp.int32).astype(jnp.float32)
        for m in range(symbols):
            code = codes[:, m : m + 1]
            for h in range(rows):
                to = 2 * (m * rows + h)
                turned_ref[own ^ d, m, h] = decode(piece[to : to + 2], code)
    for h in range(rows):
        grid, bins = {}, {}
        for m in range(symbols):
            x = [(turned_ref[s, m, h, 0], turned_ref[s, m, h, 1]) for s in range(syms)]
            for p, y in enumerate(dft4(x, -1)):
                grid[p, m] = times(y, -m * p / (syms * symbols))
        for p in range(syms):
            for q, y in enumerate(dft6([grid[p, m] for m in range(symbols)], -1)):
                f = p + syms * q
                spread_ref[h, f, 0], spread_ref[h, f, 1] = y
    for s in range(syms):
        for h in range(rows):
            values = [spread_ref[h, s * symbols + f] for f in range(symbols)]
            code = code_scale(peak_of([v[part] for v in values for part in range(2)]))
            to = s * rows + h
            for f in range(symbols):
                packed = [encode(values[f][part], code) for part in range(2)]
                out_ref[to, 2 * f : 2 * f + 2] = jnp.stack(packed).astype(jnp.int16)
            codes = jnp.broadcast_to(code, (ROWS, LANES)).astype(jnp.int32)
            out_ref[to, 2 * symbols] = codes.astype(jnp.int16)


def join_kernel(piece_ref, out_ref):
    _, symbols, channels, width = out_ref.shape
    subs = channels // ROWS
    for n in range(piece_ref.shape[0]):
        s, u = n // subs, n % subs
        code = piece_ref[n, 2 * symbols].astype(jnp.int32).astype(jnp.float32)
        gain = jnp.exp2(code * (1.0 / 64.0)) * (1.0 / 32767.0**2)
        for f in range(symbols):
            value = piece_ref[n, 2 * f : 2 * f + 2].astype(jnp.int32).astype(jnp.float32)
            value = value * jnp.abs(value) * gain
            for part in range(2):
                out_ref[part, f, u * ROWS : (u + 1) * ROWS, s * LANES : (s + 1) * LANES] = value[part]


IN_VMEM = pl.BlockSpec(memory_space=pltpu.VMEM)
IN_SMEM = pl.BlockSpec(memory_space=pltpu.SMEM)
IN_HBM = pl.BlockSpec(memory_space=pltpu.HBM)


def spectra(windows, cp_offset, pilot_offsets):
    _, symbols, channels, record = windows.shape
    groups = channels // ROWS
    tones = ACTIVE_TONES // FOLD
    return pl.pallas_call(
        spectrum_kernel,
        in_specs=[IN_HBM] * 3,
        out_specs=[IN_VMEM] * 2,
        scratch_shapes=[
            pltpu.SMEM((symbols,), jnp.int32),
            pltpu.SMEM((symbols,), jnp.int32),
            pltpu.VMEM((symbols * groups, 2, ROWS, record), jnp.float32),
            pltpu.VMEM((2 * WIDE, 2 * tones), jnp.bfloat16),
            pltpu.VMEM((2 * WIDE, 2 * tones), jnp.bfloat16),
            pltpu.VMEM((2, FOLD, WIDE), jnp.float32),
            pltpu.VMEM((2, WIDE // LANES, 4, 8, 2, ROWS, LANES), jnp.float32),
            pltpu.VMEM((symbols * groups * FOLD * ROWS, 4 * WIDE), jnp.bfloat16),
            pltpu.SemaphoreType.DMA((symbols * groups + 2,)),
        ],
        out_shape=[
            jax.ShapeDtypeStruct((symbols, groups, FOLD * ROWS, 2 * tones), jnp.float32),
            jax.ShapeDtypeStruct((symbols, 4, FOLD, tones), jnp.float32),
        ],
        compiler_params=pltpu.CompilerParams(vmem_limit_bytes=SPECTRA_VMEM_LIMIT),
        cost_estimate=pl.CostEstimate(flops=2 * 10**9, bytes_accessed=8 * 10**6, transcendentals=0),
        name="spectra",
    )(*(pltpu.with_memory_space_constraint(a, pltpu.HBM) for a in (cp_offset, pilot_offsets, windows)))


def profiles(spectrum, tables, own, other, pilot_offsets, places, syms, scale):
    symbols, groups = spectrum.shape[:2]
    high, low, twist = range_tables()
    tones = ACTIVE_TONES // FOLD
    n, column = np.arange(FOLD)[:, None], np.arange(LANES // FOLD * tones)[None, :]
    spot = (column % tones == LANES // FOLD * n + column // tones).astype(ml_dtypes.bfloat16)
    if syms:
        rows = RANGE_ROWS // syms
        piece = jax.ShapeDtypeStruct((2 * symbols * rows + 1, ROWS, LANES), jnp.int16)
        outs = [jax.ShapeDtypeStruct((symbols, rows, 2, ROWS, LANES), jnp.float32)] + [piece] * (syms - 1)
    else:
        outs = [jax.ShapeDtypeStruct((symbols, groups, 2, RANGE_ROWS, ROWS, LANES), jnp.float32)]
    return pl.pallas_call(
        functools.partial(profile_kernel, syms, scale),
        in_specs=[IN_SMEM] * 2 + [IN_VMEM] * 8,
        out_specs=[IN_VMEM] * len(outs),
        scratch_shapes=[
            pltpu.VMEM((FOLD, ROWS, LANES), jnp.float32),
            pltpu.VMEM((2, FOLD, tones), jnp.float32),
            pltpu.VMEM((2, 2, FOLD, tones), jnp.float32),
            pltpu.VMEM((2, 2, FOLD, ROWS, tones), jnp.float32),
            pltpu.VMEM((2, 2, 40, ROWS, tones), jnp.float32),
            pltpu.VMEM((symbols * groups * FOLD * ROWS, 4 * tones), jnp.bfloat16),
            pltpu.VMEM((symbols * groups * FOLD * ROWS, 2 * LANES), jnp.float32),
            pltpu.VMEM((2, RANGE_ROWS, 2, ROWS, LANES), jnp.float32),
        ],
        out_shape=outs,
        compiler_params=pltpu.CompilerParams(vmem_limit_bytes=VMEM_LIMIT),
        cost_estimate=pl.CostEstimate(flops=10**9, bytes_accessed=4 * 10**6, transcendentals=0),
        name="profiles",
    )(pilot_offsets, places, spectrum, tables, own, other, spot, high, low, twist)


def doppler_plain(own_profiles, symbols):
    turned = lax.all_to_all(own_profiles, "sub", split_axis=3, concat_axis=1, tiled=True)
    turned = lax.all_to_all(turned, "sym", split_axis=3, concat_axis=2, tiled=True)
    ids = np.arange(symbols)
    angle = TWO_PI / symbols * (ids[:, None] * ids[None, :] % symbols)
    c, s = np.cos(angle).astype(np.float32), np.sin(angle).astype(np.float32)
    product = lambda t, x: jnp.einsum("fm,cmq->cfq", t, x, precision=HIGHEST)
    re = product(c, turned[0]) + product(s, turned[1])
    im = product(c, turned[1]) - product(s, turned[0])
    return lax.all_to_all(jnp.stack([re, im]), "sym", split_axis=2, concat_axis=3, tiled=True)


def doppler_paired(pieces, places, syms, subs):
    got = [pieces[0]] + [
        lax.ppermute(pieces[d], "sym", [(i, i ^ d) for i in range(syms)]) for d in SEND_ORDER
    ]
    symbols, rows = got[0].shape[:2]
    coded = pl.pallas_call(
        doppler_kernel,
        in_specs=[IN_SMEM] + [IN_VMEM] * syms,
        out_specs=IN_VMEM,
        out_shape=jax.ShapeDtypeStruct((syms * subs, 2 * symbols + 1, ROWS, LANES), jnp.int16),
        scratch_shapes=[
            pltpu.VMEM((syms, symbols, rows, 2, ROWS, LANES), jnp.float32),
            pltpu.VMEM((rows, syms * symbols, 2, ROWS, LANES), jnp.float32),
        ],
        compiler_params=pltpu.CompilerParams(vmem_limit_bytes=VMEM_LIMIT),
        name="doppler",
    )(places, *got)
    coded = lax.all_to_all(coded, ("sym", "sub"), split_axis=0, concat_axis=0)
    out = pl.pallas_call(
        join_kernel,
        in_specs=[IN_VMEM],
        out_specs=IN_VMEM,
        out_shape=jax.ShapeDtypeStruct((2, symbols, subs * ROWS, syms * LANES), jnp.float32),
        compiler_params=pltpu.CompilerParams(vmem_limit_bytes=VMEM_LIMIT),
        name="join",
    )(coded)
    return jnp.transpose(out, (0, 2, 1, 3))


def local(samples, constellation_index, pilot_offsets, cp_offset):
    syms, subs = lax.axis_size("sym"), lax.axis_size("sub")
    place, sub = lax.axis_index("sym"), lax.axis_index("sub")
    channels, symbols = samples.shape[1:3]
    paired = syms == 4 and syms * subs == RANGE_ROWS and channels == ROWS and symbols == 6
    half = ACTIVE_TONES // 2
    if paired:
        own = constellation_index
        other = lax.ppermute(own, "sub", [(0, 1), (1, 0)])
        swapped = sub
    else:
        index = lax.all_gather(constellation_index, "sub", axis=1, tiled=True)
        own, other, swapped = index[:, :half], index[:, half:], jnp.zeros_like(sub)
    windows = jnp.transpose(samples, (0, 2, 1, 3))
    short = -channels % ROWS
    if short:
        windows = jnp.pad(windows, ((0, 0), (0, 0), (0, short), (0, 0)))
    spectrum, tables = spectra(windows, cp_offset, pilot_offsets)
    scale = ROOT_FORTYTWO / math.sqrt(WHOLE * ACTIVE_TONES * symbols * syms)
    places = jnp.stack([place, swapped])
    got = profiles(
        spectrum, tables, own, other, pilot_offsets, places, syms if paired else 0, scale
    )
    if paired:
        return doppler_paired(got, places, syms, subs)
    own = jnp.transpose(got[0], (2, 1, 4, 0, 3, 5))
    own = own.reshape(2, channels + short, symbols, GUARD_SAMPLES)[:, :channels]
    return doppler_plain(own, symbols * syms)


def solution(mesh):
    return jax.shard_map(
        local,
        mesh=mesh,
        in_specs=(
            P(None, ("chan", "sub"), "sym", None),
            P(("chan", "sym"), "sub"),
            P("sym"),
            P(("chan", "sym")),
        ),
        out_specs=P(None, "chan", "sym", "sub"),
        check_vma=False,
    )
```

```python
import functools
import math

import jax
import jax.numpy as jnp
import ml_dtypes
import numpy as np
from jax import lax
from jax.experimental import pallas as pl
from jax.experimental.pallas import tpu as pltpu
from jax.sharding import PartitionSpec as P

OUTER_FACTOR = 64
INNER_FACTOR = 128
ACTIVE_TONES = 4096
GUARD_SAMPLES = 1024
SMOOTH_HALFSPAN = 48
PSP = 12

TWO_PI = 2.0 * math.pi
ROOT_FORTYTWO = math.sqrt(42.0)
HIGHEST = lax.Precision.HIGHEST

WHOLE = OUTER_FACTOR * INNER_FACTOR
FOLD = 32
WIDE = WHOLE // FOLD
LANES = 128
ROWS = 8
LOWEST = (WHOLE - ACTIVE_TONES) // 2
RANGE_ROWS = GUARD_SAMPLES // LANES
VMEM_LIMIT = 48 * 1024 * 1024
SPECTRA_VMEM_LIMIT = 52 * 1024 * 1024


def split_table(table):
    high = table.astype(np.float32).astype(ml_dtypes.bfloat16)
    low = (table - high.astype(np.float64)).astype(np.float32).astype(ml_dtypes.bfloat16)
    return high, low


def turning(sign, product, period):
    angle = sign * TWO_PI / period * (product % period)
    cosine, sine = np.cos(angle), np.sin(angle)
    return np.block([[cosine, sine], [-sine, cosine]])


def residue_order():
    row = np.arange(FOLD)
    return row // 8 + 4 * (row % 8)


def range_tables():
    j = np.arange(ACTIVE_TONES // FOLD)
    l = np.arange(LANES)
    high, low = split_table(turning(1, j[:, None] * l[None, :], ACTIVE_TONES // FOLD))
    angle = TWO_PI / ACTIVE_TONES * (residue_order()[:, None] * l[None, :])
    return high, low, np.stack([np.cos(angle), np.sin(angle)]).astype(np.float32)


def times(x, turn):
    re, im = x
    turn = turn % 1.0
    eighth = round(turn * 8)
    if abs(turn * 8 - eighth) < 1e-9:
        eighth %= 8
        if eighth % 2 == 0:
            return [(re, im), (-im, re), (-re, -im), (im, -re)][eighth // 2]
        half = math.sqrt(0.5)
        add, sub = (re + im) * half, (re - im) * half
        return [(sub, add), (-add, sub), (-sub, -add), (add, -sub)][eighth // 2]
    c, s = math.cos(TWO_PI * turn), math.sin(TWO_PI * turn)
    return re * c - im * s, re * s + im * c


def plus(x, y):
    return x[0] + y[0], x[1] + y[1]


def minus(x, y):
    return x[0] - y[0], x[1] - y[1]


def turn_quarter(x, sign):
    return (-x[1], x[0]) if sign > 0 else (x[1], -x[0])


def dft4(x, sign):
    a, b = plus(x[0], x[2]), minus(x[0], x[2])
    c, d = plus(x[1], x[3]), turn_quarter(minus(x[1], x[3]), sign)
    return [plus(a, c), plus(b, d), minus(a, c), minus(b, d)]


def dft8(x, sign):
    even, odd = dft4(x[0::2], sign), dft4(x[1::2], sign)
    odd = [times(o, sign * k / 8) for k, o in enumerate(odd)]
    return [plus(e, o) for e, o in zip(even, odd)] + [minus(e, o) for e, o in zip(even, odd)]


def dft3(x, sign):
    total, diff = plus(x[1], x[2]), minus(x[1], x[2])
    mid = (x[0][0] - 0.5 * total[0], x[0][1] - 0.5 * total[1])
    root = sign * math.sqrt(0.75)
    side = (-root * diff[1], root * diff[0])
    return [plus(x[0], total), plus(mid, side), minus(mid, side)]


def dft6(x, sign):
    even, odd = dft3(x[0::2], sign), dft3(x[1::2], sign)
    odd = [times(o, sign * k / 6) for k, o in enumerate(odd)]
    return [plus(e, o) for e, o in zip(even, odd)] + [minus(e, o) for e, o in zip(even, odd)]


def split_rows(x):
    high = x.astype(jnp.bfloat16)
    return high, (x - high.astype(jnp.float32)).astype(jnp.bfloat16)


def dot(x, w):
    return lax.dot_general(x, w, (((1,), (0,)), ((), ())), preferred_element_type=jnp.float32)


def split_product(rows_ref, high_ref, low_ref):
    width = high_ref.shape[0]
    high, low = rows_ref[:, :width], rows_ref[:, width:]
    return dot(high, high_ref[...]) + dot(low, high_ref[...]) + dot(high, low_ref[...])


def code_scale(peak):
    return jnp.ceil(jnp.log2(jnp.maximum(peak, 1e-30)) * 64.0)


def encode(x, code):
    size = jnp.sqrt(jnp.abs(x)) * (32767.0 * jnp.exp2(code * (-1.0 / 128.0))) + 0.5
    return jnp.where(x < 0.0, -size, size).astype(jnp.int32)


def decode(n, code):
    n = n.astype(jnp.int32).astype(jnp.float32)
    return n * jnp.abs(n) * (jnp.exp2(code * (1.0 / 64.0)) * (1.0 / 32767.0**2))


def peak_of(values):
    top = functools.reduce(jnp.maximum, [jnp.abs(v) for v in values])
    return jnp.max(top, axis=1, keepdims=True)


def phase(product, period):
    n = product & (period - 1)
    quarter = (n + period // 8) // (period // 4)
    x = (n - quarter * (period // 4)).astype(jnp.float32) * (TWO_PI / period)
    y = x * x
    sine = x * (1 + y * (-1 / 6 + y * (1 / 120 + y * (-1 / 5040 + y * (1 / 362880)))))
    cosine = 1 + y * (-1 / 2 + y * (1 / 24 + y * (-1 / 720 + y * (1 / 40320 - y * (1 / 3628800)))))
    odd, low, turned = (quarter & 1) == 1, (quarter & 2) == 2, ((quarter + 1) & 2) == 2
    c, s = jnp.where(odd, sine, cosine), jnp.where(odd, cosine, sine)
    return jnp.where(turned, -c, c), jnp.where(low, -s, s)


def spectrum_kernel(off_hbm, pilot_hbm, x_hbm, out_ref, table_ref, off_ref, pilot_ref, x_ref, high_ref, low_ref, twist_ref, mid_ref, rows_ref, sems):
    symbols, groups = out_ref.shape[:2]
    tones = ACTIVE_TONES // FOLD
    tasks = [(m, g) for m in range(symbols) for g in range(groups)]
    fetches = []
    for n, (m, g) in enumerate(tasks):
        source = x_hbm.at[:, m, g * ROWS : (g + 1) * ROWS, :]
        fetches.append(pltpu.make_async_copy(source, x_ref.at[n], sems.at[n]))
        fetches[-1].start()
        if n == 0:
            scalars = [
                pltpu.make_async_copy(off_hbm, off_ref, sems.at[len(tasks)]),
                pltpu.make_async_copy(pilot_hbm, pilot_ref, sems.at[len(tasks) + 1]),
            ]
            for scalar in scalars:
                scalar.start()
    row = lax.broadcasted_iota(jnp.int32, (ROWS, WIDE), 0)
    lane = lax.broadcasted_iota(jnp.int32, (ROWS, WIDE), 1)
    for p in range(4):
        c, s = phase((p + 4 * row) * lane, WHOLE)
        twist_ref[0, p * 8 : p * 8 + 8], twist_ref[1, p * 8 : p * 8 + 8] = c, -s
    row = lax.broadcasted_iota(jnp.int32, (2 * ROWS, tones), 0)
    lane = lax.broadcasted_iota(jnp.int32, (2 * ROWS, tones), 1)
    for b in range(0, WIDE, 2 * ROWS):
        c, s = phase((b + row) * (LOWEST // FOLD + lane), WIDE)
        upper, lower = slice(b, b + 2 * ROWS), slice(WIDE + b, WIDE + b + 2 * ROWS)
        (c, c_low), (s, s_low) = split_rows(c), split_rows(s)
        high_ref[upper, :tones], high_ref[upper, tones:] = c, -s
        high_ref[lower, :tones], high_ref[lower, tones:] = s, c
        low_ref[upper, :tones], low_ref[upper, tones:] = c_low, -s_low
        low_ref[lower, :tones], low_ref[lower, tones:] = s_low, c_low
    lane = lax.broadcasted_iota(jnp.int32, (ROWS, LANES), 1)
    halves = WIDE // LANES
    for scalar in scalars:
        scalar.wait()
    symbol_tables(off_ref, pilot_ref, table_ref)
    for n, (m, g) in enumerate(tasks):
        fetches[n].wait()
        off, slot = off_ref[m], n % 2
        base = n * FOLD * ROWS

        def sample(part, chunk):
            value = x_ref[n, part, :, chunk * LANES : (chunk + 1) * LANES]
            if chunk * LANES < GUARD_SAMPLES:
                wrapped = x_ref[n, part, :, WHOLE + chunk * LANES : WHOLE + (chunk + 1) * LANES]
                value = jnp.where(lane < off - chunk * LANES, wrapped, value)
            return value

        for h in range(halves):
            for v in range(8):
                chunks = [halves * (8 * u + v) + h for u in range(4)]
                y = dft4([(sample(0, c), sample(1, c)) for c in chunks], -1)
                for p in range(4):
                    at = (slot, h, p, v)
                    mid_ref[at + (0,)], mid_ref[at + (1,)] = times(y[p], -v * p / FOLD)
        for p in range(4):
            for h in range(halves):
                at = (slot, h, p)
                y = dft8([(mid_ref[at + (v, 0)], mid_ref[at + (v, 1)]) for v in range(8)], -1)
                for q in range(0, 8, 2):
                    pair = []
                    for row in (p * 8 + q, p * 8 + q + 1):
                        re, im = y[row - p * 8]
                        c = twist_ref[0, row : row + 1, h * LANES : (h + 1) * LANES]
                        s = twist_ref[1, row : row + 1, h * LANES : (h + 1) * LANES]
                        pair.append((re * c - im * s, re * s + im * c))
                    at_rows = slice(base + (p * 8 + q) * ROWS, base + (p * 8 + q + 2) * ROWS)
                    for part in range(2):
                        high, low = split_rows(jnp.concatenate([pair[0][part], pair[1][part]], axis=0))
                        column = part * WIDE + h * LANES
                        rows_ref[at_rows, column : column + LANES] = high
                        rows_ref[at_rows, 2 * WIDE + column : 2 * WIDE + column + LANES] = low
    out_ref[...] = split_product(rows_ref, high_ref, low_ref).reshape(out_ref.shape)


def symbol_tables(off_ref, pilot_ref, table_ref):
    symbols = table_ref.shape[0]
    tones = ACTIVE_TONES // FOLD
    row = lax.broadcasted_iota(jnp.int32, (ROWS, tones), 0)
    lane = lax.broadcasted_iota(jnp.int32, (ROWS, tones), 1)
    by_row = by_lane = jnp.zeros((ROWS, tones), jnp.int32)
    for m in range(symbols):
        by_row = jnp.where(row == m, off_ref[m], by_row)
        by_lane = jnp.where(lane == m, off_ref[m], by_lane)
    lane_re, lane_im = phase(by_row * (LOWEST + FOLD * lane), WHOLE)
    row_phases = [phase(by_lane * (p + 4 * row), WHOLE) for p in range(4)]
    span = SMOOTH_HALFSPAN + 1
    for m in range(symbols):
        offset = pilot_ref[m]
        first_after = ACTIVE_TONES + lax.rem(offset + PSP * ACTIVE_TONES - ACTIVE_TONES, PSP)
        a, b = lane_re[m : m + 1, :], lane_im[m : m + 1, :]
        for p in range(4):
            at = slice(p * 8, p * 8 + 8)
            c, s = row_phases[p][0][:, m : m + 1], row_phases[p][1][:, m : m + 1]
            table_ref[m, 0, at], table_ref[m, 1, at] = a * c - b * s, a * s + b * c
            k = p + 4 * row + FOLD * lane
            is_pilot = lax.rem(k + (PSP - offset), PSP) == 0
            total = jnp.where(is_pilot, 201.0, 200.0)
            for i in range(4):
                before = span - (k - offset + PSP * (i + 1))
                after = span - (first_after + PSP * i - k)
                total -= (jnp.maximum(before, 0) + jnp.maximum(after, 0)).astype(jnp.float32)
            table_ref[m, 2, at] = 1.0 / total
            table_ref[m, 3, at] = jnp.where(is_pilot, 1.0, 0.0)


def profile_kernel(
    syms, scale, pilot_ref, s_ref, table_ref, own_ref, other_ref, spot_ref, high_ref, low_ref, twist_ref, *refs
):
    outs = refs[: max(syms, 1)]
    flat_ref, turned_ref, gain_ref, ratio_ref, num_ref, rows_ref, range_ref, prof_ref = refs[max(syms, 1) :]
    symbols, groups = s_ref.shape[:2]
    tones = ACTIVE_TONES // FOLD
    own_place = lax.axis_index("sym")
    swapped = lax.axis_index("sub") > 0 if syms else False
    for j in range(FOLD // 2):
        at = slice(j * LANES, (j + 1) * LANES)
        own, other = own_ref[:, at], other_ref[:, at]
        flat_ref[j, :symbols] = jnp.where(swapped, other, own).astype(jnp.float32)
        flat_ref[FOLD // 2 + j, :symbols] = jnp.where(swapped, own, other).astype(jnp.float32)

    for m in range(symbols):
        slot = m
        offset = pilot_ref[m]
        stood = flat_ref[:, m, :].T.astype(jnp.bfloat16)
        spread = dot(stood, spot_ref[...])
        turned_ref[slot] = sum(
            spread[FOLD * l : FOLD * (l + 1), tones * l : tones * (l + 1)] for l in range(LANES // FOLD)
        )
        lane = lax.broadcasted_iota(jnp.int32, (ROWS, tones), 1)
        for p in range(4):
            at = slice(p * 8, p * 8 + 8)
            index = turned_ref[slot, pl.ds(p, 8, stride=4), :]
            high_bits = jnp.floor(index * 0.125)
            level_re = 2.0 * (index - 8.0 * high_bits) - 7.0
            level_im = 2.0 * high_bits - 7.0
            factor = scale / (level_re * level_re + level_im * level_im)
            c, s = table_ref[m, 0, at], table_ref[m, 1, at]
            gain_ref[slot, 0, at] = (c * level_re + s * level_im) * factor
            gain_ref[slot, 1, at] = (s * level_re - c * level_im) * factor

        for g in range(groups):
            base = (m * groups + g) * FOLD * ROWS
            for i in range(FOLD):
                re = s_ref[m, g, i * ROWS : (i + 1) * ROWS, :tones]
                im = s_ref[m, g, i * ROWS : (i + 1) * ROWS, tones:]
                c = gain_ref[slot, 0, i : i + 1, :]
                s = gain_ref[slot, 1, i : i + 1, :]
                ratio_ref[slot, 0, i] = re * c - im * s
                ratio_ref[slot, 1, i] = re * s + im * c

            r = offset & 3
            for part in range(2):
                picked = [
                    ratio_ref[slot, part, r * 8 + a] * table_ref[m, 3, pl.ds(r * 8 + a, 1), :] for a in range(8)
                ]

                def pilot(i):
                    b, a = i // 8, i % 8
                    if b == 0:
                        return picked[a]
                    rolled = pltpu.roll(picked[a], (-b) % tones, 1)
                    return jnp.where((lane < tones - b) if b > 0 else (lane >= -b), rolled, 0.0)

                q = {i: pilot(i) for i in range(-13, 21)}
                slope = sum(q[i] for i in range(0, 12)) - sum(q[i] for i in range(-12, 0))
                value = sum((49 - 4 * abs(i + 1)) * q[i] for i in range(-13, 12))
                for a in range(-1, 8):
                    for s in range(4):
                        to = r + s
                        here = value if s == 0 else value + s * slope - q[a - 12]
                        num_ref[slot, part, (to & 3) * 10 + a + 1 + (to >> 2)] = here
                    value = value + 4.0 * slope - q[a - 12] + q[a + 13]
                    if a < 7:
                        slope = slope + q[a + 13] - 2.0 * q[a + 1] + q[a - 11]

            for i in range(0, FOLD, 2):
                for part in range(2):
                    pair = []
                    for n in (i, i + 1):
                        smooth = num_ref[slot, part, (n // 8) * 10 + n % 8 + 1] * table_ref[m, 2, n : n + 1, :]
                        pair.append(ratio_ref[slot, part, n] - smooth)
                    high, low = split_rows(jnp.concatenate(pair, axis=0))
                    at = slice(base + i * ROWS, base + (i + 2) * ROWS)
                    rows_ref[at, part * tones : (part + 1) * tones] = high
                    rows_ref[at, (2 + part) * tones : (3 + part) * tones] = low

    range_ref[...] = split_product(rows_ref, high_ref, low_ref)
    lane = lax.broadcasted_iota(jnp.int32, (ROWS, LANES), 1)
    codes = jnp.zeros((ROWS, LANES), jnp.float32)
    for m in range(symbols):
        for g in range(groups):
            base, slot = (m * groups + g) * FOLD * ROWS, m
            sums = None
            for p in range(4):
                x = []
                for i in range(p * 8, p * 8 + 8):
                    at = slice(base + i * ROWS, base + (i + 1) * ROWS)
                    re, im = range_ref[at, :LANES], range_ref[at, LANES:]
                    c, s = twist_ref[0, i : i + 1, :], twist_ref[1, i : i + 1, :]
                    x.append((re * c - im * s, re * s + im * c))
                y = [times(v, p * h / FOLD) for h, v in enumerate(dft8(x, 1))]
                sums = y if sums is None else [plus(a, b) for a, b in zip(sums, y)]
            if not syms:
                for h in range(RANGE_ROWS):
                    outs[0][m, g, 0, h], outs[0][m, g, 1, h] = sums[h]
                continue
            code = code_scale(peak_of([v for pair in sums for v in pair]))
            codes = jnp.where(lane == m, code, codes)
            for h in range(RANGE_ROWS):
                prof_ref[slot, h, 0], prof_ref[slot, h, 1] = sums[h]
            for h in range(RANGE_ROWS // syms):
                for d in range(syms):
                    row = syms * h + (own_place ^ d)
                    if d == 0:
                        outs[0][m, h] = prof_ref[slot, row]
                        continue
                    packed = [encode(prof_ref[slot, row, part], code) for part in range(2)]
                    outs[d][m * (RANGE_ROWS // syms) + h] = jnp.concatenate(packed, axis=0).astype(jnp.int16)
    if syms:
        packed = jnp.concatenate([codes, codes], axis=0).astype(jnp.int32).astype(jnp.int16)
        for d in range(1, syms):
            outs[d][symbols * (RANGE_ROWS // syms)] = packed


SEND_ORDER = (3, 1, 2)


def doppler_kernel(own_ref, *refs):
    pieces, (out_ref, turned_ref, spread_ref) = refs[:3], refs[3:]
    symbols, rows = own_ref.shape[:2]
    syms = 4
    own = lax.axis_index("sym")
    turned_ref[own] = own_ref[...]
    for d, piece in zip(SEND_ORDER, pieces):
        codes = piece[symbols * rows].astype(jnp.int32).astype(jnp.float32)
        for m in range(symbols):
            code = codes[:, m : m + 1]
            for h in range(rows):
                value = decode(piece[m * rows + h], code)
                turned_ref[own ^ d, m, h, 0], turned_ref[own ^ d, m, h, 1] = value[:ROWS], value[ROWS:]
    for h in range(rows):
        grid, bins = {}, {}
        for m in range(symbols):
            x = [(turned_ref[s, m, h, 0], turned_ref[s, m, h, 1]) for s in range(syms)]
            for p, y in enumerate(dft4(x, -1)):
                grid[p, m] = times(y, -m * p / (syms * symbols))
        for p in range(syms):
            for q, y in enumerate(dft6([grid[p, m] for m in range(symbols)], -1)):
                f = p + syms * q
                spread_ref[h, f, 0], spread_ref[h, f, 1] = y
    for s in range(syms):
        for h in range(rows):
            values = [spread_ref[h, s * symbols + f] for f in range(symbols)]
            code = code_scale(peak_of([v[part] for v in values for part in range(2)]))
            to = s * rows + h
            for f in range(symbols):
                packed = [encode(values[f][part], code) for part in range(2)]
                out_ref[to, f] = jnp.concatenate(packed, axis=0).astype(jnp.int16)
            codes = jnp.broadcast_to(code, (ROWS, LANES)).astype(jnp.int32)
            out_ref[to, symbols] = jnp.concatenate([codes, codes], axis=0).astype(jnp.int16)


def join_kernel(piece_ref, out_ref):
    _, symbols, channels, width = out_ref.shape
    subs = channels // ROWS
    for n in range(piece_ref.shape[0]):
        s, u = n // subs, n % subs
        code = piece_ref[n, symbols].astype(jnp.int32).astype(jnp.float32)
        gain = jnp.exp2(code * (1.0 / 64.0)) * (1.0 / 32767.0**2)
        for f in range(symbols):
            value = piece_ref[n, f].astype(jnp.int32).astype(jnp.float32)
            value = value * jnp.abs(value) * gain
            for part in range(2):
                at = slice(part * ROWS, (part + 1) * ROWS)
                out_ref[part, f, u * ROWS : (u + 1) * ROWS, s * LANES : (s + 1) * LANES] = value[at]


IN_VMEM = pl.BlockSpec(memory_space=pltpu.VMEM)
IN_SMEM = pl.BlockSpec(memory_space=pltpu.SMEM)
IN_HBM = pl.BlockSpec(memory_space=pltpu.HBM)


def spectra(windows, cp_offset, pilot_offsets):
    _, symbols, channels, record = windows.shape
    groups = channels // ROWS
    tones = ACTIVE_TONES // FOLD
    return pl.pallas_call(
        spectrum_kernel,
        in_specs=[IN_HBM] * 3,
        out_specs=[IN_VMEM] * 2,
        scratch_shapes=[
            pltpu.SMEM((symbols,), jnp.int32),
            pltpu.SMEM((symbols,), jnp.int32),
            pltpu.VMEM((symbols * groups, 2, ROWS, record), jnp.float32),
            pltpu.VMEM((2 * WIDE, 2 * tones), jnp.bfloat16),
            pltpu.VMEM((2 * WIDE, 2 * tones), jnp.bfloat16),
            pltpu.VMEM((2, FOLD, WIDE), jnp.float32),
            pltpu.VMEM((2, WIDE // LANES, 4, 8, 2, ROWS, LANES), jnp.float32),
            pltpu.VMEM((symbols * groups * FOLD * ROWS, 4 * WIDE), jnp.bfloat16),
            pltpu.SemaphoreType.DMA((symbols * groups + 2,)),
        ],
        out_shape=[
            jax.ShapeDtypeStruct((symbols, groups, FOLD * ROWS, 2 * tones), jnp.float32),
            jax.ShapeDtypeStruct((symbols, 4, FOLD, tones), jnp.float32),
        ],
        compiler_params=pltpu.CompilerParams(vmem_limit_bytes=SPECTRA_VMEM_LIMIT),
        cost_estimate=pl.CostEstimate(flops=2 * 10**9, bytes_accessed=8 * 10**6, transcendentals=0),
        name="spectra",
    )(*(pltpu.with_memory_space_constraint(a, pltpu.HBM) for a in (cp_offset, pilot_offsets, windows)))


def profiles(spectrum, tables, own, other, pilot_offsets, syms, scale):
    symbols, groups = spectrum.shape[:2]
    high, low, twist = range_tables()
    tones = ACTIVE_TONES // FOLD
    n, column = np.arange(FOLD)[:, None], np.arange(LANES // FOLD * tones)[None, :]
    spot = (column % tones == LANES // FOLD * n + column // tones).astype(ml_dtypes.bfloat16)
    if syms:
        rows = RANGE_ROWS // syms
        piece = jax.ShapeDtypeStruct((symbols * rows + 1, 2 * ROWS, LANES), jnp.int16)
        outs = [jax.ShapeDtypeStruct((symbols, rows, 2, ROWS, LANES), jnp.float32)] + [piece] * (syms - 1)
    else:
        outs = [jax.ShapeDtypeStruct((symbols, groups, 2, RANGE_ROWS, ROWS, LANES), jnp.float32)]
    return pl.pallas_call(
        functools.partial(profile_kernel, syms, scale),
        in_specs=[IN_SMEM] + [IN_VMEM] * 8,
        out_specs=[IN_VMEM] * len(outs),
        scratch_shapes=[
            pltpu.VMEM((FOLD, ROWS, LANES), jnp.float32),
            pltpu.VMEM((symbols, FOLD, tones), jnp.float32),
            pltpu.VMEM((symbols, 2, FOLD, tones), jnp.float32),
            pltpu.VMEM((symbols, 2, FOLD, ROWS, tones), jnp.float32),
            pltpu.VMEM((symbols, 2, 40, ROWS, tones), jnp.float32),
            pltpu.VMEM((symbols * groups * FOLD * ROWS, 4 * tones), jnp.bfloat16),
            pltpu.VMEM((symbols * groups * FOLD * ROWS, 2 * LANES), jnp.float32),
            pltpu.VMEM((symbols, RANGE_ROWS, 2, ROWS, LANES), jnp.float32),
        ],
        out_shape=outs,
        compiler_params=pltpu.CompilerParams(vmem_limit_bytes=VMEM_LIMIT),
        cost_estimate=pl.CostEstimate(flops=10**9, bytes_accessed=4 * 10**6, transcendentals=0),
        name="profiles",
    )(pilot_offsets, spectrum, tables, own, other, spot, high, low, twist)


def doppler_plain(own_profiles, symbols):
    turned = lax.all_to_all(own_profiles, "sub", split_axis=3, concat_axis=1, tiled=True)
    turned = lax.all_to_all(turned, "sym", split_axis=3, concat_axis=2, tiled=True)
    ids = np.arange(symbols)
    angle = TWO_PI / symbols * (ids[:, None] * ids[None, :] % symbols)
    c, s = np.cos(angle).astype(np.float32), np.sin(angle).astype(np.float32)
    product = lambda t, x: jnp.einsum("fm,cmq->cfq", t, x, precision=HIGHEST)
    re = product(c, turned[0]) + product(s, turned[1])
    im = product(c, turned[1]) - product(s, turned[0])
    return lax.all_to_all(jnp.stack([re, im]), "sym", split_axis=2, concat_axis=3, tiled=True)


def doppler_paired(pieces, syms, subs):
    got = [pieces[0]] + [
        lax.ppermute(pieces[d], "sym", [(i, i ^ d) for i in range(syms)]) for d in SEND_ORDER
    ]
    symbols, rows = got[0].shape[:2]
    coded = pl.pallas_call(
        doppler_kernel,
        in_specs=[IN_VMEM] * syms,
        out_specs=IN_VMEM,
        out_shape=jax.ShapeDtypeStruct((syms * subs, symbols + 1, 2 * ROWS, LANES), jnp.int16),
        scratch_shapes=[
            pltpu.VMEM((syms, symbols, rows, 2, ROWS, LANES), jnp.float32),
            pltpu.VMEM((rows, syms * symbols, 2, ROWS, LANES), jnp.float32),
        ],
        compiler_params=pltpu.CompilerParams(vmem_limit_bytes=VMEM_LIMIT),
        name="doppler",
    )(*got)
    coded = lax.all_to_all(coded, ("sym", "sub"), split_axis=0, concat_axis=0)
    out = pl.pallas_call(
        join_kernel,
        in_specs=[IN_VMEM],
        out_specs=IN_VMEM,
        out_shape=jax.ShapeDtypeStruct((2, symbols, subs * ROWS, syms * LANES), jnp.float32),
        compiler_params=pltpu.CompilerParams(vmem_limit_bytes=VMEM_LIMIT),
        name="join",
    )(coded)
    return jnp.transpose(out, (0, 2, 1, 3))


def local(samples, constellation_index, pilot_offsets, cp_offset):
    syms, subs = lax.axis_size("sym"), lax.axis_size("sub")
    channels, symbols = samples.shape[1:3]
    paired = syms == 4 and syms * subs == RANGE_ROWS and channels == ROWS and symbols == 6
    half = ACTIVE_TONES // 2
    if paired:
        own = constellation_index
        other = lax.ppermute(own, "sub", [(0, 1), (1, 0)])
    else:
        index = lax.all_gather(constellation_index, "sub", axis=1, tiled=True)
        own, other = index[:, :half], index[:, half:]
    windows = jnp.transpose(samples, (0, 2, 1, 3))
    short = -channels % ROWS
    if short:
        windows = jnp.pad(windows, ((0, 0), (0, 0), (0, short), (0, 0)))
    spectrum, tables = spectra(windows, cp_offset, pilot_offsets)
    scale = ROOT_FORTYTWO / math.sqrt(WHOLE * ACTIVE_TONES * symbols * syms)
    got = profiles(
        spectrum, tables, own, other, pilot_offsets, syms if paired else 0, scale
    )
    if paired:
        return doppler_paired(got, syms, subs)
    own = jnp.transpose(got[0], (2, 1, 4, 0, 3, 5))
    own = own.reshape(2, channels + short, symbols, GUARD_SAMPLES)[:, :channels]
    return doppler_plain(own, symbols * syms)


def solution(mesh):
    return jax.shard_map(
        local,
        mesh=mesh,
        in_specs=(
            P(None, ("chan", "sub"), "sym", None),
            P(("chan", "sym"), "sub"),
            P("sym"),
            P(("chan", "sym")),
        ),
        out_specs=P(None, "chan", "sym", "sub"),
        check_vma=False,
    )
```
